32 devices in a mesh: grp: 2 (over y), kpt: 4 (over z), pw: 2 (over x), band: 2 (over core).
Axes of the slice: x: 2, y: 2, z: 4, core: 2. Of those that a mesh axis runs over, the one named last changes fastest.
Arguments:
- conduction: bfloat16 [4, 32, 64, 4000], P('grp', 'kpt', 'band', 'pw'), parts along dimension 0, may hold values from -6 to 6
- conduction_head: bfloat16 [4, 32, 64], P('grp', 'kpt', 'band'), parts along dimension 0, may hold values from -6 to 6
- valence: bfloat16 [4, 32, 64, 4000], P('grp', 'kpt', None, 'pw'), parts along dimension 0, may hold values from -6 to 6
- valence_head: bfloat16 [4, 32, 64], P('grp', 'kpt'), parts along dimension 0, may hold values from -6 to 6
- screened: bfloat16 [4, 4000, 4000], P('grp', 'kpt', 'pw'), parts along dimension 0, may hold values from -0.0014648438 to 0.0014648438
- wing_column: bfloat16 [4, 4000], P('grp'), parts along dimension 0, may hold values from -0.09375 to 0.09375
- wing_row: bfloat16 [4, 4000], P('grp', 'pw'), parts along dimension 0, may hold values from -0.09375 to 0.09375
- head_value: float32 [4], P('grp'), parts along dimension 0, may hold values from -4 to 4
- partner: int32 [64], P('grp'), parts along dimension 0, may hold values from 0 to 31, as said below
- pair_select: int32 [64], replicated, may hold values from 0 to 63, each once
- neighbors: int32 [64, 4], replicated, may hold values from 0 to 31
- weights: float32 [64, 4], replicated, may hold values from 0.2 to 1
- counts: int32 [64], replicated, may hold values from 1 to 4
Outputs:
- fine_kernel: float32 [4, 64, 4096], P('grp', 'kpt', 'band'), parts along dimension 0
The draws below stay inside these ranges and needn't reach their ends.
There are 2 independent parts, one for each index of `grp`. The reference program is written for one: setup_inputs(seed, part) draws one part's arguments, and reference() takes and returns one part's arrays. A program takes and returns all parts, laid end to end along the dimension named above; an argument that names none is the same for every part. Nothing has to cross between parts.
Inputs may be any that keep to these rules, and one draw needn't show every extreme that they name: partner is a permutation of the 32 rows; the 8 points of one kpt index find their rows on any one kpt index at most 2 times, and some pair of indices reaches 2.
All inputs are finite; a program needn't handle non-finite values.
Results may differ from the reference program's by a relative error of at most 0.0032.
Values may be sent and summed in bfloat16 or wider, within the bound.
No kernel may reach another device: no remote copies, remote signals or barrier semaphores. Data moves between devices by JAX's collectives and lax.ppermute only.
A program may use at most 192 MiB of HBM per device.

```python
import jax
import jax.numpy as jnp
from jax import lax

NG = 4000
PC = 64
PV = 64
NNB = 4
K_DEV = 8
NK = 32
NF = 64


def draw_partner(key, part):
    key = jax.random.fold_in(key, 7)
    blocks = NK // K_DEV
    offset_key, row_key, slot_key = jax.random.split(key, 3)
    offset = jax.random.randint(offset_key, (), 0, blocks)
    target = jnp.arange(blocks)[:, None]
    position = jnp.arange(K_DEV)[None, :]
    source = (target + position + offset) % blocks
    flat_source = source.reshape(-1)
    hits = (flat_source[:, None] == jnp.arange(blocks)[None, :]).astype(jnp.int32)
    ordinal = jnp.sum((jnp.cumsum(hits, axis=0) - 1) * hits, axis=1)
    row_orders = jax.vmap(lambda single: jax.random.permutation(single, K_DEV))(jax.random.split(row_key, blocks))
    local_row = row_orders[flat_source, ordinal]
    canonical = (flat_source * K_DEV + local_row).reshape(blocks, K_DEV)
    slot_orders = jax.vmap(lambda single: jax.random.permutation(single, K_DEV))(jax.random.split(slot_key, blocks))
    shuffled = jnp.take_along_axis(canonical, slot_orders, axis=1)
    return shuffled.reshape(-1).astype(jnp.int32)


def set_ends(drawn, stream_key, least, top_value):
    longest = drawn.shape.index(max(drawn.shape))
    spots = []
    for shift in (0, 1):
        where = [jax.random.randint(jax.random.fold_in(stream_key, axis), (), 0, length) for axis, length in enumerate(drawn.shape)]
        where[longest] = (where[longest] + shift) % drawn.shape[longest]
        spots.append(tuple(where))
    return drawn.at[spots[0]].set(least).at[spots[1]].set(top_value)


def levels(own_key, shape, cuts, smallest, largest):
    loudness, own = 1.0, jax.random.fold_in(own_key, 6)
    for axis_at, shards_of in cuts:
        draws = jnp.exp(jax.random.uniform(jax.random.fold_in(own, axis_at), (shards_of,), jnp.float32, smallest / len(cuts), largest / len(cuts)))
        loudness = loudness * jnp.repeat(draws, shape[axis_at] // shards_of).reshape([-1 if axis == axis_at else 1 for axis in range(len(shape))])
    return loudness


def scatter_about(rng, extent, width, reach, cuts=(), dtype=jnp.bfloat16):
    entries = width * jax.random.normal(rng, extent, jnp.float32)
    if cuts:
        entries = entries * levels(rng, extent, cuts, -0.22, 0.18)
    return jnp.clip(entries, -reach, reach).astype(dtype)


def setup_inputs(seed: int = 0, part: int = 0) -> dict:
    key_of = jax.random.split(jax.random.key(seed), 14)
    part_splits = jax.random.split(jax.random.fold_in(key_of[13], part), 14)
    conduction = scatter_about(part_splits[0], (2, NK, PC, NG), 1.0, 6.0, ((1, 4), (2, 2), (3, 2)))
    conduction_head = scatter_about(part_splits[1], (2, NK, PC), 1.0, 6.0, ((1, 4), (2, 2)))
    valence = scatter_about(part_splits[2], (2, NK, PV, NG), 1.0, 6.0, ((1, 4), (3, 2)))
    valence_head = scatter_about(part_splits[3], (2, NK, PV), 1.0, 6.0, ((1, 4),))
    screened = scatter_about(part_splits[4], (2, NG, NG), (NG * NG) ** -0.5, 0.0014648438, ((1, 4), (2, 2)))
    wing_column = scatter_about(part_splits[5], (2, NG), NG ** -0.5, 0.09375)
    wing_row = scatter_about(part_splits[6], (2, NG), NG ** -0.5, 0.09375, ((1, 2),))
    head_value = scatter_about(part_splits[7], (2,), 1.0, 4.0, (), jnp.float32)
    partner = draw_partner(jax.random.fold_in(jax.random.fold_in(key_of[13], part), 71), part)
    pair_select = jax.random.permutation(key_of[9], PV).astype(jnp.int32)
    neighbors = set_ends(jax.random.randint(key_of[10], (NF, NNB), 0, NK), jax.random.fold_in(key_of[10], 1), 0, NK - 1).astype(jnp.int32)
    weights = jnp.clip(jax.random.uniform(key_of[11], (NF, NNB), jnp.float32, 0.2, 1.0), 0.2, 1.0)
    counts = set_ends(jax.random.randint(key_of[12], (NF,), 1, NNB + 1), jax.random.fold_in(key_of[12], 1), 1, NNB).astype(jnp.int32)
    return dict(conduction=conduction, conduction_head=conduction_head, valence=valence, valence_head=valence_head, screened=screened, wing_column=wing_column, wing_row=wing_row, head_value=head_value, partner=partner, pair_select=pair_select, neighbors=neighbors, weights=weights, counts=counts)


highest = lax.Precision.HIGHEST


def product(left, right):
    return jnp.dot(left, right, precision=highest)


def pair_sum(left, right):
    return jnp.einsum("kcg,kvg->kcv", left, right, precision=highest)


def reference(conduction, conduction_head, valence, valence_head, screened, wing_column, wing_row, head_value, partner, pair_select, neighbors, weights, counts):
    points = conduction.shape[1]
    pairs = conduction.shape[2]
    planes = conduction.shape[3]
    valence_pairs = valence.shape[2]
    left_real = conduction[0].astype(jnp.float32).reshape(points * pairs, planes)
    left_imag = conduction[1].astype(jnp.float32).reshape(points * pairs, planes)
    screen_real = screened[0].astype(jnp.float32)
    screen_imag = screened[1].astype(jnp.float32)
    rows_real = product(left_real, screen_real) + product(left_imag, screen_imag)
    rows_imag = product(left_real, screen_imag) - product(left_imag, screen_real)
    rounded = lax.optimization_barrier(jnp.stack([rows_real, rows_imag]).astype(jnp.bfloat16))
    rounded = rounded.astype(jnp.float32).reshape(2, points, pairs, planes)
    moved = jnp.take(valence, partner, axis=1).astype(jnp.float32)
    moved_head = jnp.take(valence_head, partner, axis=1).astype(jnp.float32)
    body_real = pair_sum(rounded[0], moved[0]) - pair_sum(rounded[1], moved[1])
    body_imag = pair_sum(rounded[0], moved[1]) + pair_sum(rounded[1], moved[0])
    row_wing = wing_row.astype(jnp.float32)
    wing_real = jnp.einsum("g,kvg->kv", row_wing[0], moved[0], precision=highest) - jnp.einsum("g,kvg->kv", row_wing[1], moved[1], precision=highest)
    wing_imag = jnp.einsum("g,kvg->kv", row_wing[0], moved[1], precision=highest) + jnp.einsum("g,kvg->kv", row_wing[1], moved[0], precision=highest)
    column_wing = wing_column.astype(jnp.float32)
    full_real = conduction[0].astype(jnp.float32)
    full_imag = conduction[1].astype(jnp.float32)
    side_real = jnp.einsum("kcg,g->kc", full_real, column_wing[0], precision=highest) + jnp.einsum("kcg,g->kc", full_imag, column_wing[1], precision=highest)
    side_imag = jnp.einsum("kcg,g->kc", full_real, column_wing[1], precision=highest) - jnp.einsum("kcg,g->kc", full_imag, column_wing[0], precision=highest)
    conj_real = conduction_head[0].astype(jnp.float32)
    conj_imag = -conduction_head[1].astype(jnp.float32)
    first_real = conj_real[:, :, None] * wing_real[:, None, :] - conj_imag[:, :, None] * wing_imag[:, None, :]
    first_imag = conj_real[:, :, None] * wing_imag[:, None, :] + conj_imag[:, :, None] * wing_real[:, None, :]
    scaled_real = side_real + conj_real * head_value[0] - conj_imag * head_value[1]
    scaled_imag = side_imag + conj_real * head_value[1] + conj_imag * head_value[0]
    second_real = scaled_real[:, :, None] * moved_head[0][:, None, :] - scaled_imag[:, :, None] * moved_head[1][:, None, :]
    second_imag = scaled_real[:, :, None] * moved_head[1][:, None, :] + scaled_imag[:, :, None] * moved_head[0][:, None, :]
    kernel = jnp.stack([body_real + first_real + second_real, body_imag + first_imag + second_imag])
    kernel = jnp.take(kernel, pair_select, axis=3)
    coarse = lax.optimization_barrier(kernel.astype(jnp.bfloat16).reshape(2, points, pairs * valence_pairs))
    coarse = coarse.astype(jnp.float32)
    live = jnp.where(jnp.arange(NNB)[None, :] < counts[:, None], weights, jnp.float32(0.0))
    fine_kernel = jnp.zeros((2, neighbors.shape[0], pairs * valence_pairs), jnp.float32)
    for stencil_slot in range(NNB):
        fine_kernel = fine_kernel + live[:, stencil_slot][None, :, None] * jnp.take(coarse, neighbors[:, stencil_slot], axis=1)
    return fine_kernel
```

```python
import jax
import jax.numpy as jnp
from jax import lax
from jax.experimental import pallas as pl
from jax.experimental.pallas import tpu as pltpu
from jax.sharding import PartitionSpec as P

highest = lax.Precision.HIGHEST
f32 = jnp.float32
bf16 = jnp.bfloat16
HEAD_PARTS = 3
VMEM_BYTES = 48 * 1024 * 1024


def round_up(value, step):
    return -(-value // step) * step


def shifted(x, name, shift):
    count = lax.axis_size(name)
    pairs = [(source, (source + shift) % count) for source in range(count)]
    return lax.ppermute(x, name, pairs)


def share(x, name):
    return [x] + [shifted(x, name, shift) for shift in range(1, lax.axis_size(name))]


def deal(x, name):
    count = lax.axis_size(name)
    me = lax.axis_index(name)
    pieces = []
    for shift in range(count):
        piece = lax.dynamic_index_in_dim(x, (me + shift) % count, 0, keepdims=False)
        pieces.append(shifted(piece, name, shift) if shift else piece)
    return pieces


def valence_columns(valence, valence_head, selector, core, width, last):
    parts, points, pairs, columns = valence.shape
    head_at = columns - last * width

    def kernel(core_ref, valence_ref, head_ref, selector_ref, out_ref):
        column = lax.broadcasted_iota(jnp.int32, (pairs, width), 1)
        at_last = core_ref[0] == last
        limit = jnp.where(at_last, head_at, width)
        head_column = jnp.where(at_last, head_at, width)
        for point in range(points):
            rows = valence_ref[0, point].astype(f32)
            head = jnp.broadcast_to(head_ref[0, point].astype(f32), (pairs, width))
            rows = jnp.where(column < limit, rows, 0.0)
            rows = jnp.where(column == head_column, head, rows)
            moved = jnp.dot(selector_ref[...], rows.astype(bf16), preferred_element_type=f32)
            out_ref[0, point] = moved.astype(bf16)

    return pl.pallas_call(
        kernel,
        out_shape=jax.ShapeDtypeStruct((parts, points, pairs, width), bf16),
        grid_spec=pltpu.PrefetchScalarGridSpec(
            num_scalar_prefetch=1,
            grid=(parts,),
            in_specs=[
                pl.BlockSpec((1, points, pairs, width), lambda x, core: (x, 0, 0, core[0])),
                pl.BlockSpec((1, points, pairs, 1), lambda x, core: (x, 0, 0, 0)),
                pl.BlockSpec((pairs, pairs), lambda x, core: (0, 0)),
            ],
            out_specs=pl.BlockSpec((1, points, pairs, width), lambda x, core: (x, 0, 0, 0)),
        ),
        compiler_params=pltpu.CompilerParams(vmem_limit_bytes=VMEM_BYTES),
        name="valence_columns",
    )(core.reshape(1), valence, valence_head[..., None], selector)


def screen_product(places, pieces, right, per_index, half):
    _, deep, width = right.shape
    planes = deep // 2
    rows = per_index * half
    count = len(pieces)
    bands = 2
    pw_count = count // bands
    points = pw_count * per_index
    tile = min(256, width)

    def kernel(place_ref, *refs):
        piece_refs, right_ref, out_ref, left_ref = refs[:count], refs[count], refs[count + 1], refs[count + 2]

        @pl.when((pl.program_id(0) == 0) & (pl.program_id(1) == 0))
        def _():
            for index in range(count):
                start = pl.multiple_of(place_ref[index] * rows, rows)
                left_ref[pl.ds(start, rows), 0:planes] = piece_refs[index][0]
                left_ref[pl.ds(start, rows), planes:deep] = piece_refs[index][1]

        total = jnp.dot(left_ref[...], right_ref[0], preferred_element_type=f32).astype(bf16)
        for pw in range(pw_count):
            for band in range(bands):
                for point in range(per_index):
                    start = (pw * bands + band) * rows + point * half
                    out_ref[pw * per_index + point, band, 0] = total[start : start + half]

    whole = pl.BlockSpec((2, rows, planes), lambda x, n, place: (0, 0, 0))
    return pl.pallas_call(
        kernel,
        out_shape=jax.ShapeDtypeStruct((points, bands, 2, half, width), bf16),
        grid_spec=pltpu.PrefetchScalarGridSpec(
            num_scalar_prefetch=1,
            grid=(2, width // tile),
            in_specs=[whole] * count + [pl.BlockSpec((1, deep, tile), lambda x, n, place: (x, 0, n))],
            out_specs=pl.BlockSpec((points, bands, 1, half, tile), lambda x, n, place: (0, 0, x, 0, n)),
            scratch_shapes=[pltpu.VMEM((count * rows, deep), bf16)],
        ),
        compiler_params=pltpu.CompilerParams(vmem_limit_bytes=VMEM_BYTES),
        cost_estimate=pl.CostEstimate(
            flops=2 * count * rows * deep * width * 2,
            bytes_accessed=2 * (2 * deep * width + 2 * points * bands * half * width),
            transcendentals=0,
        ),
        name="screen_product",
    )(places, *pieces, right)


def contract(rows, product, gathered):
    points, bands, _, half, width = product.shape
    _, _, stored, pairs, _ = gathered.shape
    group = 4 if points % 4 == 0 else 1

    def kernel(row_ref, product_ref, *refs):
        out_ref = refs[group]
        lane = lax.broadcasted_iota(jnp.int32, (half, 2 * pairs), 1)
        for index in range(group):
            left = product_ref[index].reshape(bands * 2 * half, width)
            right = refs[index][0, :, 0].reshape(2 * pairs, width)
            square = lax.dot_general(left, right, (((1,), (1,)), ((), ())), preferred_element_type=f32)
            for band in range(bands):
                first = square[2 * band * half : (2 * band + 1) * half]
                second = square[(2 * band + 1) * half : (2 * band + 2) * half]
                turned = pltpu.roll(second, pairs, 1)
                total = first + jnp.where(lane < pairs, -turned, turned)
                out_ref[index, band * half : (band + 1) * half, :] = total

    def valence_spec(index):
        return pl.BlockSpec(
            (1, 2, 1, pairs, width),
            lambda step, row: (row[step * group + index] // stored, 0, row[step * group + index] % stored, 0, 0),
        )

    return pl.pallas_call(
        kernel,
        out_shape=jax.ShapeDtypeStruct((points, bands * half, 2 * pairs), f32),
        grid_spec=pltpu.PrefetchScalarGridSpec(
            num_scalar_prefetch=1,
            grid=(points // group,),
            in_specs=[pl.BlockSpec((group, bands, 2, half, width), lambda step, row: (step, 0, 0, 0, 0))]
            + [valence_spec(index) for index in range(group)],
            out_specs=pl.BlockSpec((group, bands * half, 2 * pairs), lambda step, row: (step, 0, 0)),
        ),
        compiler_params=pltpu.CompilerParams(vmem_limit_bytes=VMEM_BYTES),
        cost_estimate=pl.CostEstimate(
            flops=2 * points * bands * 2 * half * 2 * pairs * width,
            bytes_accessed=2 * points * width * (bands * 2 * half + 2 * pairs),
            transcendentals=0,
        ),
        name="contract",
    )(rows, product, *([gathered] * group))


def on_device(
    conduction,
    conduction_head,
    valence,
    valence_head,
    screened,
    wing_column,
    wing_row,
    head_value,
    partner,
    pair_select,
    neighbors,
    weights,
    counts,
):
    points = conduction.shape[1]
    half = conduction.shape[2]
    pairs = valence.shape[2]
    block, columns = screened.shape[1], screened.shape[2]
    kpt_count, pw_count, band_count = lax.axis_size("kpt"), lax.axis_size("pw"), lax.axis_size("band")
    kpt, pw, band = lax.axis_index("kpt"), lax.axis_index("pw"), lax.axis_index("band")
    per_index = points // pw_count
    rows = per_index * half
    blocks_here = columns // block
    deep = round_up(block + HEAD_PARTS, 128)
    width = round_up(-(-(columns + 1) // band_count), 128)
    last = band_count - 1
    head_at = columns - last * width

    selector = (pair_select[:, None] == jnp.arange(pairs)[None, :]).astype(bf16)
    own_valence = valence_columns(valence, valence_head, selector, band, width, last)
    gathered = lax.all_gather(own_valence, "kpt", axis=0)

    plane = jnp.arange(deep)
    is_head = (plane >= block) & (plane < block + HEAD_PARTS)
    cut = []
    for index in range(blocks_here):
        padded = jnp.pad(
            conduction[..., index * block : (index + 1) * block], ((0, 0), (0, 0), (0, 0), (0, deep - block))
        )
        cut.append(jnp.where(is_head, conduction_head[..., None], padded))
    cut = jnp.stack(cut).reshape(blocks_here, 2, pw_count, rows, deep)
    dealt = jnp.stack(deal(jnp.moveaxis(cut, 2, 0), "pw"))

    def block_for(target):
        owner = target // blocks_here
        return lax.dynamic_index_in_dim(
            lax.dynamic_index_in_dim(dealt, (pw - owner) % pw_count, 0, keepdims=False),
            target % blocks_here,
            0,
            keepdims=False,
        )

    screen = jnp.pad(screened, ((0, 0), (0, deep - block), (0, band_count * width - columns)))
    screen = lax.dynamic_slice_in_dim(screen, band * width, width, 2)
    row_part = jnp.pad(wing_row, ((0, 0), (0, band_count * width - columns)))
    row_part = lax.dynamic_slice_in_dim(row_part, band * width, width, 1)
    first_kpt = kpt == 0
    row_part = jnp.where(first_kpt, row_part, 0)
    corner = []
    rest = head_value
    for _ in range(HEAD_PARTS):
        part = lax.reduce_precision(rest, 8, 7)
        corner.append(jnp.where(first_kpt, part, 0.0))
        rest = rest - part
    corner = jnp.stack(corner, axis=1).astype(bf16)
    column_part = jnp.concatenate(
        [lax.dynamic_slice_in_dim(wing_column, kpt * block, block, 1), corner], axis=1
    )
    column_part = jnp.pad(column_part, ((0, 0), (0, deep - block - HEAD_PARTS)))
    has_column = (pw == 0) & (band == last)
    screen = jnp.where(plane[None, :, None] == block, row_part[:, None, :], screen)
    screen = jnp.where(
        (jnp.arange(width)[None, None, :] == head_at) & has_column, column_part[:, :, None], screen
    )
    right = jnp.stack(
        [
            jnp.concatenate([screen[0], screen[1]], axis=0),
            jnp.concatenate([screen[1], -screen[0]], axis=0),
        ]
    )

    places = jnp.stack(
        [
            ((pw - pw_shift) % pw_count) * band_count + (band - band_shift) % band_count
            for pw_shift in range(pw_count)
            for band_shift in range(band_count)
        ]
    ).astype(jnp.int32)

    live = jnp.where(jnp.arange(neighbors.shape[1])[None, :] < counts[:, None], weights, 0.0)
    all_points = kpt_count * points
    match = neighbors[:, :, None] == jnp.arange(all_points)[None, None, :]
    stencil = jnp.sum(jnp.where(match, live[:, :, None], 0.0), axis=1)

    products = []
    for shift in range(kpt_count):
        piece = block_for((kpt + shift) % kpt_count)
        if shift:
            piece = shifted(piece, "kpt", shift)
        pieces = [own for across in share(piece, "pw") for own in share(across, "band")]
        products.append(screen_product(places, pieces, right, per_index, half))

    totals = []
    stencils = []
    for shift in range(kpt_count):
        source = (kpt - shift) % kpt_count
        row_ids = lax.dynamic_slice_in_dim(partner, source * points, points, 0)
        totals.append(contract(row_ids, products[shift], gathered))
        stencils.append(lax.dynamic_slice_in_dim(stencil, source * points, points, 1))
    body = jnp.concatenate(totals, axis=0)
    stencil = jnp.concatenate(stencils, axis=1)

    lanes = 2 * pairs
    body = body.reshape(all_points, band_count, half, lanes)
    body = sum(deal(jnp.moveaxis(body, 1, 0), "band"))
    kept = half // pw_count
    body = body.reshape(all_points, pw_count, kept, lanes)
    body = sum(deal(jnp.moveaxis(body, 1, 0), "pw"))
    fine = jnp.dot(stencil, body.reshape(all_points, kept * lanes), precision=highest)
    fine_here = neighbors.shape[0] // kpt_count
    fine = fine.astype(bf16).reshape(kpt_count, fine_here, kept, lanes)
    fine = sum(piece.astype(f32) for piece in deal(fine, "kpt"))
    fine = lax.all_gather(fine, "pw", axis=0)
    fine = fine.reshape(pw_count, fine_here, kept, 2, pairs)
    return jnp.transpose(fine, (3, 1, 0, 2, 4)).reshape(2, fine_here, half * pairs)


def solution(mesh):
    return jax.shard_map(
        on_device,
        mesh=mesh,
        in_specs=(
            P("grp", "kpt", "band", "pw"),
            P("grp", "kpt", "band"),
            P("grp", "kpt", None, "pw"),
            P("grp", "kpt", None),
            P("grp", "kpt", "pw"),
            P("grp", None),
            P("grp", "pw"),
            P("grp"),
            P("grp"),
            P(),
            P(),
            P(),
            P(),
        ),
        out_specs=P("grp", "kpt", "band"),
        check_vma=False,
    )
```

```python
import jax
import jax.numpy as jnp
from jax import lax
from jax.experimental import pallas as pl
from jax.experimental.pallas import tpu as pltpu
from jax.sharding import PartitionSpec as P

highest = lax.Precision.HIGHEST
f32 = jnp.float32
bf16 = jnp.bfloat16
HEAD_PARTS = 3
VMEM_BYTES = 48 * 1024 * 1024


def round_up(value, step):
    return -(-value // step) * step


def shifted(x, name, shift):
    count = lax.axis_size(name)
    pairs = [(source, (source + shift) % count) for source in range(count)]
    return lax.ppermute(x, name, pairs)


def share(x, name):
    return [x] + [shifted(x, name, shift) for shift in range(1, lax.axis_size(name))]


def deal(x, name):
    count = lax.axis_size(name)
    me = lax.axis_index(name)
    pieces = []
    for shift in range(count):
        piece = lax.dynamic_index_in_dim(x, (me + shift) % count, 0, keepdims=False)
        pieces.append(shifted(piece, name, shift) if shift else piece)
    return pieces


def valence_columns(valence, valence_head, selector, core, width, last, chunks):
    parts, points, pairs, columns = valence.shape
    head_at = columns - last * width
    each = points // chunks

    def kernel(core_ref, valence_ref, head_ref, selector_ref, *out_refs):
        column = lax.broadcasted_iota(jnp.int32, (pairs, width), 1)
        at_last = core_ref[0] == last
        limit = jnp.where(at_last, head_at, width)
        head_column = jnp.where(at_last, head_at, width)
        for point in range(points):
            rows = valence_ref[0, point].astype(f32)
            head = jnp.broadcast_to(head_ref[0, point].astype(f32), (pairs, width))
            rows = jnp.where(column < limit, rows, 0.0)
            rows = jnp.where(column == head_column, head, rows)
            moved = jnp.dot(selector_ref[...], rows.astype(bf16), preferred_element_type=f32)
            out_refs[point // each][0, point % each] = moved.astype(bf16)

    return pl.pallas_call(
        kernel,
        out_shape=[jax.ShapeDtypeStruct((parts, each, pairs, width), bf16)] * chunks,
        grid_spec=pltpu.PrefetchScalarGridSpec(
            num_scalar_prefetch=1,
            grid=(parts,),
            in_specs=[
                pl.BlockSpec((1, points, pairs, width), lambda x, core: (x, 0, 0, core[0])),
                pl.BlockSpec((1, points, pairs, 1), lambda x, core: (x, 0, 0, 0)),
                pl.BlockSpec((pairs, pairs), lambda x, core: (0, 0)),
            ],
            out_specs=[pl.BlockSpec((1, each, pairs, width), lambda x, core: (x, 0, 0, 0))] * chunks,
        ),
        compiler_params=pltpu.CompilerParams(vmem_limit_bytes=VMEM_BYTES),
        name="valence_columns",
    )(core.reshape(1), valence, valence_head[..., None], selector)


def along_line(x, name):
    count = lax.axis_size(name)
    below, above, steps = x, x, []
    for step in range(1, count):
        below = lax.ppermute(below, name, [(s, s + 1) for s in range(step - 1, count - 1)])
        above = lax.ppermute(above, name, [(s, s - 1) for s in range(1, count - step + 1)])
        steps.append((below, above))
    return steps


def screen_product(places, pieces, right, per_index, half, store, blocks):
    _, deep, width = right.shape
    planes = deep // 2
    rows = per_index * half
    count = len(pieces)
    bands = 2
    pw_count = count // bands
    points = pw_count * per_index
    tile = min(256, width)

    def kernel(place_ref, *refs):
        piece_refs, right_ref, out_ref, left_ref = refs[:count], refs[count], refs[-2], refs[-1]

        @pl.when((pl.program_id(0) == 0) & (pl.program_id(1) == 0))
        def _():
            for index in range(count):
                start = pl.multiple_of(place_ref[index] * rows, rows)
                left_ref[pl.ds(start, rows), 0:planes] = piece_refs[index][0]
                left_ref[pl.ds(start, rows), planes:deep] = piece_refs[index][1]

        total = jnp.dot(left_ref[...], right_ref[0], preferred_element_type=f32).astype(bf16)
        for pw in range(pw_count):
            for band in range(bands):
                for point in range(per_index):
                    start = (pw * bands + band) * rows + point * half
                    out_ref[pw * per_index + point, band, 0] = total[start : start + half]

    whole = pl.BlockSpec((2, rows, planes), lambda x, n, place: (0, 0, 0))
    kept = [] if store is None else [store]
    return pl.pallas_call(
        kernel,
        out_shape=jax.ShapeDtypeStruct((blocks * points, bands, 2, half, width), bf16),
        grid_spec=pltpu.PrefetchScalarGridSpec(
            num_scalar_prefetch=1,
            grid=(2, width // tile),
            in_specs=[whole] * count
            + [pl.BlockSpec((1, deep, tile), lambda x, n, place: (x, 0, n))]
            + [pl.BlockSpec(memory_space=pl.ANY)] * len(kept),
            out_specs=pl.BlockSpec(
                (points, bands, 1, half, tile), lambda x, n, place: (place[count], 0, x, 0, n)
            ),
            scratch_shapes=[pltpu.VMEM((count * rows, deep), bf16)],
        ),
        input_output_aliases={count + 2: 0} if kept else {},
        compiler_params=pltpu.CompilerParams(vmem_limit_bytes=VMEM_BYTES),
        cost_estimate=pl.CostEstimate(
            flops=2 * count * rows * deep * width * 2,
            bytes_accessed=2 * (2 * deep * width + 2 * points * bands * half * width),
            transcendentals=0,
        ),
        name="screen_product",
    )(places, *pieces, right, *kept)


def contract(row_ids, sides, store, below, above):
    _, bands, _, half, width = store.shape
    _, each, pairs, _ = below[0].shape
    chunks, slots = len(below), sides.shape[0]
    given = list(below) + list(above)

    def kernel(row_ref, side_ref, *refs):
        store_refs, valence_refs, out_ref = refs[:each], refs[each:-1], refs[-1]
        lane = lax.broadcasted_iota(jnp.int32, (half, 2 * pairs), 1)
        side = side_ref[pl.program_id(0)]

        def rows_of(valence_ref):
            for index in range(each):
                left = store_refs[index][0].reshape(bands * 2 * half, width)
                right = valence_ref[:, index].reshape(2 * pairs, width)
                square = lax.dot_general(left, right, (((1,), (1,)), ((), ())), preferred_element_type=f32)
                for band in range(bands):
                    first = square[2 * band * half : (2 * band + 1) * half]
                    second = square[(2 * band + 1) * half : (2 * band + 2) * half]
                    turned = pltpu.roll(second, pairs, 1)
                    total = first + jnp.where(lane < pairs, -turned, turned)
                    out_ref[index, band * half : (band + 1) * half, :] = total

        for place in range(len(given)):

            @pl.when((side == place // chunks) & (pl.program_id(1) == place % chunks))
            def _(place=place):
                rows_of(valence_refs[place])

        @pl.when(side == 2)
        def _():
            out_ref[...] = jnp.zeros_like(out_ref)

    def store_spec(index):
        return pl.BlockSpec(
            (1, bands, 2, half, width),
            lambda slot, chunk, row, side: (row[(slot * chunks + chunk) * each + index], 0, 0, 0, 0),
        )

    whole = pl.BlockSpec((2, each, pairs, width), lambda slot, chunk, row, side: (0, 0, 0, 0))
    return pl.pallas_call(
        kernel,
        out_shape=jax.ShapeDtypeStruct((slots * chunks * each, bands * half, 2 * pairs), f32),
        grid_spec=pltpu.PrefetchScalarGridSpec(
            num_scalar_prefetch=2,
            grid=(slots, chunks),
            in_specs=[store_spec(index) for index in range(each)] + [whole] * len(given),
            out_specs=pl.BlockSpec(
                (each, bands * half, 2 * pairs), lambda slot, chunk, row, side: (slot * chunks + chunk, 0, 0)
            ),
        ),
        compiler_params=pltpu.CompilerParams(vmem_limit_bytes=VMEM_BYTES),
        cost_estimate=pl.CostEstimate(
            flops=2 * slots * chunks * each * bands * 2 * half * 2 * pairs * width,
            bytes_accessed=2 * slots * chunks * each * width * (bands * 2 * half + 2 * pairs),
            transcendentals=0,
        ),
        name="contract",
    )(row_ids, sides, *([store] * each), *given)


def on_device(
    conduction,
    conduction_head,
    valence,
    valence_head,
    screened,
    wing_column,
    wing_row,
    head_value,
    partner,
    pair_select,
    neighbors,
    weights,
    counts,
):
    points = conduction.shape[1]
    half = conduction.shape[2]
    pairs = valence.shape[2]
    block, columns = screened.shape[1], screened.shape[2]
    kpt_count, pw_count, band_count = lax.axis_size("kpt"), lax.axis_size("pw"), lax.axis_size("band")
    kpt, pw, band = lax.axis_index("kpt"), lax.axis_index("pw"), lax.axis_index("band")
    per_index = points // pw_count
    rows = per_index * half
    blocks_here = columns // block
    deep = round_up(block + HEAD_PARTS, 128)
    width = round_up(-(-(columns + 1) // band_count), 128)
    last = band_count - 1
    head_at = columns - last * width

    selector = (pair_select[:, None] == jnp.arange(pairs)[None, :]).astype(bf16)
    chunks = 2 if points % 2 == 0 else 1
    own_valence = valence_columns(valence, valence_head, selector, band, width, last, chunks)
    lines = [along_line(chunk, "kpt") for chunk in own_valence]

    plane = jnp.arange(deep)
    is_head = (plane >= block) & (plane < block + HEAD_PARTS)
    cut = []
    for index in range(blocks_here):
        padded = jnp.pad(
            conduction[..., index * block : (index + 1) * block], ((0, 0), (0, 0), (0, 0), (0, deep - block))
        )
        cut.append(jnp.where(is_head, conduction_head[..., None], padded))
    cut = jnp.stack(cut).reshape(blocks_here, 2, pw_count, rows, deep)
    dealt = jnp.stack(deal(jnp.moveaxis(cut, 2, 0), "pw"))

    def block_for(target):
        owner = target // blocks_here
        return lax.dynamic_index_in_dim(
            lax.dynamic_index_in_dim(dealt, (pw - owner) % pw_count, 0, keepdims=False),
            target % blocks_here,
            0,
            keepdims=False,
        )

    screen = jnp.pad(screened, ((0, 0), (0, deep - block), (0, band_count * width - columns)))
    screen = lax.dynamic_slice_in_dim(screen, band * width, width, 2)
    row_part = jnp.pad(wing_row, ((0, 0), (0, band_count * width - columns)))
    row_part = lax.dynamic_slice_in_dim(row_part, band * width, width, 1)
    first_kpt = kpt == 0
    row_part = jnp.where(first_kpt, row_part, 0)
    corner = []
    rest = head_value
    for _ in range(HEAD_PARTS):
        part = lax.reduce_precision(rest, 8, 7)
        corner.append(jnp.where(first_kpt, part, 0.0))
        rest = rest - part
    corner = jnp.stack(corner, axis=1).astype(bf16)
    column_part = jnp.concatenate(
        [lax.dynamic_slice_in_dim(wing_column, kpt * block, block, 1), corner], axis=1
    )
    column_part = jnp.pad(column_part, ((0, 0), (0, deep - block - HEAD_PARTS)))
    has_column = (pw == 0) & (band == last)
    screen = jnp.where(plane[None, :, None] == block, row_part[:, None, :], screen)
    screen = jnp.where(
        (jnp.arange(width)[None, None, :] == head_at) & has_column, column_part[:, :, None], screen
    )
    right = jnp.stack(
        [
            jnp.concatenate([screen[0], screen[1]], axis=0),
            jnp.concatenate([screen[1], -screen[0]], axis=0),
        ]
    )

    places = jnp.stack(
        [
            ((pw - pw_shift) % pw_count) * band_count + (band - band_shift) % band_count
            for pw_shift in range(pw_count)
            for band_shift in range(band_count)
        ]
    ).astype(jnp.int32)

    live = jnp.where(jnp.arange(neighbors.shape[1])[None, :] < counts[:, None], weights, 0.0)
    all_points = kpt_count * points
    point_of_row = jnp.sum(
        jnp.where(partner[None, :] == jnp.arange(all_points)[:, None], jnp.arange(all_points)[None, :], 0), axis=1
    ).astype(jnp.int32)

    store = None
    for shift in range(kpt_count):
        piece = block_for((kpt + shift) % kpt_count)
        if shift:
            piece = shifted(piece, "kpt", shift)
        pieces = [own for across in share(piece, "pw") for own in share(across, "band")]
        source = ((kpt - shift) % kpt_count).astype(jnp.int32)
        store = screen_product(
            jnp.append(places, source), pieces, right, per_index, half, store, kpt_count
        )

    lanes = 2 * pairs
    kept = half // pw_count

    def fine_part(sides, owners, below, above):
        owners = jnp.stack(owners)
        sides = jnp.stack(sides).astype(jnp.int32)
        live_slot = jnp.repeat(sides < 2, points)
        row_ids = (owners[:, None] * points + jnp.arange(points)[None, :]).reshape(-1)
        row_ids = jnp.where(live_slot, jnp.take(point_of_row, row_ids, mode="clip"), 0)
        body = contract(row_ids, sides, store, below, above)
        body = body.reshape(-1, band_count, half, lanes)
        body = sum(deal(jnp.moveaxis(body, 1, 0), "band"))
        body = body.reshape(-1, pw_count, kept, lanes)
        body = sum(deal(jnp.moveaxis(body, 1, 0), "pw"))
        match = (neighbors[:, :, None] == row_ids[None, None, :]) & live_slot[None, None, :]
        stencil = jnp.sum(jnp.where(match, live[:, :, None], 0.0), axis=1)
        return jnp.dot(stencil, body.reshape(-1, kept * lanes), precision=highest)

    fine = fine_part([jnp.zeros((), jnp.int32)], [kpt], own_valence, [])
    for step in range(1, kpt_count):
        below = [line[step - 1][0] for line in lines]
        above = [line[step - 1][1] for line in lines]
        has_below, has_above = kpt >= step, kpt + step < kpt_count
        if 2 * step < kpt_count:
            sides = [jnp.where(has_below, 0, 2), jnp.where(has_above, 1, 2)]
            owners = [kpt - step, kpt + step]
        else:
            sides = [jnp.where(has_below, 0, jnp.where(has_above, 1, 2))]
            owners = [jnp.where(has_below, kpt - step, kpt + step)]
        fine = fine + fine_part(sides, owners, below, above)

    fine_here = neighbors.shape[0] // kpt_count
    fine = fine.reshape(kpt_count, fine_here, kept, lanes)
    fine = sum(deal(fine, "kpt"))
    fine = lax.all_gather(fine, "pw", axis=0)
    fine = fine.reshape(pw_count, fine_here, kept, 2, pairs)
    return jnp.transpose(fine, (3, 1, 0, 2, 4)).reshape(2, fine_here, half * pairs)


def solution(mesh):
    return jax.shard_map(
        on_device,
        mesh=mesh,
        in_specs=(
            P("grp", "kpt", "band", "pw"),
            P("grp", "kpt", "band"),
            P("grp", "kpt", None, "pw"),
            P("grp", "kpt", None),
            P("grp", "kpt", "pw"),
            P("grp", None),
            P("grp", "pw"),
            P("grp"),
            P("grp"),
            P(),
            P(),
            P(),
            P(),
        ),
        out_specs=P("grp", "kpt", "band"),
        check_vma=False,
    )
```

```python
import jax
import jax.numpy as jnp
from jax import lax
from jax.experimental import pallas as pl
from jax.experimental.pallas import tpu as pltpu
from jax.sharding import PartitionSpec as P

highest = lax.Precision.HIGHEST
f32 = jnp.float32
bf16 = jnp.bfloat16
HEAD_PARTS = 3
VMEM_BYTES = 48 * 1024 * 1024


def round_up(value, step):
    return -(-value // step) * step


def shifted(x, name, shift):
    count = lax.axis_size(name)
    pairs = [(source, (source + shift) % count) for source in range(count)]
    return lax.ppermute(x, name, pairs)


def after(x, others):
    return lax.optimization_barrier((x, others))[0]


def share(x, name):
    return [x] + [shifted(x, name, shift) for shift in range(1, lax.axis_size(name))]


def deal(x, name):
    count = lax.axis_size(name)
    me = lax.axis_index(name)
    pieces = []
    for shift in range(count):
        piece = lax.dynamic_index_in_dim(x, (me + shift) % count, 0, keepdims=False)
        pieces.append(shifted(piece, name, shift) if shift else piece)
    return pieces


def valence_columns(valence, valence_head, selector, core, width, last):
    parts, points, pairs, columns = valence.shape
    head_at = columns - last * width

    def kernel(core_ref, valence_ref, head_ref, selector_ref, out_ref):
        column = lax.broadcasted_iota(jnp.int32, (pairs, width), 1)
        at_last = core_ref[0] == last
        limit = jnp.where(at_last, head_at, width)
        head_column = jnp.where(at_last, head_at, width)
        for point in range(points):
            rows = valence_ref[0, point].astype(f32)
            head = jnp.broadcast_to(head_ref[0, point].astype(f32), (pairs, width))
            rows = jnp.where(column < limit, rows, 0.0)
            rows = jnp.where(column == head_column, head, rows)
            moved = jnp.dot(selector_ref[...], rows.astype(bf16), preferred_element_type=f32)
            out_ref[0, point] = moved.astype(bf16)

    return pl.pallas_call(
        kernel,
        out_shape=jax.ShapeDtypeStruct((parts, points, pairs, width), bf16),
        grid_spec=pltpu.PrefetchScalarGridSpec(
            num_scalar_prefetch=1,
            grid=(parts,),
            in_specs=[
                pl.BlockSpec((1, points, pairs, width), lambda x, core: (x, 0, 0, core[0])),
                pl.BlockSpec((1, points, pairs, 1), lambda x, core: (x, 0, 0, 0)),
                pl.BlockSpec((pairs, pairs), lambda x, core: (0, 0)),
            ],
            out_specs=pl.BlockSpec((1, points, pairs, width), lambda x, core: (x, 0, 0, 0)),
        ),
        compiler_params=pltpu.CompilerParams(vmem_limit_bytes=VMEM_BYTES),
        name="valence_columns",
    )(core.reshape(1), valence, valence_head[..., None], selector)


def along_line(below, above, name, step):
    count = lax.axis_size(name)
    below = lax.ppermute(below, name, [(s, s + 1) for s in range(step - 1, count - 1)])
    above = lax.ppermute(above, name, [(s, s - 1) for s in range(1, count - step + 1)])
    return below, above


def screen_product(places, pieces, right, per_index, half, store, blocks):
    _, deep, width = right.shape
    planes = deep // 2
    rows = per_index * half
    count = len(pieces)
    sources = pieces[0].shape[0]
    bands = 2
    pw_count = count // bands
    points = pw_count * per_index
    tile = min(256, width)

    def kernel(place_ref, *refs):
        piece_refs, right_ref, out_ref, left_ref = refs[:count], refs[count], refs[-2], refs[-1]

        @pl.when((pl.program_id(1) == 0) & (pl.program_id(2) == 0))
        def _():
            for index in range(count):
                start = pl.multiple_of(place_ref[index] * rows, rows)
                left_ref[pl.ds(start, rows), 0:planes] = piece_refs[index][0, 0]
                left_ref[pl.ds(start, rows), planes:deep] = piece_refs[index][0, 1]

        total = jnp.dot(left_ref[...], right_ref[0], preferred_element_type=f32).astype(bf16)
        for pw in range(pw_count):
            for band in range(bands):
                for point in range(per_index):
                    start = (pw * bands + band) * rows + point * half
                    out_ref[pw * per_index + point, band, 0] = total[start : start + half]

    whole = pl.BlockSpec((1, 2, rows, planes), lambda s, x, n, place: (s, 0, 0, 0))
    kept = [] if store is None else [store]
    return pl.pallas_call(
        kernel,
        out_shape=jax.ShapeDtypeStruct((blocks * points, bands, 2, half, width), bf16),
        grid_spec=pltpu.PrefetchScalarGridSpec(
            num_scalar_prefetch=1,
            grid=(sources, 2, width // tile),
            in_specs=[whole] * count
            + [pl.BlockSpec((1, deep, tile), lambda s, x, n, place: (x, 0, n))]
            + [pl.BlockSpec(memory_space=pl.ANY)] * len(kept),
            out_specs=pl.BlockSpec(
                (points, bands, 1, half, tile), lambda s, x, n, place: (place[count + s], 0, x, 0, n)
            ),
            scratch_shapes=[pltpu.VMEM((count * rows, deep), bf16)],
        ),
        input_output_aliases={count + 2: 0} if kept else {},
        compiler_params=pltpu.CompilerParams(vmem_limit_bytes=VMEM_BYTES),
        cost_estimate=pl.CostEstimate(flops=1, bytes_accessed=1, transcendentals=0),
        name="screen_product",
    )(places, *pieces, right, *kept)


def contract(row_ids, sides, owners, store, valences, body, blocks):
    _, bands, _, half, width = store.shape
    _, points, pairs, _ = valences[0].shape
    slots = sides.shape[0]
    group = 4 if points % 4 == 0 else 1
    steps = points // group

    def kernel(row_ref, side_ref, owner_ref, *refs):
        store_refs, valence_refs, out_ref = refs[:group], refs[group : group + len(valences)], refs[-1]
        lane = lax.broadcasted_iota(jnp.int32, (half, 2 * pairs), 1)
        side = side_ref[pl.program_id(0)]
        step = pl.program_id(1)

        def rows_of(valence_ref):
            for index in range(group):
                left = store_refs[index][0].reshape(bands * 2 * half, width)
                right = valence_ref[:, step * group + index].reshape(2 * pairs, width)
                square = lax.dot_general(left, right, (((1,), (1,)), ((), ())), preferred_element_type=f32)
                for band in range(bands):
                    first = square[2 * band * half : (2 * band + 1) * half]
                    second = square[(2 * band + 1) * half : (2 * band + 2) * half]
                    turned = pltpu.roll(second, pairs, 1)
                    total = first + jnp.where(lane < pairs, -turned, turned)
                    out_ref[index, band * half : (band + 1) * half, :] = total

        for place in range(len(valences)):

            @pl.when(side == place)
            def _(place=place):
                rows_of(valence_refs[place])

    def store_spec(index):
        return pl.BlockSpec(
            (1, bands, 2, half, width),
            lambda slot, step, row, side, owner: (row[slot * points + step * group + index], 0, 0, 0, 0),
        )

    whole = pl.BlockSpec((2, points, pairs, width), lambda slot, step, row, side, owner: (0, 0, 0, 0))
    kept = [] if body is None else [body]
    return pl.pallas_call(
        kernel,
        out_shape=jax.ShapeDtypeStruct((blocks * points, bands * half, 2 * pairs), f32),
        grid_spec=pltpu.PrefetchScalarGridSpec(
            num_scalar_prefetch=3,
            grid=(slots, steps),
            in_specs=[store_spec(index) for index in range(group)]
            + [whole] * len(valences)
            + [pl.BlockSpec(memory_space=pl.ANY)] * len(kept),
            out_specs=pl.BlockSpec(
                (group, bands * half, 2 * pairs),
                lambda slot, step, row, side, owner: (owner[slot] * steps + step, 0, 0),
            ),
        ),
        input_output_aliases={3 + group + len(valences): 0} if kept else {},
        compiler_params=pltpu.CompilerParams(vmem_limit_bytes=VMEM_BYTES),
        cost_estimate=pl.CostEstimate(flops=1, bytes_accessed=1, transcendentals=0),
        name="contract",
    )(row_ids, sides, owners, *([store] * group), *valences, *kept)


def on_device(
    conduction,
    conduction_head,
    valence,
    valence_head,
    screened,
    wing_column,
    wing_row,
    head_value,
    partner,
    pair_select,
    neighbors,
    weights,
    counts,
):
    points = conduction.shape[1]
    half = conduction.shape[2]
    pairs = valence.shape[2]
    block, columns = screened.shape[1], screened.shape[2]
    kpt_count, pw_count, band_count = lax.axis_size("kpt"), lax.axis_size("pw"), lax.axis_size("band")
    kpt, pw, band = lax.axis_index("kpt"), lax.axis_index("pw"), lax.axis_index("band")
    per_index = points // pw_count
    rows = per_index * half
    blocks_here = columns // block
    deep = round_up(block + HEAD_PARTS, 128)
    width = round_up(-(-(columns + 1) // band_count), 128)
    last = band_count - 1
    head_at = columns - last * width

    plane = jnp.arange(deep)
    is_head = (plane >= block) & (plane < block + HEAD_PARTS)
    cut = []
    for index in range(blocks_here):
        padded = jnp.pad(
            conduction[..., index * block : (index + 1) * block], ((0, 0), (0, 0), (0, 0), (0, deep - block))
        )
        cut.append(jnp.where(is_head, conduction_head[..., None], padded))
    cut = jnp.stack(cut).reshape(blocks_here, 2, pw_count, rows, deep)
    selector = (pair_select[:, None] == jnp.arange(pairs)[None, :]).astype(bf16)
    own_valence = valence_columns(valence, valence_head, selector, after(band, cut), width, last)

    dealt = deal(jnp.moveaxis(cut, 2, 0), "pw")
    by_owner = []
    for owner in range(pw_count):
        blocks_of = dealt[0]
        for shift in range(1, pw_count):
            blocks_of = jnp.where((pw - owner) % pw_count == shift, dealt[shift], blocks_of)
        by_owner.append(blocks_of)
    by_block = jnp.concatenate(by_owner, axis=0)
    arrived = deal(by_block, "kpt")
    own_block = arrived[0]
    middle = kpt_count // 2 + 1

    screen = jnp.pad(screened, ((0, 0), (0, deep - block), (0, band_count * width - columns)))
    screen = lax.dynamic_slice_in_dim(screen, band * width, width, 2)
    row_part = jnp.pad(wing_row, ((0, 0), (0, band_count * width - columns)))
    row_part = lax.dynamic_slice_in_dim(row_part, band * width, width, 1)
    first_kpt = kpt == 0
    row_part = jnp.where(first_kpt, row_part, 0)
    corner = []
    rest = head_value
    for _ in range(HEAD_PARTS):
        part = lax.reduce_precision(rest, 8, 7)
        corner.append(jnp.where(first_kpt, part, 0.0))
        rest = rest - part
    corner = jnp.stack(corner, axis=1).astype(bf16)
    column_part = jnp.concatenate(
        [lax.dynamic_slice_in_dim(wing_column, kpt * block, block, 1), corner], axis=1
    )
    column_part = jnp.pad(column_part, ((0, 0), (0, deep - block - HEAD_PARTS)))
    has_column = (pw == 0) & (band == last)
    screen = jnp.where(plane[None, :, None] == block, row_part[:, None, :], screen)
    screen = jnp.where(
        (jnp.arange(width)[None, None, :] == head_at) & has_column, column_part[:, :, None], screen
    )
    right = jnp.stack(
        [
            jnp.concatenate([screen[0], screen[1]], axis=0),
            jnp.concatenate([screen[1], -screen[0]], axis=0),
        ]
    )

    places = jnp.stack(
        [
            ((pw - pw_shift) % pw_count) * band_count + (band - band_shift) % band_count
            for pw_shift in range(pw_count)
            for band_shift in range(band_count)
        ]
    ).astype(jnp.int32)

    live = jnp.where(jnp.arange(neighbors.shape[1])[None, :] < counts[:, None], weights, 0.0)
    all_points = kpt_count * points
    point_of_row = jnp.sum(
        jnp.where(partner[None, :] == jnp.arange(all_points)[:, None], jnp.arange(all_points)[None, :], 0), axis=1
    ).astype(jnp.int32)

    line = [along_line(own_valence, own_valence, "kpt", 1)]
    own_pieces = [own for across in share(own_block[None], "pw") for own in share(across, "band")]
    line.append(along_line(*after(line[0], [own_pieces, arrived[1:middle]]), "kpt", 2))

    pieces = [own_pieces]
    groups = [[0], list(range(1, middle)), list(range(middle, kpt_count))]
    for shifts in groups[1:]:
        group = jnp.stack(after([arrived[shift] for shift in shifts], line[0]))
        pieces.append([own for across in share(group, "pw") for own in share(across, "band")])

    store = None
    for index, shifts in enumerate(groups):
        sources = jnp.stack([((kpt - shift) % kpt_count).astype(jnp.int32) for shift in shifts])
        store = screen_product(
            jnp.append(places, sources), pieces[index], right, per_index, half, store, kpt_count
        )
        if index == 0:
            gates = [store, pieces[1:]]
            for step in range(3, kpt_count):
                line.append(along_line(*after(line[-1], gates), "kpt", step))
            right = after(right, line[1])

    lanes = 2 * pairs
    kept = half // pw_count

    def add_blocks(body, sides, owners, valences):
        sides, owners = jnp.stack(sides).astype(jnp.int32), jnp.stack(owners).astype(jnp.int32)
        row_ids = (owners[:, None] * points + jnp.arange(points)[None, :]).reshape(-1)
        row_ids = jnp.take(point_of_row, row_ids, mode="clip")
        return contract(row_ids, sides, owners, store, valences, body, kpt_count)

    body = add_blocks(None, [jnp.zeros((), jnp.int32)], [kpt], [own_valence])
    for step in range(1, kpt_count):
        has_below, has_above = kpt >= step, kpt + step < kpt_count
        if 2 * step < kpt_count:
            sides = [jnp.where(has_below, 0, 2), jnp.where(has_above, 1, 2)]
            owners = [jnp.where(has_below, kpt - step, kpt), jnp.where(has_above, kpt + step, kpt)]
        else:
            sides = [jnp.where(has_below, 0, jnp.where(has_above, 1, 2))]
            owners = [jnp.where(has_below, kpt - step, jnp.where(has_above, kpt + step, kpt))]
        body = add_blocks(body, sides, owners, [*line[step - 1], own_valence])

    match = neighbors[:, :, None] == point_of_row[None, None, :]
    stencil = jnp.sum(jnp.where(match, live[:, :, None], 0.0), axis=1)
    body = body.reshape(all_points, band_count, half, lanes)
    body = sum(deal(jnp.moveaxis(body, 1, 0), "band"))
    body = body.reshape(all_points, pw_count, kept, lanes)
    body = sum(deal(jnp.moveaxis(body, 1, 0), "pw"))
    fine_here = neighbors.shape[0] // kpt_count
    fine = jnp.dot(stencil, body.reshape(all_points, kept * lanes), precision=highest)
    fine = sum(deal(fine.reshape(kpt_count, fine_here, kept, lanes), "kpt"))
    fine = lax.all_gather(fine, "pw", axis=0)
    fine = fine.reshape(pw_count, fine_here, kept, 2, pairs)
    return jnp.transpose(fine, (3, 1, 0, 2, 4)).reshape(2, fine_here, half * pairs)


def solution(mesh):
    return jax.shard_map(
        on_device,
        mesh=mesh,
        in_specs=(
            P("grp", "kpt", "band", "pw"),
            P("grp", "kpt", "band"),
            P("grp", "kpt", None, "pw"),
            P("grp", "kpt", None),
            P("grp", "kpt", "pw"),
            P("grp", None),
            P("grp", "pw"),
            P("grp"),
            P("grp"),
            P(),
            P(),
            P(),
            P(),
        ),
        out_specs=P("grp", "kpt", "band"),
        check_vma=False,
    )
```

```python
import jax
import jax.numpy as jnp
from jax import lax
from jax.experimental import pallas as pl
from jax.experimental.pallas import tpu as pltpu
from jax.sharding import PartitionSpec as P

highest = lax.Precision.HIGHEST
f32 = jnp.float32
bf16 = jnp.bfloat16
HEAD_PARTS = 3
VMEM_BYTES = 48 * 1024 * 1024


def round_up(value, step):
    return -(-value // step) * step


def shifted(x, name, shift):
    count = lax.axis_size(name)
    pairs = [(source, (source + shift) % count) for source in range(count)]
    return lax.ppermute(x, name, pairs)


def after(x, others):
    return lax.optimization_barrier((x, others))[0]


def share(x, name):
    return [x] + [shifted(x, name, shift) for shift in range(1, lax.axis_size(name))]


def deal(x, name):
    count = lax.axis_size(name)
    me = lax.axis_index(name)
    pieces = []
    for shift in range(count):
        piece = lax.dynamic_index_in_dim(x, (me + shift) % count, 0, keepdims=False)
        pieces.append(shifted(piece, name, shift) if shift else piece)
    return pieces


def valence_columns(valence, valence_head, selector, core, width, last):
    parts, points, pairs, columns = valence.shape
    head_at = columns - last * width

    def kernel(core_ref, valence_ref, head_ref, selector_ref, out_ref):
        column = lax.broadcasted_iota(jnp.int32, (pairs, width), 1)
        at_last = core_ref[0] == last
        limit = jnp.where(at_last, head_at, width)
        head_column = jnp.where(at_last, head_at, width)
        for point in range(points):
            rows = valence_ref[0, point].astype(f32)
            head = jnp.broadcast_to(head_ref[0, point].astype(f32), (pairs, width))
            rows = jnp.where(column < limit, rows, 0.0)
            rows = jnp.where(column == head_column, head, rows)
            moved = jnp.dot(selector_ref[...], rows.astype(bf16), preferred_element_type=f32)
            out_ref[0, point] = moved.astype(bf16)

    return pl.pallas_call(
        kernel,
        out_shape=jax.ShapeDtypeStruct((parts, points, pairs, width), bf16),
        grid_spec=pltpu.PrefetchScalarGridSpec(
            num_scalar_prefetch=1,
            grid=(parts,),
            in_specs=[
                pl.BlockSpec((1, points, pairs, width), lambda x, core: (x, 0, 0, core[0])),
                pl.BlockSpec((1, points, pairs, 1), lambda x, core: (x, 0, 0, 0)),
                pl.BlockSpec((pairs, pairs), lambda x, core: (0, 0)),
            ],
            out_specs=pl.BlockSpec((1, points, pairs, width), lambda x, core: (x, 0, 0, 0)),
        ),
        compiler_params=pltpu.CompilerParams(vmem_limit_bytes=VMEM_BYTES),
        name="valence_columns",
    )(core.reshape(1), valence, valence_head[..., None], selector)


def along_line(below, above, name, step):
    count = lax.axis_size(name)
    below = lax.ppermute(below, name, [(s, s + 1) for s in range(step - 1, count - 1)])
    above = lax.ppermute(above, name, [(s, s - 1) for s in range(1, count - step + 1)])
    return below, above


def screen_product(places, pieces, right, per_index, half, store, blocks):
    _, deep, width = right.shape
    planes = deep // 2
    rows = per_index * half
    count = len(pieces)
    sources = pieces[0].shape[0]
    bands = 2
    pw_count = count // bands
    points = pw_count * per_index
    tile = 512 if width % 512 == 0 else min(256, width)

    def kernel(place_ref, *refs):
        piece_refs, right_ref, out_ref, left_ref = refs[:count], refs[count], refs[-2], refs[-1]

        @pl.when((pl.program_id(1) == 0) & (pl.program_id(2) == 0))
        def _():
            for index in range(count):
                start = pl.multiple_of(place_ref[index] * rows, rows)
                left_ref[pl.ds(start, rows), 0:planes] = piece_refs[index][0, 0]
                left_ref[pl.ds(start, rows), planes:deep] = piece_refs[index][0, 1]

        total = jnp.dot(left_ref[...], right_ref[0], preferred_element_type=f32).astype(bf16)
        for pw in range(pw_count):
            for band in range(bands):
                for point in range(per_index):
                    start = (pw * bands + band) * rows + point * half
                    out_ref[pw * per_index + point, band, 0] = total[start : start + half]

    whole = pl.BlockSpec((1, 2, rows, planes), lambda s, x, n, place: (s, 0, 0, 0))
    kept = [] if store is None else [store]
    return pl.pallas_call(
        kernel,
        out_shape=jax.ShapeDtypeStruct((blocks * points, bands, 2, half, width), bf16),
        grid_spec=pltpu.PrefetchScalarGridSpec(
            num_scalar_prefetch=1,
            grid=(sources, 2, width // tile),
            in_specs=[whole] * count
            + [pl.BlockSpec((1, deep, tile), lambda s, x, n, place: (x, 0, n))]
            + [pl.BlockSpec(memory_space=pl.ANY)] * len(kept),
            out_specs=pl.BlockSpec(
                (points, bands, 1, half, tile), lambda s, x, n, place: (place[count + s], 0, x, 0, n)
            ),
            scratch_shapes=[pltpu.VMEM((count * rows, deep), bf16)],
        ),
        input_output_aliases={count + 2: 0} if kept else {},
        compiler_params=pltpu.CompilerParams(vmem_limit_bytes=VMEM_BYTES),
        cost_estimate=pl.CostEstimate(flops=1, bytes_accessed=1, transcendentals=0),
        name="screen_product",
    )(places, *pieces, right, *kept)


def contract(row_ids, sides, owners, store, valences, body, blocks):
    _, bands, _, half, width = store.shape
    _, points, pairs, _ = valences[0].shape
    slots = sides.shape[0]
    group = 2 if points % 2 == 0 else 1
    steps = points // group

    def kernel(row_ref, side_ref, owner_ref, *refs):
        store_refs, valence_refs, out_ref = refs[:group], refs[group : group + len(valences)], refs[-1]
        lane = lax.broadcasted_iota(jnp.int32, (half, 2 * pairs), 1)
        side = side_ref[pl.program_id(0)]

        def rows_of(valence_ref):
            for index in range(group):
                left = store_refs[index][0].reshape(bands * 2 * half, width)
                right = valence_ref[:, index].reshape(2 * pairs, width)
                square = lax.dot_general(left, right, (((1,), (1,)), ((), ())), preferred_element_type=f32)
                for band in range(bands):
                    first = square[2 * band * half : (2 * band + 1) * half]
                    second = square[(2 * band + 1) * half : (2 * band + 2) * half]
                    turned = pltpu.roll(second, pairs, 1)
                    total = first + jnp.where(lane < pairs, -turned, turned)
                    out_ref[index, band * half : (band + 1) * half, :] = total

        for place in range(len(valences)):

            @pl.when(side == place)
            def _(place=place):
                rows_of(valence_refs[place])

    def store_spec(index):
        return pl.BlockSpec(
            (1, bands, 2, half, width),
            lambda slot, step, row, side, owner: (row[slot * points + step * group + index], 0, 0, 0, 0),
        )

    def valence_spec(place):
        return pl.BlockSpec(
            (2, group, pairs, width),
            lambda slot, step, row, side, owner: (0, jnp.where(side[slot] == place, step, 0), 0, 0),
        )

    kept = [] if body is None else [body]
    return pl.pallas_call(
        kernel,
        out_shape=jax.ShapeDtypeStruct((blocks * points, bands * half, 2 * pairs), f32),
        grid_spec=pltpu.PrefetchScalarGridSpec(
            num_scalar_prefetch=3,
            grid=(slots, steps),
            in_specs=[store_spec(index) for index in range(group)]
            + [valence_spec(place) for place in range(len(valences))]
            + [pl.BlockSpec(memory_space=pl.ANY)] * len(kept),
            out_specs=pl.BlockSpec(
                (group, bands * half, 2 * pairs),
                lambda slot, step, row, side, owner: (owner[slot] * steps + step, 0, 0),
            ),
        ),
        input_output_aliases={3 + group + len(valences): 0} if kept else {},
        compiler_params=pltpu.CompilerParams(vmem_limit_bytes=VMEM_BYTES),
        cost_estimate=pl.CostEstimate(flops=1, bytes_accessed=1, transcendentals=0),
        name="contract",
    )(row_ids, sides, owners, *([store] * group), *valences, *kept)


def on_device(
    conduction,
    conduction_head,
    valence,
    valence_head,
    screened,
    wing_column,
    wing_row,
    head_value,
    partner,
    pair_select,
    neighbors,
    weights,
    counts,
):
    points = conduction.shape[1]
    half = conduction.shape[2]
    pairs = valence.shape[2]
    block, columns = screened.shape[1], screened.shape[2]
    kpt_count, pw_count, band_count = lax.axis_size("kpt"), lax.axis_size("pw"), lax.axis_size("band")
    kpt, pw, band = lax.axis_index("kpt"), lax.axis_index("pw"), lax.axis_index("band")
    per_index = points // pw_count
    rows = per_index * half
    blocks_here = columns // block
    deep = round_up(block + HEAD_PARTS, 128)
    width = round_up(-(-(columns + 1) // band_count), 128)
    last = band_count - 1
    head_at = columns - last * width

    selector = (pair_select[:, None] == jnp.arange(pairs)[None, :]).astype(bf16)
    own_valence = valence_columns(valence, valence_head, selector, band, width, last)
    line = [along_line(own_valence, own_valence, "kpt", 1)]

    plane = jnp.arange(deep)
    is_head = (plane >= block) & (plane < block + HEAD_PARTS)
    cut = []
    for index in range(blocks_here):
        padded = jnp.pad(
            conduction[..., index * block : (index + 1) * block], ((0, 0), (0, 0), (0, 0), (0, deep - block))
        )
        cut.append(jnp.where(is_head, conduction_head[..., None], padded))
    cut = jnp.stack(cut).reshape(blocks_here, 2, pw_count, rows, deep)
    dealt = deal(jnp.moveaxis(cut, 2, 0), "pw")
    by_owner = []
    for owner in range(pw_count):
        blocks_of = dealt[0]
        for shift in range(1, pw_count):
            blocks_of = jnp.where((pw - owner) % pw_count == shift, dealt[shift], blocks_of)
        by_owner.append(blocks_of)
    by_block = jnp.concatenate(by_owner, axis=0)
    arrived = deal(by_block, "kpt")
    own_block = arrived[0]
    middle = kpt_count // 2 + 1

    screen = jnp.pad(screened, ((0, 0), (0, deep - block), (0, band_count * width - columns)))
    screen = lax.dynamic_slice_in_dim(screen, band * width, width, 2)
    row_part = jnp.pad(wing_row, ((0, 0), (0, band_count * width - columns)))
    row_part = lax.dynamic_slice_in_dim(row_part, band * width, width, 1)
    first_kpt = kpt == 0
    row_part = jnp.where(first_kpt, row_part, 0)
    corner = []
    rest = head_value
    for _ in range(HEAD_PARTS):
        part = lax.reduce_precision(rest, 8, 7)
        corner.append(jnp.where(first_kpt, part, 0.0))
        rest = rest - part
    corner = jnp.stack(corner, axis=1).astype(bf16)
    column_part = jnp.concatenate(
        [lax.dynamic_slice_in_dim(wing_column, kpt * block, block, 1), corner], axis=1
    )
    column_part = jnp.pad(column_part, ((0, 0), (0, deep - block - HEAD_PARTS)))
    has_column = (pw == 0) & (band == last)
    screen = jnp.where(plane[None, :, None] == block, row_part[:, None, :], screen)
    screen = jnp.where(
        (jnp.arange(width)[None, None, :] == head_at) & has_column, column_part[:, :, None], screen
    )
    right = jnp.stack(
        [
            jnp.concatenate([screen[0], screen[1]], axis=0),
            jnp.concatenate([screen[1], -screen[0]], axis=0),
        ]
    )

    places = jnp.stack(
        [
            ((pw - pw_shift) % pw_count) * band_count + (band - band_shift) % band_count
            for pw_shift in range(pw_count)
            for band_shift in range(band_count)
        ]
    ).astype(jnp.int32)

    live = jnp.where(jnp.arange(neighbors.shape[1])[None, :] < counts[:, None], weights, 0.0)
    all_points = kpt_count * points
    point_of_row = jnp.sum(
        jnp.where(partner[None, :] == jnp.arange(all_points)[:, None], jnp.arange(all_points)[None, :], 0), axis=1
    ).astype(jnp.int32)

    def spread(group):
        return [own for across in share(group, "pw") for own in share(across, "band")]

    def product(shifts, pieces, right, store):
        sources = jnp.stack([((kpt - shift) % kpt_count).astype(jnp.int32) for shift in shifts])
        where = jnp.append(places, sources)
        return screen_product(where, pieces, right, per_index, half, store, kpt_count)

    near, far = list(range(1, middle)), list(range(middle, kpt_count))
    store = product([0], spread(own_block[None]), right, None)
    line.append(along_line(*after(line[0], store), "kpt", 2))
    near_group = jnp.stack(after([arrived[shift] for shift in near], [store, line[0]]))
    near_pieces = spread(near_group)
    far_pieces = spread(jnp.stack([arrived[shift] for shift in far]))
    store = product(near, near_pieces, right, store)
    for step in range(3, kpt_count):
        line.append(along_line(*after(line[-1], [store, far_pieces]), "kpt", step))
    store = product(far, far_pieces, after(right, line[1]), store)

    lanes = 2 * pairs
    kept = half // pw_count

    def add_blocks(body, sides, owners, valences):
        sides, owners = jnp.stack(sides).astype(jnp.int32), jnp.stack(owners).astype(jnp.int32)
        row_ids = (owners[:, None] * points + jnp.arange(points)[None, :]).reshape(-1)
        row_ids = jnp.take(point_of_row, row_ids, mode="clip")
        return contract(row_ids, sides, owners, store, valences, body, kpt_count)

    body = add_blocks(None, [jnp.zeros((), jnp.int32)], [kpt], [own_valence])
    for step in range(1, kpt_count):
        has_below, has_above = kpt >= step, kpt + step < kpt_count
        if 2 * step < kpt_count:
            sides = [jnp.where(has_below, 0, 2), jnp.where(has_above, 1, 2)]
            owners = [jnp.where(has_below, kpt - step, kpt), jnp.where(has_above, kpt + step, kpt)]
        else:
            sides = [jnp.where(has_below, 0, jnp.where(has_above, 1, 2))]
            owners = [jnp.where(has_below, kpt - step, jnp.where(has_above, kpt + step, kpt))]
        body = add_blocks(body, sides, owners, [*line[step - 1], own_valence])

    match = neighbors[:, :, None] == point_of_row[None, None, :]
    stencil = jnp.sum(jnp.where(match, live[:, :, None], 0.0), axis=1)
    body = body.reshape(all_points, band_count, half, lanes)
    body = sum(deal(jnp.moveaxis(body, 1, 0), "band"))
    body = body.reshape(all_points, pw_count, kept, lanes)
    body = sum(deal(jnp.moveaxis(body, 1, 0), "pw"))
    fine_here = neighbors.shape[0] // kpt_count
    fine = jnp.dot(stencil, body.reshape(all_points, kept * lanes), precision=highest)
    fine = sum(deal(fine.reshape(kpt_count, fine_here, kept, lanes), "kpt"))
    fine = lax.all_gather(fine, "pw", axis=0)
    fine = fine.reshape(pw_count, fine_here, kept, 2, pairs)
    return jnp.transpose(fine, (3, 1, 0, 2, 4)).reshape(2, fine_here, half * pairs)


def solution(mesh):
    return jax.shard_map(
        on_device,
        mesh=mesh,
        in_specs=(
            P("grp", "kpt", "band", "pw"),
            P("grp", "kpt", "band"),
            P("grp", "kpt", None, "pw"),
            P("grp", "kpt", None),
            P("grp", "kpt", "pw"),
            P("grp", None),
            P("grp", "pw"),
            P("grp"),
            P("grp"),
            P(),
            P(),
            P(),
            P(),
        ),
        out_specs=P("grp", "kpt", "band"),
        check_vma=False,
    )
```

```python
import jax
import jax.numpy as jnp
from jax import lax
from jax.experimental import pallas as pl
from jax.experimental.pallas import tpu as pltpu
from jax.sharding import PartitionSpec as P

highest = lax.Precision.HIGHEST
f32 = jnp.float32
bf16 = jnp.bfloat16
HEAD_PARTS = 3
VMEM_BYTES = 48 * 1024 * 1024


def round_up(value, step):
    return -(-value // step) * step


def shifted(x, name, shift):
    count = lax.axis_size(name)
    pairs = [(source, (source + shift) % count) for source in range(count)]
    return lax.ppermute(x, name, pairs)


def after(x, others):
    return lax.optimization_barrier((x, others))[0]


def share(x, name):
    return [x] + [shifted(x, name, shift) for shift in range(1, lax.axis_size(name))]


def deal(x, name):
    count = lax.axis_size(name)
    me = lax.axis_index(name)
    pieces = []
    for shift in range(count):
        piece = lax.dynamic_index_in_dim(x, (me + shift) % count, 0, keepdims=False)
        pieces.append(shifted(piece, name, shift) if shift else piece)
    return pieces


def valence_columns(valence, valence_head, selector, core, width, last):
    parts, points, pairs, columns = valence.shape
    head_at = columns - last * width

    def kernel(core_ref, valence_ref, head_ref, selector_ref, out_ref):
        column = lax.broadcasted_iota(jnp.int32, (pairs, width), 1)
        at_last = core_ref[0] == last
        limit = jnp.where(at_last, head_at, width)
        head_column = jnp.where(at_last, head_at, width)
        for point in range(points):
            rows = valence_ref[0, point].astype(f32)
            head = jnp.broadcast_to(head_ref[0, point].astype(f32), (pairs, width))
            rows = jnp.where(column < limit, rows, 0.0)
            rows = jnp.where(column == head_column, head, rows)
            moved = jnp.dot(selector_ref[...], rows.astype(bf16), preferred_element_type=f32)
            out_ref[0, point] = moved.astype(bf16)

    return pl.pallas_call(
        kernel,
        out_shape=jax.ShapeDtypeStruct((parts, points, pairs, width), bf16),
        grid_spec=pltpu.PrefetchScalarGridSpec(
            num_scalar_prefetch=1,
            grid=(parts,),
            in_specs=[
                pl.BlockSpec((1, points, pairs, width), lambda x, core: (x, 0, 0, core[0])),
                pl.BlockSpec((1, points, pairs, 1), lambda x, core: (x, 0, 0, 0)),
                pl.BlockSpec((pairs, pairs), lambda x, core: (0, 0)),
            ],
            out_specs=pl.BlockSpec((1, points, pairs, width), lambda x, core: (x, 0, 0, 0)),
        ),
        compiler_params=pltpu.CompilerParams(vmem_limit_bytes=VMEM_BYTES),
        name="valence_columns",
    )(core.reshape(1), valence, valence_head[..., None], selector)


def along_line(below, above, name, step):
    count = lax.axis_size(name)
    below = lax.ppermute(below, name, [(s, s + 1) for s in range(step - 1, count - 1)])
    above = lax.ppermute(above, name, [(s, s - 1) for s in range(1, count - step + 1)])
    return below, above


def screen_product(places, pieces, right, per_index, half, store, blocks):
    _, deep, width = right.shape
    planes = deep // 2
    rows = per_index * half
    count = len(pieces)
    sources = pieces[0].shape[0]
    bands = 2
    pw_count = count // bands
    points = pw_count * per_index
    tile = 512 if width % 512 == 0 else min(256, width)

    def kernel(place_ref, *refs):
        piece_refs, right_ref, out_ref, left_ref = refs[:count], refs[count], refs[-2], refs[-1]

        @pl.when((pl.program_id(1) == 0) & (pl.program_id(2) == 0))
        def _():
            for index in range(count):
                start = pl.multiple_of(place_ref[index] * rows, rows)
                left_ref[pl.ds(start, rows), 0:planes] = piece_refs[index][0, 0]
                left_ref[pl.ds(start, rows), planes:deep] = piece_refs[index][0, 1]

        total = jnp.dot(left_ref[...], right_ref[0], preferred_element_type=f32).astype(bf16)
        for pw in range(pw_count):
            for band in range(bands):
                for point in range(per_index):
                    start = (pw * bands + band) * rows + point * half
                    out_ref[pw * per_index + point, band, 0] = total[start : start + half]

    whole = pl.BlockSpec((1, 2, rows, planes), lambda s, x, n, place: (s, 0, 0, 0))
    kept = [] if store is None else [store]
    return pl.pallas_call(
        kernel,
        out_shape=jax.ShapeDtypeStruct((blocks * points, bands, 2, half, width), bf16),
        grid_spec=pltpu.PrefetchScalarGridSpec(
            num_scalar_prefetch=1,
            grid=(sources, 2, width // tile),
            in_specs=[whole] * count
            + [pl.BlockSpec((1, deep, tile), lambda s, x, n, place: (x, 0, n))]
            + [pl.BlockSpec(memory_space=pl.ANY)] * len(kept),
            out_specs=pl.BlockSpec(
                (points, bands, 1, half, tile), lambda s, x, n, place: (place[count + s], 0, x, 0, n)
            ),
            scratch_shapes=[pltpu.VMEM((count * rows, deep), bf16)],
        ),
        input_output_aliases={count + 2: 0} if kept else {},
        compiler_params=pltpu.CompilerParams(vmem_limit_bytes=VMEM_BYTES),
        cost_estimate=pl.CostEstimate(flops=1, bytes_accessed=1, transcendentals=0),
        name="screen_product",
    )(places, *pieces, right, *kept)


def contract(row_ids, sides, owners, store, valences, body, blocks):
    _, bands, _, half, width = store.shape
    _, points, pairs, _ = valences[0].shape
    slots = sides.shape[0]
    group = 2 if points % 2 == 0 else 1
    steps = points // group

    def kernel(row_ref, side_ref, owner_ref, *refs):
        store_refs, valence_refs, out_ref = refs[:group], refs[group : group + len(valences)], refs[-1]
        lane = lax.broadcasted_iota(jnp.int32, (half, 2 * pairs), 1)
        side = side_ref[pl.program_id(0)]

        def rows_of(valence_ref):
            for index in range(group):
                left = store_refs[index][0].reshape(bands * 2 * half, width)
                right = valence_ref[:, index].reshape(2 * pairs, width)
                square = lax.dot_general(left, right, (((1,), (1,)), ((), ())), preferred_element_type=f32)
                for band in range(bands):
                    first = square[2 * band * half : (2 * band + 1) * half]
                    second = square[(2 * band + 1) * half : (2 * band + 2) * half]
                    turned = pltpu.roll(second, pairs, 1)
                    total = first + jnp.where(lane < pairs, -turned, turned)
                    out_ref[index, band * half : (band + 1) * half, :] = total

        for place in range(len(valences)):

            @pl.when(side == place)
            def _(place=place):
                rows_of(valence_refs[place])

    def store_spec(index):
        return pl.BlockSpec(
            (1, bands, 2, half, width),
            lambda slot, step, row, side, owner: (row[slot * points + step * group + index], 0, 0, 0, 0),
        )

    def valence_spec(place):
        return pl.BlockSpec(
            (2, group, pairs, width),
            lambda slot, step, row, side, owner: (0, jnp.where(side[slot] == place, step, 0), 0, 0),
        )

    kept = [] if body is None else [body]
    return pl.pallas_call(
        kernel,
        out_shape=jax.ShapeDtypeStruct((blocks * points, bands * half, 2 * pairs), f32),
        grid_spec=pltpu.PrefetchScalarGridSpec(
            num_scalar_prefetch=3,
            grid=(slots, steps),
            in_specs=[store_spec(index) for index in range(group)]
            + [valence_spec(place) for place in range(len(valences))]
            + [pl.BlockSpec(memory_space=pl.ANY)] * len(kept),
            out_specs=pl.BlockSpec(
                (group, bands * half, 2 * pairs),
                lambda slot, step, row, side, owner: (owner[slot] * steps + step, 0, 0),
            ),
        ),
        input_output_aliases={3 + group + len(valences): 0} if kept else {},
        compiler_params=pltpu.CompilerParams(vmem_limit_bytes=VMEM_BYTES),
        cost_estimate=pl.CostEstimate(flops=1, bytes_accessed=1, transcendentals=0),
        name="contract",
    )(row_ids, sides, owners, *([store] * group), *valences, *kept)


def on_device(
    conduction,
    conduction_head,
    valence,
    valence_head,
    screened,
    wing_column,
    wing_row,
    head_value,
    partner,
    pair_select,
    neighbors,
    weights,
    counts,
):
    points = conduction.shape[1]
    half = conduction.shape[2]
    pairs = valence.shape[2]
    block, columns = screened.shape[1], screened.shape[2]
    kpt_count, pw_count, band_count = lax.axis_size("kpt"), lax.axis_size("pw"), lax.axis_size("band")
    kpt, pw, band = lax.axis_index("kpt"), lax.axis_index("pw"), lax.axis_index("band")
    per_index = points // pw_count
    rows = per_index * half
    blocks_here = columns // block
    deep = round_up(block + HEAD_PARTS, 128)
    width = round_up(-(-(columns + 1) // band_count), 128)
    last = band_count - 1
    head_at = columns - last * width

    halves = jnp.moveaxis(conduction.reshape(2, pw_count, per_index, half, columns), 1, 0)
    first = halves if pw_count == 1 else lax.dynamic_index_in_dim(halves, (pw + 1) % pw_count, 0, keepdims=False)
    dealt = deal(halves, "pw")

    selector = (pair_select[:, None] == jnp.arange(pairs)[None, :]).astype(bf16)
    own_valence = valence_columns(valence, valence_head, selector, after(band, first), width, last)
    line = [along_line(own_valence, own_valence, "kpt", 1)]

    plane = jnp.arange(deep)
    is_head = (plane >= block) & (plane < block + HEAD_PARTS)
    heads = lax.dynamic_slice_in_dim(conduction_head, pw * per_index, per_index, 1)
    by_block = []
    for owner in range(pw_count):
        whole = dealt[0]
        for shift in range(1, pw_count):
            whole = jnp.where((pw - owner) % pw_count == shift, dealt[shift], whole)
        for index in range(blocks_here):
            cut = jnp.pad(
                whole[..., index * block : (index + 1) * block], ((0, 0), (0, 0), (0, 0), (0, deep - block))
            )
            by_block.append(jnp.where(is_head, heads[..., None], cut).reshape(2, rows, deep))
    by_block = jnp.stack(by_block)
    arrived = deal(by_block, "kpt")
    own_block = arrived[0]
    middle = kpt_count // 2 + 1

    screen = jnp.pad(screened, ((0, 0), (0, deep - block), (0, band_count * width - columns)))
    screen = lax.dynamic_slice_in_dim(screen, band * width, width, 2)
    row_part = jnp.pad(wing_row, ((0, 0), (0, band_count * width - columns)))
    row_part = lax.dynamic_slice_in_dim(row_part, band * width, width, 1)
    first_kpt = kpt == 0
    row_part = jnp.where(first_kpt, row_part, 0)
    corner = []
    rest = head_value
    for _ in range(HEAD_PARTS):
        part = lax.reduce_precision(rest, 8, 7)
        corner.append(jnp.where(first_kpt, part, 0.0))
        rest = rest - part
    corner = jnp.stack(corner, axis=1).astype(bf16)
    column_part = jnp.concatenate(
        [lax.dynamic_slice_in_dim(wing_column, kpt * block, block, 1), corner], axis=1
    )
    column_part = jnp.pad(column_part, ((0, 0), (0, deep - block - HEAD_PARTS)))
    has_column = (pw == 0) & (band == last)
    screen = jnp.where(plane[None, :, None] == block, row_part[:, None, :], screen)
    screen = jnp.where(
        (jnp.arange(width)[None, None, :] == head_at) & has_column, column_part[:, :, None], screen
    )
    right = jnp.stack(
        [
            jnp.concatenate([screen[0], screen[1]], axis=0),
            jnp.concatenate([screen[1], -screen[0]], axis=0),
        ]
    )

    places = jnp.stack(
        [
            ((pw - pw_shift) % pw_count) * band_count + (band - band_shift) % band_count
            for pw_shift in range(pw_count)
            for band_shift in range(band_count)
        ]
    ).astype(jnp.int32)

    live = jnp.where(jnp.arange(neighbors.shape[1])[None, :] < counts[:, None], weights, 0.0)
    all_points = kpt_count * points
    point_of_row = jnp.sum(
        jnp.where(partner[None, :] == jnp.arange(all_points)[:, None], jnp.arange(all_points)[None, :], 0), axis=1
    ).astype(jnp.int32)

    def spread(group):
        return [own for across in share(group, "pw") for own in share(across, "band")]

    def product(shifts, pieces, right, store):
        sources = jnp.stack([((kpt - shift) % kpt_count).astype(jnp.int32) for shift in shifts])
        where = jnp.append(places, sources)
        return screen_product(where, pieces, right, per_index, half, store, kpt_count)

    near, far = list(range(1, middle)), list(range(middle, kpt_count))
    store = product([0], spread(own_block[None]), right, None)
    near_group = jnp.stack(after([arrived[shift] for shift in near], [store, line[0]]))
    near_pieces = spread(near_group)
    line.append(along_line(*after(line[0], [store, near_group, [arrived[shift] for shift in far]]), "kpt", 2))
    far_pieces = spread(jnp.stack([arrived[shift] for shift in far]))
    store = product(near, near_pieces, right, store)
    for step in range(3, kpt_count):
        line.append(along_line(*after(line[-1], [store, far_pieces]), "kpt", step))
    store = product(far, far_pieces, after(right, line[1]), store)

    lanes = 2 * pairs
    kept = half // pw_count

    def add_blocks(body, sides, owners, valences, targets, blocks):
        sides, owners = jnp.stack(sides).astype(jnp.int32), jnp.stack(owners)
        targets = jnp.stack(targets).astype(jnp.int32)
        row_ids = (owners[:, None] * points + jnp.arange(points)[None, :]).reshape(-1)
        row_ids = jnp.take(point_of_row, row_ids, mode="clip")
        return contract(row_ids, sides, targets, store, valences, body, blocks)

    def summed(body):
        body = body.reshape(-1, band_count, half, lanes)
        body = sum(deal(jnp.moveaxis(body, 1, 0), "band"))
        body = body.reshape(-1, pw_count, kept, lanes)
        return sum(deal(jnp.moveaxis(body, 1, 0), "pw")).reshape(-1, kept * lanes)

    body = add_blocks(None, [jnp.zeros((), jnp.int32)], [kpt], [own_valence], [kpt], kpt_count)
    for step in range(1, kpt_count):
        has_below, has_above = kpt >= step, kpt + step < kpt_count
        if 2 * step < kpt_count:
            sides = [jnp.where(has_below, 0, 2), jnp.where(has_above, 1, 2)]
            owners = [jnp.where(has_below, kpt - step, kpt), jnp.where(has_above, kpt + step, kpt)]
        else:
            sides = [jnp.where(has_below, 0, jnp.where(has_above, 1, 2))]
            owners = [jnp.where(has_below, kpt - step, jnp.where(has_above, kpt + step, kpt))]
        valences = [*line[step - 1], own_valence]
        if step < kpt_count - 1:
            body = add_blocks(body, sides, owners, valences, owners, kpt_count)
    early = summed(body)
    last_owner = owners[-1]
    late = summed(add_blocks(None, sides[-1:], owners[-1:], valences, [jnp.zeros((), jnp.int32)], 1))

    match = neighbors[:, :, None] == point_of_row[None, None, :]
    stencil = jnp.sum(jnp.where(match, live[:, :, None], 0.0), axis=1)
    is_late = jnp.arange(all_points) // points == last_owner
    fine = jnp.dot(stencil, jnp.where(is_late[:, None], 0.0, early), precision=highest)
    late_stencil = lax.dynamic_slice_in_dim(stencil, last_owner * points, points, 1)
    fine = fine + jnp.dot(late_stencil, late, precision=highest)
    fine_here = neighbors.shape[0] // kpt_count
    fine = sum(deal(fine.reshape(kpt_count, fine_here, kept, lanes), "kpt"))
    fine = lax.all_gather(fine, "pw", axis=0)
    fine = fine.reshape(pw_count, fine_here, kept, 2, pairs)
    return jnp.transpose(fine, (3, 1, 0, 2, 4)).reshape(2, fine_here, half * pairs)


def solution(mesh):
    return jax.shard_map(
        on_device,
        mesh=mesh,
        in_specs=(
            P("grp", "kpt", "band", "pw"),
            P("grp", "kpt", "band"),
            P("grp", "kpt", None, "pw"),
            P("grp", "kpt", None),
            P("grp", "kpt", "pw"),
            P("grp", None),
            P("grp", "pw"),
            P("grp"),
            P("grp"),
            P(),
            P(),
            P(),
            P(),
        ),
        out_specs=P("grp", "kpt", "band"),
        check_vma=False,
    )
```

```python
import jax
import jax.numpy as jnp
from jax import lax
from jax.experimental import pallas as pl
from jax.experimental.pallas import tpu as pltpu
from jax.sharding import PartitionSpec as P

highest = lax.Precision.HIGHEST
f32 = jnp.float32
bf16 = jnp.bfloat16
HEAD_PARTS = 3
VMEM_BYTES = 48 * 1024 * 1024


def round_up(value, step):
    return -(-value // step) * step


def shifted(x, name, shift):
    count = lax.axis_size(name)
    pairs = [(source, (source + shift) % count) for source in range(count)]
    return lax.ppermute(x, name, pairs)


def after(x, others):
    return lax.optimization_barrier((x, others))[0]


def share(x, name):
    return [x] + [shifted(x, name, shift) for shift in range(1, lax.axis_size(name))]


def deal(x, name):
    count = lax.axis_size(name)
    me = lax.axis_index(name)
    pieces = []
    for shift in range(count):
        piece = lax.dynamic_index_in_dim(x, (me + shift) % count, 0, keepdims=False)
        pieces.append(shifted(piece, name, shift) if shift else piece)
    return pieces


def valence_columns(valence, valence_head, selector, core, width, last):
    parts, points, pairs, columns = valence.shape
    head_at = columns - last * width

    def kernel(core_ref, valence_ref, head_ref, selector_ref, out_ref):
        column = lax.broadcasted_iota(jnp.int32, (pairs, width), 1)
        at_last = core_ref[0] == last
        limit = jnp.where(at_last, head_at, width)
        head_column = jnp.where(at_last, head_at, width)
        for point in range(points):
            rows = valence_ref[0, point].astype(f32)
            head = jnp.broadcast_to(head_ref[0, point].astype(f32), (pairs, width))
            rows = jnp.where(column < limit, rows, 0.0)
            rows = jnp.where(column == head_column, head, rows)
            moved = jnp.dot(selector_ref[...], rows.astype(bf16), preferred_element_type=f32)
            out_ref[0, point] = moved.astype(bf16)

    return pl.pallas_call(
        kernel,
        out_shape=jax.ShapeDtypeStruct((parts, points, pairs, width), bf16),
        grid_spec=pltpu.PrefetchScalarGridSpec(
            num_scalar_prefetch=1,
            grid=(parts,),
            in_specs=[
                pl.BlockSpec((1, points, pairs, width), lambda x, core: (x, 0, 0, core[0])),
                pl.BlockSpec((1, points, pairs, 1), lambda x, core: (x, 0, 0, 0)),
                pl.BlockSpec((pairs, pairs), lambda x, core: (0, 0)),
            ],
            out_specs=pl.BlockSpec((1, points, pairs, width), lambda x, core: (x, 0, 0, 0)),
        ),
        compiler_params=pltpu.CompilerParams(vmem_limit_bytes=VMEM_BYTES),
        name="valence_columns",
    )(core.reshape(1), valence, valence_head[..., None], selector)


def one_way(below, above, pairs_below, pairs_above, name):
    senders = [pair[0] for pair in pairs_below + pairs_above]
    takers = [pair[1] for pair in pairs_below + pairs_above]
    if len(set(senders)) < len(senders) or len(set(takers)) < len(takers):
        return lax.ppermute(below, name, pairs_below), lax.ppermute(above, name, pairs_above)
    sent = below
    if above is not below:
        sends_below = jnp.isin(lax.axis_index(name), jnp.array([pair[0] for pair in pairs_below]))
        sent = jnp.where(sends_below, below, above)
    moved = lax.ppermute(sent, name, pairs_below + pairs_above)
    return moved, moved


def line_pairs(count, step):
    below = [(s, s + 1) for s in range(step - 1, count - 1)]
    above = [(s, s - 1) for s in range(1, count - step + 1)]
    to_ends = [[pair for pair in below if pair[1] == count - 1], [pair for pair in above if pair[1] == 0]]
    to_others = [[pair for pair in below if pair[1] < count - 1], [pair for pair in above if pair[1] > 0]]
    return to_ends, to_others


def screen_product(places, pieces, right, per_index, half, store, blocks):
    _, deep, width = right.shape
    planes = deep // 2
    rows = per_index * half
    count = len(pieces)
    sources = pieces[0].shape[0]
    bands = 2
    pw_count = count // bands
    points = pw_count * per_index
    tile = 512 if width % 512 == 0 else min(256, width)

    def kernel(place_ref, *refs):
        piece_refs, right_ref, out_ref, left_ref = refs[:count], refs[count], refs[-2], refs[-1]

        @pl.when((pl.program_id(1) == 0) & (pl.program_id(2) == 0))
        def _():
            for index in range(count):
                start = pl.multiple_of(place_ref[index] * rows, rows)
                left_ref[pl.ds(start, rows), 0:planes] = piece_refs[index][0, 0]
                left_ref[pl.ds(start, rows), planes:deep] = piece_refs[index][0, 1]

        total = jnp.dot(left_ref[...], right_ref[0], preferred_element_type=f32).astype(bf16)
        for pw in range(pw_count):
            for band in range(bands):
                for point in range(per_index):
                    start = (pw * bands + band) * rows + point * half
                    out_ref[pw * per_index + point, band, 0] = total[start : start + half]

    whole = pl.BlockSpec((1, 2, rows, planes), lambda s, x, n, place: (s, 0, 0, 0))
    kept = [] if store is None else [store]
    return pl.pallas_call(
        kernel,
        out_shape=jax.ShapeDtypeStruct((blocks * points, bands, 2, half, width), bf16),
        grid_spec=pltpu.PrefetchScalarGridSpec(
            num_scalar_prefetch=1,
            grid=(sources, 2, width // tile),
            in_specs=[whole] * count
            + [pl.BlockSpec((1, deep, tile), lambda s, x, n, place: (x, 0, n))]
            + [pl.BlockSpec(memory_space=pl.ANY)] * len(kept),
            out_specs=pl.BlockSpec(
                (points, bands, 1, half, tile), lambda s, x, n, place: (place[count + s], 0, x, 0, n)
            ),
            scratch_shapes=[pltpu.VMEM((count * rows, deep), bf16)],
        ),
        input_output_aliases={count + 2: 0} if kept else {},
        compiler_params=pltpu.CompilerParams(vmem_limit_bytes=VMEM_BYTES),
        cost_estimate=pl.CostEstimate(flops=1, bytes_accessed=1, transcendentals=0),
        name="screen_product",
    )(places, *pieces, right, *kept)


def contract(row_ids, sides, owners, store, valences, body, blocks):
    _, bands, _, half, width = store.shape
    _, _, pairs, _ = valences[0][0].shape
    points = sum(part.shape[1] for part in valences[0])
    slots = sides.shape[0]
    group = 2 if points % 2 == 0 else 1
    steps = points // group
    given, places = [], []
    for side, parts in enumerate(valences):
        first = 0
        for part in parts:
            given.append(part)
            places.append((side, first, first + part.shape[1] // group))
            first = places[-1][2]

    def kernel(row_ref, side_ref, owner_ref, *refs):
        store_refs, valence_refs, out_ref = refs[:group], refs[group : group + len(given)], refs[-1]
        lane = lax.broadcasted_iota(jnp.int32, (half, 2 * pairs), 1)
        side = side_ref[pl.program_id(0)]
        step = pl.program_id(1)

        def rows_of(valence_ref):
            for index in range(group):
                left = store_refs[index][0].reshape(bands * 2 * half, width)
                right = valence_ref[:, index].reshape(2 * pairs, width)
                square = lax.dot_general(left, right, (((1,), (1,)), ((), ())), preferred_element_type=f32)
                for band in range(bands):
                    first = square[2 * band * half : (2 * band + 1) * half]
                    second = square[(2 * band + 1) * half : (2 * band + 2) * half]
                    turned = pltpu.roll(second, pairs, 1)
                    total = first + jnp.where(lane < pairs, -turned, turned)
                    out_ref[index, band * half : (band + 1) * half, :] = total

        for valence_ref, (place, first, end) in zip(valence_refs, places):

            @pl.when((side == place) & (step >= first) & (step < end))
            def _(valence_ref=valence_ref):
                rows_of(valence_ref)

    def store_spec(index):
        return pl.BlockSpec(
            (1, bands, 2, half, width),
            lambda slot, step, row, side, owner: (row[slot * points + step * group + index], 0, 0, 0, 0),
        )

    def valence_spec(place, first, end):
        return pl.BlockSpec(
            (2, group, pairs, width),
            lambda slot, step, row, side, owner: (
                0,
                jnp.where((side[slot] == place) & (step >= first) & (step < end), step - first, 0),
                0,
                0,
            ),
        )

    kept = [] if body is None else [body]
    return pl.pallas_call(
        kernel,
        out_shape=jax.ShapeDtypeStruct((blocks * points, bands * half, 2 * pairs), f32),
        grid_spec=pltpu.PrefetchScalarGridSpec(
            num_scalar_prefetch=3,
            grid=(slots, steps),
            in_specs=[store_spec(index) for index in range(group)]
            + [valence_spec(*place) for place in places]
            + [pl.BlockSpec(memory_space=pl.ANY)] * len(kept),
            out_specs=pl.BlockSpec(
                (group, bands * half, 2 * pairs),
                lambda slot, step, row, side, owner: (owner[slot] * steps + step, 0, 0),
            ),
        ),
        input_output_aliases={3 + group + len(given): 0} if kept else {},
        compiler_params=pltpu.CompilerParams(vmem_limit_bytes=VMEM_BYTES),
        cost_estimate=pl.CostEstimate(flops=1, bytes_accessed=1, transcendentals=0),
        name="contract",
    )(row_ids, sides, owners, *([store] * group), *given, *kept)


def on_device(
    conduction,
    conduction_head,
    valence,
    valence_head,
    screened,
    wing_column,
    wing_row,
    head_value,
    partner,
    pair_select,
    neighbors,
    weights,
    counts,
):
    points = conduction.shape[1]
    half = conduction.shape[2]
    pairs = valence.shape[2]
    block, columns = screened.shape[1], screened.shape[2]
    kpt_count, pw_count, band_count = lax.axis_size("kpt"), lax.axis_size("pw"), lax.axis_size("band")
    kpt, pw, band = lax.axis_index("kpt"), lax.axis_index("pw"), lax.axis_index("band")
    per_index = points // pw_count
    rows = per_index * half
    blocks_here = columns // block
    deep = round_up(block + HEAD_PARTS, 128)
    width = round_up(-(-(columns + 1) // band_count), 128)
    last = band_count - 1
    head_at = columns - last * width

    halves = jnp.moveaxis(conduction.reshape(2, pw_count, per_index, half, columns), 1, 0)
    first = halves if pw_count == 1 else lax.dynamic_index_in_dim(halves, (pw + 1) % pw_count, 0, keepdims=False)
    dealt = deal(halves, "pw")

    selector = (pair_select[:, None] == jnp.arange(pairs)[None, :]).astype(bf16)
    own_valence = valence_columns(valence, valence_head, selector, after(band, first), width, last)
    step_one = [
        lax.ppermute(own_valence, "kpt", [(s, s + 1) for s in range(kpt_count - 1)]),
        lax.ppermute(own_valence, "kpt", [(s, s - 1) for s in range(1, kpt_count)]),
    ]

    plane = jnp.arange(deep)
    is_head = (plane >= block) & (plane < block + HEAD_PARTS)
    heads = lax.dynamic_slice_in_dim(conduction_head, pw * per_index, per_index, 1)
    by_block = []
    for owner in range(pw_count):
        whole = dealt[0]
        for shift in range(1, pw_count):
            whole = jnp.where((pw - owner) % pw_count == shift, dealt[shift], whole)
        for index in range(blocks_here):
            cut = jnp.pad(
                whole[..., index * block : (index + 1) * block], ((0, 0), (0, 0), (0, 0), (0, deep - block))
            )
            by_block.append(jnp.where(is_head, heads[..., None], cut).reshape(2, rows, deep))
    by_block = jnp.stack(by_block)
    arrived = deal(by_block, "kpt")
    own_block = arrived[0]
    middle = kpt_count // 2 + 1

    screen = jnp.pad(screened, ((0, 0), (0, deep - block), (0, band_count * width - columns)))
    screen = lax.dynamic_slice_in_dim(screen, band * width, width, 2)
    row_part = jnp.pad(wing_row, ((0, 0), (0, band_count * width - columns)))
    row_part = lax.dynamic_slice_in_dim(row_part, band * width, width, 1)
    first_kpt = kpt == 0
    row_part = jnp.where(first_kpt, row_part, 0)
    corner = []
    rest = head_value
    for _ in range(HEAD_PARTS):
        part = lax.reduce_precision(rest, 8, 7)
        corner.append(jnp.where(first_kpt, part, 0.0))
        rest = rest - part
    corner = jnp.stack(corner, axis=1).astype(bf16)
    column_part = jnp.concatenate(
        [lax.dynamic_slice_in_dim(wing_column, kpt * block, block, 1), corner], axis=1
    )
    column_part = jnp.pad(column_part, ((0, 0), (0, deep - block - HEAD_PARTS)))
    has_column = (pw == 0) & (band == last)
    screen = jnp.where(plane[None, :, None] == block, row_part[:, None, :], screen)
    screen = jnp.where(
        (jnp.arange(width)[None, None, :] == head_at) & has_column, column_part[:, :, None], screen
    )
    right = jnp.stack(
        [
            jnp.concatenate([screen[0], screen[1]], axis=0),
            jnp.concatenate([screen[1], -screen[0]], axis=0),
        ]
    )

    places = jnp.stack(
        [
            ((pw - pw_shift) % pw_count) * band_count + (band - band_shift) % band_count
            for pw_shift in range(pw_count)
            for band_shift in range(band_count)
        ]
    ).astype(jnp.int32)

    live = jnp.where(jnp.arange(neighbors.shape[1])[None, :] < counts[:, None], weights, 0.0)
    all_points = kpt_count * points
    point_of_row = jnp.sum(
        jnp.where(partner[None, :] == jnp.arange(all_points)[:, None], jnp.arange(all_points)[None, :], 0), axis=1
    ).astype(jnp.int32)

    def spread(group):
        return [own for across in share(group, "pw") for own in share(across, "band")]

    def product(shifts, pieces, right, store):
        sources = jnp.stack([((kpt - shift) % kpt_count).astype(jnp.int32) for shift in shifts])
        where = jnp.append(places, sources)
        return screen_product(where, pieces, right, per_index, half, store, kpt_count)

    near, far = list(range(1, middle)), list(range(middle, kpt_count))
    store = product([0], spread(own_block[None]), right, None)
    first_half = points // 2
    held = after(step_one, store)
    held = [[value[:, :first_half] for value in held], [value[:, first_half:] for value in held]]
    near_group = jnp.stack(after([arrived[shift] for shift in near], [store, step_one]))
    near_pieces = spread(near_group)
    far_across = share(jnp.stack([arrived[shift] for shift in far]), "pw")
    ready = [near_group, [arrived[shift] for shift in far]]
    ends, others = {}, {}

    def move(step, part, gates):
        below, above = held[part]
        values = [after(below, gates)] * 2 if above is below else after([below, above], gates)
        to_ends, to_others = line_pairs(kpt_count, step)
        if step == 2 and part == 0:
            ends[step, part] = one_way(*held[part], *to_ends, "kpt")
            values = after(values, ends[step, part])
        else:
            ends[step, part] = one_way(*values, *to_ends, "kpt")
        if step < kpt_count - 1:
            held[part] = others[step, part] = one_way(*values, *to_others, "kpt")

    move(2, 0, ready)
    move(2, 1, [ready, ends[2, 0]])
    store = product(near, near_pieces, right, store)
    if kpt_count > 3:
        move(3, 0, [store, ends[2, 1]])
    far_pieces = [own for across in after(far_across, store) for own in share(across, "band")]
    store = product(far, far_pieces, after(right, others[2, 0]), store)

    lanes = 2 * pairs
    kept = half // pw_count

    def add_blocks(body, sides, owners, valences, targets, blocks):
        sides, owners = jnp.stack(sides).astype(jnp.int32), jnp.stack(owners)
        targets = jnp.stack(targets).astype(jnp.int32)
        row_ids = (owners[:, None] * points + jnp.arange(points)[None, :]).reshape(-1)
        row_ids = jnp.take(point_of_row, row_ids, mode="clip")
        return contract(row_ids, sides, targets, store, valences, body, blocks)

    def summed(body):
        body = body.reshape(-1, band_count, half, lanes)
        body = sum(deal(jnp.moveaxis(body, 1, 0), "band"))
        body = body.reshape(-1, pw_count, kept, lanes)
        return sum(deal(jnp.moveaxis(body, 1, 0), "pw")).reshape(-1, kept * lanes)

    has_below = [kpt >= step for step in range(kpt_count)]
    has_above = [kpt + step < kpt_count for step in range(kpt_count)]

    def blocks_of(step):
        if step == 1:
            return [[value] for value in step_one] + [[own_valence]], 0, 1
        places, index = [], {}
        for name, moved in (("ends", ends), ("others", others)):
            if (step, 0) not in moved:
                continue
            pair = moved[step, 0], moved[step, 1]
            for side in range(2):
                if side and pair[0][1] is pair[0][0]:
                    index[name, side] = index[name, 0]
                    continue
                index[name, side] = len(places)
                places.append([pair[0][side], pair[1][side]])
        from_below = jnp.where(kpt == kpt_count - 1, index["ends", 0], index.get(("others", 0), 0))
        from_above = jnp.where(kpt == 0, index["ends", 1], index.get(("others", 1), 0))
        return places + [[own_valence]], from_below, from_above

    def slots_of(step):
        places, from_below, from_above = blocks_of(step)
        none = len(places) - 1
        below = jnp.where(has_below[step], from_below, none), jnp.where(has_below[step], kpt - step, kpt)
        above = jnp.where(has_above[step], from_above, none), jnp.where(has_above[step], kpt + step, kpt)
        if 2 * step < kpt_count:
            return places, [below[0], above[0]], [below[1], above[1]]
        return places, [jnp.where(has_below[step], below[0], above[0])], [jnp.where(has_below[step], below[1], above[1])]

    body = add_blocks(None, [jnp.zeros((), jnp.int32)], [kpt], [[own_valence]], [kpt], kpt_count)
    for step in range(1, kpt_count - 1):
        places_here, sides, owners = slots_of(step)
        if step == 2:
            body = after(body, ends[3, 0])
        body = add_blocks(body, sides, owners, places_here, owners, kpt_count)
        if step == 1:
            if kpt_count > 3:
                move(3, 1, body)
            for later in range(4, kpt_count):
                move(later, 0, body)
                move(later, 1, body)
    early = summed(body)
    places_here, sides, owners = slots_of(kpt_count - 1)
    last_owner = owners[0]
    places_here[0] = after(places_here[0], early)
    late = summed(add_blocks(None, sides, owners, places_here, [jnp.zeros((), jnp.int32)], 1))

    match = neighbors[:, :, None] == point_of_row[None, None, :]
    stencil = jnp.sum(jnp.where(match, live[:, :, None], 0.0), axis=1)
    is_late = jnp.arange(all_points) // points == last_owner
    fine = jnp.dot(stencil, jnp.where(is_late[:, None], 0.0, early), precision=highest)
    late_stencil = lax.dynamic_slice_in_dim(stencil, last_owner * points, points, 1)
    fine = fine + jnp.dot(late_stencil, late, precision=highest)
    fine_here = neighbors.shape[0] // kpt_count
    fine = sum(deal(fine.reshape(kpt_count, fine_here, kept, lanes), "kpt"))
    fine = lax.all_gather(fine, "pw", axis=0)
    fine = fine.reshape(pw_count, fine_here, kept, 2, pairs)
    return jnp.transpose(fine, (3, 1, 0, 2, 4)).reshape(2, fine_here, half * pairs)


def solution(mesh):
    return jax.shard_map(
        on_device,
        mesh=mesh,
        in_specs=(
            P("grp", "kpt", "band", "pw"),
            P("grp", "kpt", "band"),
            P("grp", "kpt", None, "pw"),
            P("grp", "kpt", None),
            P("grp", "kpt", "pw"),
            P("grp", None),
            P("grp", "pw"),
            P("grp"),
            P("grp"),
            P(),
            P(),
            P(),
            P(),
        ),
        out_specs=P("grp", "kpt", "band"),
        check_vma=False,
    )
```

```python
import jax
import jax.numpy as jnp
from jax import lax
from jax.experimental import pallas as pl
from jax.experimental.pallas import tpu as pltpu
from jax.sharding import PartitionSpec as P

highest = lax.Precision.HIGHEST
f32 = jnp.float32
bf16 = jnp.bfloat16
HEAD_PARTS = 3
VMEM_BYTES = 48 * 1024 * 1024


def round_up(value, step):
    return -(-value // step) * step


def shifted(x, name, shift):
    count = lax.axis_size(name)
    pairs = [(source, (source + shift) % count) for source in range(count)]
    return lax.ppermute(x, name, pairs)


def after(x, others):
    return lax.optimization_barrier((x, others))[0]


def share(x, name):
    return [x] + [shifted(x, name, shift) for shift in range(1, lax.axis_size(name))]


def deal(x, name):
    count = lax.axis_size(name)
    me = lax.axis_index(name)
    pieces = []
    for shift in range(count):
        piece = lax.dynamic_index_in_dim(x, (me + shift) % count, 0, keepdims=False)
        pieces.append(shifted(piece, name, shift) if shift else piece)
    return pieces


def valence_columns(valence, valence_head, selector, core, width, last):
    parts, points, pairs, columns = valence.shape
    head_at = columns - last * width

    def kernel(core_ref, valence_ref, head_ref, selector_ref, out_ref):
        column = lax.broadcasted_iota(jnp.int32, (pairs, width), 1)
        at_last = core_ref[0] == last
        limit = jnp.where(at_last, head_at, width)
        head_column = jnp.where(at_last, head_at, width)
        for point in range(points):
            rows = valence_ref[0, point].astype(f32)
            head = jnp.broadcast_to(head_ref[0, point].astype(f32), (pairs, width))
            rows = jnp.where(column < limit, rows, 0.0)
            rows = jnp.where(column == head_column, head, rows)
            moved = jnp.dot(selector_ref[...], rows.astype(bf16), preferred_element_type=f32)
            out_ref[0, point] = moved.astype(bf16)

    return pl.pallas_call(
        kernel,
        out_shape=jax.ShapeDtypeStruct((parts, points, pairs, width), bf16),
        grid_spec=pltpu.PrefetchScalarGridSpec(
            num_scalar_prefetch=1,
            grid=(parts,),
            in_specs=[
                pl.BlockSpec((1, points, pairs, width), lambda x, core: (x, 0, 0, core[0])),
                pl.BlockSpec((1, points, pairs, 1), lambda x, core: (x, 0, 0, 0)),
                pl.BlockSpec((pairs, pairs), lambda x, core: (0, 0)),
            ],
            out_specs=pl.BlockSpec((1, points, pairs, width), lambda x, core: (x, 0, 0, 0)),
        ),
        compiler_params=pltpu.CompilerParams(vmem_limit_bytes=VMEM_BYTES),
        name="valence_columns",
    )(core.reshape(1), valence, valence_head[..., None], selector)


def one_way(below, above, pairs_below, pairs_above, name):
    senders = [pair[0] for pair in pairs_below + pairs_above]
    takers = [pair[1] for pair in pairs_below + pairs_above]
    if len(set(senders)) < len(senders) or len(set(takers)) < len(takers):
        return lax.ppermute(below, name, pairs_below), lax.ppermute(above, name, pairs_above)
    sent = below
    if above is not below:
        sends_below = jnp.isin(lax.axis_index(name), jnp.array([pair[0] for pair in pairs_below]))
        sent = jnp.where(sends_below, below, above)
    moved = lax.ppermute(sent, name, pairs_below + pairs_above)
    return moved, moved


def line_pairs(count, step):
    below = [(s, s + 1) for s in range(step - 1, count - 1)]
    above = [(s, s - 1) for s in range(1, count - step + 1)]
    to_ends = [[pair for pair in below if pair[1] == count - 1], [pair for pair in above if pair[1] == 0]]
    to_others = [[pair for pair in below if pair[1] < count - 1], [pair for pair in above if pair[1] > 0]]
    return to_ends, to_others


def screen_product(places, pieces, right, per_index, half, store, blocks):
    _, deep, width = right.shape
    planes = deep // 2
    rows = per_index * half
    count = len(pieces)
    sources = pieces[0].shape[0]
    bands = 2
    pw_count = count // bands
    points = pw_count * per_index
    tile = 512 if width % 512 == 0 else min(256, width)

    def kernel(place_ref, *refs):
        piece_refs, right_ref, out_ref, left_ref = refs[:count], refs[count], refs[-2], refs[-1]

        @pl.when((pl.program_id(1) == 0) & (pl.program_id(2) == 0))
        def _():
            for index in range(count):
                start = pl.multiple_of(place_ref[index] * rows, rows)
                left_ref[pl.ds(start, rows), 0:planes] = piece_refs[index][0, 0]
                left_ref[pl.ds(start, rows), planes:deep] = piece_refs[index][0, 1]

        total = jnp.dot(left_ref[...], right_ref[0], preferred_element_type=f32).astype(bf16)
        for pw in range(pw_count):
            for band in range(bands):
                for point in range(per_index):
                    start = (pw * bands + band) * rows + point * half
                    out_ref[pw * per_index + point, band, 0] = total[start : start + half]

    whole = pl.BlockSpec((1, 2, rows, planes), lambda s, x, n, place: (s, 0, 0, 0))
    kept = [] if store is None else [store]
    return pl.pallas_call(
        kernel,
        out_shape=jax.ShapeDtypeStruct((blocks * points, bands, 2, half, width), bf16),
        grid_spec=pltpu.PrefetchScalarGridSpec(
            num_scalar_prefetch=1,
            grid=(sources, 2, width // tile),
            in_specs=[whole] * count
            + [pl.BlockSpec((1, deep, tile), lambda s, x, n, place: (x, 0, n))]
            + [pl.BlockSpec(memory_space=pl.ANY)] * len(kept),
            out_specs=pl.BlockSpec(
                (points, bands, 1, half, tile), lambda s, x, n, place: (place[count + s], 0, x, 0, n)
            ),
            scratch_shapes=[pltpu.VMEM((count * rows, deep), bf16)],
        ),
        input_output_aliases={count + 2: 0} if kept else {},
        compiler_params=pltpu.CompilerParams(vmem_limit_bytes=VMEM_BYTES),
        cost_estimate=pl.CostEstimate(flops=1, bytes_accessed=1, transcendentals=0),
        name="screen_product",
    )(places, *pieces, right, *kept)


def contract(row_ids, sides, owners, store, valences, body, blocks):
    _, bands, _, half, width = store.shape
    _, _, pairs, _ = valences[0][0].shape
    points = sum(part.shape[1] for part in valences[0])
    slots = sides.shape[0]
    group = 2 if points % 2 == 0 else 1
    steps = points // group
    given, places = [], []
    for side, parts in enumerate(valences):
        first = 0
        for part in parts:
            given.append(part)
            places.append((side, first, first + part.shape[1] // group))
            first = places[-1][2]

    def kernel(row_ref, side_ref, owner_ref, *refs):
        store_refs, valence_refs, out_ref = refs[:group], refs[group : group + len(given)], refs[-1]
        lane = lax.broadcasted_iota(jnp.int32, (half, 2 * pairs), 1)
        side = side_ref[pl.program_id(0)]
        step = pl.program_id(1)

        def rows_of(valence_ref):
            for index in range(group):
                left = store_refs[index][0].reshape(bands * 2 * half, width)
                right = valence_ref[:, index].reshape(2 * pairs, width)
                square = lax.dot_general(left, right, (((1,), (1,)), ((), ())), preferred_element_type=f32)
                for band in range(bands):
                    first = square[2 * band * half : (2 * band + 1) * half]
                    second = square[(2 * band + 1) * half : (2 * band + 2) * half]
                    turned = pltpu.roll(second, pairs, 1)
                    total = first + jnp.where(lane < pairs, -turned, turned)
                    out_ref[index, band * half : (band + 1) * half, :] = total

        for valence_ref, (place, first, end) in zip(valence_refs, places):

            @pl.when((side == place) & (step >= first) & (step < end))
            def _(valence_ref=valence_ref):
                rows_of(valence_ref)

    def store_spec(index):
        return pl.BlockSpec(
            (1, bands, 2, half, width),
            lambda slot, step, row, side, owner: (row[slot * points + step * group + index], 0, 0, 0, 0),
        )

    def valence_spec(place, first, end):
        return pl.BlockSpec(
            (2, group, pairs, width),
            lambda slot, step, row, side, owner: (
                0,
                jnp.where((side[slot] == place) & (step >= first) & (step < end), step - first, 0),
                0,
                0,
            ),
        )

    kept = [] if body is None else [body]
    return pl.pallas_call(
        kernel,
        out_shape=jax.ShapeDtypeStruct((blocks * points, bands * half, 2 * pairs), f32),
        grid_spec=pltpu.PrefetchScalarGridSpec(
            num_scalar_prefetch=3,
            grid=(slots, steps),
            in_specs=[store_spec(index) for index in range(group)]
            + [valence_spec(*place) for place in places]
            + [pl.BlockSpec(memory_space=pl.ANY)] * len(kept),
            out_specs=pl.BlockSpec(
                (group, bands * half, 2 * pairs),
                lambda slot, step, row, side, owner: (owner[slot] * steps + step, 0, 0),
            ),
        ),
        input_output_aliases={3 + group + len(given): 0} if kept else {},
        compiler_params=pltpu.CompilerParams(vmem_limit_bytes=VMEM_BYTES),
        cost_estimate=pl.CostEstimate(flops=1, bytes_accessed=1, transcendentals=0),
        name="contract",
    )(row_ids, sides, owners, *([store] * group), *given, *kept)


def on_device(
    conduction,
    conduction_head,
    valence,
    valence_head,
    screened,
    wing_column,
    wing_row,
    head_value,
    partner,
    pair_select,
    neighbors,
    weights,
    counts,
):
    points = conduction.shape[1]
    half = conduction.shape[2]
    pairs = valence.shape[2]
    block, columns = screened.shape[1], screened.shape[2]
    kpt_count, pw_count, band_count = lax.axis_size("kpt"), lax.axis_size("pw"), lax.axis_size("band")
    kpt, pw, band = lax.axis_index("kpt"), lax.axis_index("pw"), lax.axis_index("band")
    per_index = points // pw_count
    rows = per_index * half
    blocks_here = columns // block
    deep = round_up(block + HEAD_PARTS, 128)
    width = round_up(-(-(columns + 1) // band_count), 128)
    last = band_count - 1
    head_at = columns - last * width

    selector = (pair_select[:, None] == jnp.arange(pairs)[None, :]).astype(bf16)
    own_valence = valence_columns(valence, valence_head, selector, band, width, last)
    step_one = [
        lax.ppermute(own_valence, "kpt", [(s, s + 1) for s in range(kpt_count - 1)]),
        lax.ppermute(own_valence, "kpt", [(s, s - 1) for s in range(1, kpt_count)]),
    ]

    halves = jnp.moveaxis(conduction.reshape(2, pw_count, per_index, half, columns), 1, 0)
    dealt = deal(halves, "pw")

    plane = jnp.arange(deep)
    is_head = (plane >= block) & (plane < block + HEAD_PARTS)
    heads = lax.dynamic_slice_in_dim(conduction_head, pw * per_index, per_index, 1)
    by_block = []
    for owner in range(pw_count):
        whole = dealt[0]
        for shift in range(1, pw_count):
            whole = jnp.where((pw - owner) % pw_count == shift, dealt[shift], whole)
        for index in range(blocks_here):
            cut = jnp.pad(
                whole[..., index * block : (index + 1) * block], ((0, 0), (0, 0), (0, 0), (0, deep - block))
            )
            by_block.append(jnp.where(is_head, heads[..., None], cut).reshape(2, rows, deep))
    by_block = jnp.stack(by_block)
    arrived = deal(by_block, "kpt")
    own_block = arrived[0]
    middle = kpt_count // 2 + 1

    screen = jnp.pad(screened, ((0, 0), (0, deep - block), (0, band_count * width - columns)))
    screen = lax.dynamic_slice_in_dim(screen, band * width, width, 2)
    row_part = jnp.pad(wing_row, ((0, 0), (0, band_count * width - columns)))
    row_part = lax.dynamic_slice_in_dim(row_part, band * width, width, 1)
    first_kpt = kpt == 0
    row_part = jnp.where(first_kpt, row_part, 0)
    corner = []
    rest = head_value
    for _ in range(HEAD_PARTS):
        part = lax.reduce_precision(rest, 8, 7)
        corner.append(jnp.where(first_kpt, part, 0.0))
        rest = rest - part
    corner = jnp.stack(corner, axis=1).astype(bf16)
    column_part = jnp.concatenate(
        [lax.dynamic_slice_in_dim(wing_column, kpt * block, block, 1), corner], axis=1
    )
    column_part = jnp.pad(column_part, ((0, 0), (0, deep - block - HEAD_PARTS)))
    has_column = (pw == 0) & (band == last)
    screen = jnp.where(plane[None, :, None] == block, row_part[:, None, :], screen)
    screen = jnp.where(
        (jnp.arange(width)[None, None, :] == head_at) & has_column, column_part[:, :, None], screen
    )
    right = jnp.stack(
        [
            jnp.concatenate([screen[0], screen[1]], axis=0),
            jnp.concatenate([screen[1], -screen[0]], axis=0),
        ]
    )

    places = jnp.stack(
        [
            ((pw - pw_shift) % pw_count) * band_count + (band - band_shift) % band_count
            for pw_shift in range(pw_count)
            for band_shift in range(band_count)
        ]
    ).astype(jnp.int32)

    live = jnp.where(jnp.arange(neighbors.shape[1])[None, :] < counts[:, None], weights, 0.0)
    all_points = kpt_count * points
    point_of_row = jnp.sum(
        jnp.where(partner[None, :] == jnp.arange(all_points)[:, None], jnp.arange(all_points)[None, :], 0), axis=1
    ).astype(jnp.int32)

    def spread(group):
        return [own for across in share(group, "pw") for own in share(across, "band")]

    def product(shifts, pieces, right, store):
        sources = jnp.stack([((kpt - shift) % kpt_count).astype(jnp.int32) for shift in shifts])
        where = jnp.append(places, sources)
        return screen_product(where, pieces, right, per_index, half, store, kpt_count)

    near, far = list(range(1, middle)), list(range(middle, kpt_count))
    distant = [arrived[shift] for shift in far]
    store = product([0], spread(own_block[None]), right, None)
    near_group = jnp.stack(after([arrived[shift] for shift in near], [store, step_one, distant]))
    near_pieces = spread(near_group)
    far_across = share(jnp.stack(distant), "pw")
    to_ends, to_others = line_pairs(kpt_count, 2)
    early_rows = max(points // 4, 1)
    first_part = one_way(*[value[:, :early_rows] for value in step_one], *to_ends, "kpt")
    held = after(step_one, [near_group, distant, first_part])
    ends = {2: [first_part, one_way(*[value[:, early_rows:] for value in held], *to_ends, "kpt")]}
    others = {}
    if kpt_count > 3:
        others[2] = [one_way(*held, *to_others, "kpt")]
    store = product(near, near_pieces, right, store)
    for step in range(3, kpt_count):
        below, above = others[step - 1][0]
        gates = [store, ends[2]]
        below, above = [after(below, gates)] * 2 if above is below else after([below, above], gates)
        to_ends, to_others = line_pairs(kpt_count, step)
        ends[step] = [one_way(below, above, *to_ends, "kpt")]
        if step < kpt_count - 1:
            others[step] = [one_way(below, above, *to_others, "kpt")]
    far_pieces = [own for across in after(far_across, store) for own in share(across, "band")]
    store = product(far, far_pieces, after(right, others.get(2, ends[2])), store)

    lanes = 2 * pairs
    kept = half // pw_count

    def add_blocks(body, sides, owners, valences, targets, blocks):
        sides, owners = jnp.stack(sides).astype(jnp.int32), jnp.stack(owners)
        targets = jnp.stack(targets).astype(jnp.int32)
        row_ids = (owners[:, None] * points + jnp.arange(points)[None, :]).reshape(-1)
        row_ids = jnp.take(point_of_row, row_ids, mode="clip")
        return contract(row_ids, sides, targets, store, valences, body, blocks)

    def summed(body):
        body = body.reshape(-1, band_count, half, lanes)
        body = sum(deal(jnp.moveaxis(body, 1, 0), "band"))
        body = body.reshape(-1, pw_count, kept, lanes)
        return sum(deal(jnp.moveaxis(body, 1, 0), "pw")).reshape(-1, kept * lanes)

    has_below = [kpt >= step for step in range(kpt_count)]
    has_above = [kpt + step < kpt_count for step in range(kpt_count)]

    def blocks_of(step):
        if step == 1:
            return [[value] for value in step_one] + [[own_valence]], 0, 1
        places, index = [], {}
        for name, moved in (("ends", ends), ("others", others)):
            if step not in moved:
                continue
            parts = moved[step]
            for side in range(2):
                if side and parts[0][1] is parts[0][0]:
                    index[name, side] = index[name, 0]
                    continue
                index[name, side] = len(places)
                places.append([part[side] for part in parts])
        from_below = jnp.where(kpt == kpt_count - 1, index["ends", 0], index.get(("others", 0), 0))
        from_above = jnp.where(kpt == 0, index["ends", 1], index.get(("others", 1), 0))
        return places + [[own_valence]], from_below, from_above

    def slots_of(step):
        places, from_below, from_above = blocks_of(step)
        none = len(places) - 1
        below = jnp.where(has_below[step], from_below, none), jnp.where(has_below[step], kpt - step, kpt)
        above = jnp.where(has_above[step], from_above, none), jnp.where(has_above[step], kpt + step, kpt)
        if 2 * step < kpt_count:
            return places, [below[0], above[0]], [below[1], above[1]]
        return places, [jnp.where(has_below[step], below[0], above[0])], [jnp.where(has_below[step], below[1], above[1])]

    body = add_blocks(None, [jnp.zeros((), jnp.int32)], [kpt], [[own_valence]], [kpt], kpt_count)
    for step in range(1, kpt_count - 1):
        places_here, sides, owners = slots_of(step)
        body = add_blocks(body, sides, owners, places_here, owners, kpt_count)
    early = summed(body)
    places_here, sides, owners = slots_of(kpt_count - 1)
    last_owner = owners[0]
    late = summed(add_blocks(None, sides, owners, places_here, [jnp.zeros((), jnp.int32)], 1))

    match = neighbors[:, :, None] == point_of_row[None, None, :]
    stencil = jnp.sum(jnp.where(match, live[:, :, None], 0.0), axis=1)
    is_late = jnp.arange(all_points) // points == last_owner
    fine = jnp.dot(stencil, jnp.where(is_late[:, None], 0.0, early), precision=highest)
    late_stencil = lax.dynamic_slice_in_dim(stencil, last_owner * points, points, 1)
    fine = fine + jnp.dot(late_stencil, late, precision=highest)
    fine_here = neighbors.shape[0] // kpt_count
    fine = sum(deal(fine.reshape(kpt_count, fine_here, kept, lanes), "kpt"))
    gathered = share(fine, "pw")
    whole = []
    for owner in range(pw_count):
        part = gathered[0]
        for shift in range(1, pw_count):
            part = jnp.where((pw - owner) % pw_count == shift, gathered[shift], part)
        whole.append(part)
    fine = jnp.concatenate(whole, axis=1).reshape(fine_here, half, 2, pairs)
    return jnp.transpose(fine, (2, 0, 1, 3)).reshape(2, fine_here, half * pairs)


def solution(mesh):
    return jax.shard_map(
        on_device,
        mesh=mesh,
        in_specs=(
            P("grp", "kpt", "band", "pw"),
            P("grp", "kpt", "band"),
            P("grp", "kpt", None, "pw"),
            P("grp", "kpt", None),
            P("grp", "kpt", "pw"),
            P("grp", None),
            P("grp", "pw"),
            P("grp"),
            P("grp"),
            P(),
            P(),
            P(),
            P(),
        ),
        out_specs=P("grp", "kpt", "band"),
        check_vma=False,
    )
```

```python
import jax
import jax.numpy as jnp
from jax import lax
from jax.experimental import pallas as pl
from jax.experimental.pallas import tpu as pltpu
from jax.sharding import PartitionSpec as P

highest = lax.Precision.HIGHEST
f32 = jnp.float32
bf16 = jnp.bfloat16
HEAD_PARTS = 3
VMEM_BYTES = 48 * 1024 * 1024


def round_up(value, step):
    return -(-value // step) * step


def shifted(x, name, shift):
    count = lax.axis_size(name)
    pairs = [(source, (source + shift) % count) for source in range(count)]
    return lax.ppermute(x, name, pairs)


def after(x, others):
    return lax.optimization_barrier((x, others))[0]


def share(x, name):
    return [x] + [shifted(x, name, shift) for shift in range(1, lax.axis_size(name))]


def deal(x, name):
    count = lax.axis_size(name)
    me = lax.axis_index(name)
    pieces = []
    for shift in range(count):
        piece = lax.dynamic_index_in_dim(x, (me + shift) % count, 0, keepdims=False)
        pieces.append(shifted(piece, name, shift) if shift else piece)
    return pieces


def valence_columns(valence, valence_head, selector, core, width, last):
    parts, points, pairs, columns = valence.shape
    head_at = columns - last * width

    def kernel(core_ref, valence_ref, head_ref, selector_ref, out_ref):
        column = lax.broadcasted_iota(jnp.int32, (pairs, width), 1)
        at_last = core_ref[0] == last
        limit = jnp.where(at_last, head_at, width)
        head_column = jnp.where(at_last, head_at, width)
        for point in range(points):
            rows = valence_ref[0, point].astype(f32)
            head = jnp.broadcast_to(head_ref[0, point].astype(f32), (pairs, width))
            rows = jnp.where(column < limit, rows, 0.0)
            rows = jnp.where(column == head_column, head, rows)
            moved = jnp.dot(selector_ref[...], rows.astype(bf16), preferred_element_type=f32)
            out_ref[0, point] = moved.astype(bf16)

    return pl.pallas_call(
        kernel,
        out_shape=jax.ShapeDtypeStruct((parts, points, pairs, width), bf16),
        grid_spec=pltpu.PrefetchScalarGridSpec(
            num_scalar_prefetch=1,
            grid=(parts,),
            in_specs=[
                pl.BlockSpec((1, points, pairs, width), lambda x, core: (x, 0, 0, core[0])),
                pl.BlockSpec((1, points, pairs, 1), lambda x, core: (x, 0, 0, 0)),
                pl.BlockSpec((pairs, pairs), lambda x, core: (0, 0)),
            ],
            out_specs=pl.BlockSpec((1, points, pairs, width), lambda x, core: (x, 0, 0, 0)),
        ),
        compiler_params=pltpu.CompilerParams(vmem_limit_bytes=VMEM_BYTES),
        name="valence_columns",
    )(core.reshape(1), valence, valence_head[..., None], selector)


def one_way(below, above, pairs_below, pairs_above, name, gates=()):
    senders = [pair[0] for pair in pairs_below + pairs_above]
    takers = [pair[1] for pair in pairs_below + pairs_above]
    if len(set(senders)) < len(senders) or len(set(takers)) < len(takers):
        below, above = after((below, above), gates)
        return lax.ppermute(below, name, pairs_below), lax.ppermute(above, name, pairs_above)
    sent = below
    if above is not below:
        sends_below = jnp.isin(lax.axis_index(name), jnp.array([pair[0] for pair in pairs_below]))
        sent = jnp.where(sends_below, below, above)
    moved = lax.ppermute(after(sent, gates), name, pairs_below + pairs_above)
    return moved, moved


def line_pairs(count, step):
    below = [(s, s + 1) for s in range(step - 1, count - 1)]
    above = [(s, s - 1) for s in range(1, count - step + 1)]
    to_ends = [[pair for pair in below if pair[1] == count - 1], [pair for pair in above if pair[1] == 0]]
    to_others = [[pair for pair in below if pair[1] < count - 1], [pair for pair in above if pair[1] > 0]]
    return to_ends, to_others


def screen_product(places, pieces, right, per_index, half, store, blocks):
    _, deep, width = right.shape
    planes = deep // 2
    rows = per_index * half
    count = len(pieces)
    sources = pieces[0].shape[0]
    bands = 2
    pw_count = count // bands
    points = pw_count * per_index
    tile = 512 if width % 512 == 0 else min(256, width)

    def kernel(place_ref, *refs):
        piece_refs, right_ref, out_ref, left_ref = refs[:count], refs[count], refs[-2], refs[-1]

        @pl.when((pl.program_id(1) == 0) & (pl.program_id(2) == 0))
        def _():
            for index in range(count):
                start = pl.multiple_of(place_ref[index] * rows, rows)
                left_ref[pl.ds(start, rows), 0:planes] = piece_refs[index][0, 0]
                left_ref[pl.ds(start, rows), planes:deep] = piece_refs[index][0, 1]

        total = jnp.dot(left_ref[...], right_ref[0], preferred_element_type=f32).astype(bf16)
        for pw in range(pw_count):
            for band in range(bands):
                for point in range(per_index):
                    start = (pw * bands + band) * rows + point * half
                    out_ref[pw * per_index + point, band, 0] = total[start : start + half]

    whole = pl.BlockSpec((1, 2, rows, planes), lambda s, x, n, place: (s, 0, 0, 0))
    kept = [] if store is None else [store]
    return pl.pallas_call(
        kernel,
        out_shape=jax.ShapeDtypeStruct((blocks * points, bands, 2, half, width), bf16),
        grid_spec=pltpu.PrefetchScalarGridSpec(
            num_scalar_prefetch=1,
            grid=(sources, 2, width // tile),
            in_specs=[whole] * count
            + [pl.BlockSpec((1, deep, tile), lambda s, x, n, place: (x, 0, n))]
            + [pl.BlockSpec(memory_space=pl.ANY)] * len(kept),
            out_specs=pl.BlockSpec(
                (points, bands, 1, half, tile), lambda s, x, n, place: (place[count + s], 0, x, 0, n)
            ),
            scratch_shapes=[pltpu.VMEM((count * rows, deep), bf16)],
        ),
        input_output_aliases={count + 2: 0} if kept else {},
        compiler_params=pltpu.CompilerParams(vmem_limit_bytes=VMEM_BYTES),
        cost_estimate=pl.CostEstimate(flops=1, bytes_accessed=1, transcendentals=0),
        name="screen_product",
    )(places, *pieces, right, *kept)


def contract(row_ids, sides, owners, store, valences, body, blocks):
    _, bands, _, half, width = store.shape
    _, _, pairs, _ = valences[0][0].shape
    points = sum(part.shape[1] for part in valences[0])
    slots = sides.shape[0]
    group = 2 if points % 2 == 0 else 1
    steps = points // group
    given, places = [], []
    for side, parts in enumerate(valences):
        first = 0
        for part in parts:
            given.append(part)
            places.append((side, first, first + part.shape[1] // group))
            first = places[-1][2]

    def kernel(row_ref, side_ref, owner_ref, *refs):
        store_refs, valence_refs, out_ref = refs[:group], refs[group : group + len(given)], refs[-1]
        lane = lax.broadcasted_iota(jnp.int32, (half, 2 * pairs), 1)
        side = side_ref[pl.program_id(0)]
        step = pl.program_id(1)

        def rows_of(valence_ref):
            for index in range(group):
                left = store_refs[index][0].reshape(bands * 2 * half, width)
                right = valence_ref[:, index].reshape(2 * pairs, width)
                square = lax.dot_general(left, right, (((1,), (1,)), ((), ())), preferred_element_type=f32)
                for band in range(bands):
                    first = square[2 * band * half : (2 * band + 1) * half]
                    second = square[(2 * band + 1) * half : (2 * band + 2) * half]
                    turned = pltpu.roll(second, pairs, 1)
                    total = first + jnp.where(lane < pairs, -turned, turned)
                    out_ref[index, band * half : (band + 1) * half, :] = total

        for valence_ref, (place, first, end) in zip(valence_refs, places):

            @pl.when((side == place) & (step >= first) & (step < end))
            def _(valence_ref=valence_ref):
                rows_of(valence_ref)

    def store_spec(index):
        return pl.BlockSpec(
            (1, bands, 2, half, width),
            lambda slot, step, row, side, owner: (row[slot * points + step * group + index], 0, 0, 0, 0),
        )

    def valence_spec(place, first, end):
        return pl.BlockSpec(
            (2, group, pairs, width),
            lambda slot, step, row, side, owner: (
                0,
                jnp.where((side[slot] == place) & (step >= first) & (step < end), step - first, 0),
                0,
                0,
            ),
        )

    kept = [] if body is None else [body]
    return pl.pallas_call(
        kernel,
        out_shape=jax.ShapeDtypeStruct((blocks * points, bands * half, 2 * pairs), f32),
        grid_spec=pltpu.PrefetchScalarGridSpec(
            num_scalar_prefetch=3,
            grid=(slots, steps),
            in_specs=[store_spec(index) for index in range(group)]
            + [valence_spec(*place) for place in places]
            + [pl.BlockSpec(memory_space=pl.ANY)] * len(kept),
            out_specs=pl.BlockSpec(
                (group, bands * half, 2 * pairs),
                lambda slot, step, row, side, owner: (owner[slot] * steps + step, 0, 0),
            ),
        ),
        input_output_aliases={3 + group + len(given): 0} if kept else {},
        compiler_params=pltpu.CompilerParams(vmem_limit_bytes=VMEM_BYTES),
        cost_estimate=pl.CostEstimate(flops=1, bytes_accessed=1, transcendentals=0),
        name="contract",
    )(row_ids, sides, owners, *([store] * group), *given, *kept)


def on_device(
    conduction,
    conduction_head,
    valence,
    valence_head,
    screened,
    wing_column,
    wing_row,
    head_value,
    partner,
    pair_select,
    neighbors,
    weights,
    counts,
):
    points = conduction.shape[1]
    half = conduction.shape[2]
    pairs = valence.shape[2]
    block, columns = screened.shape[1], screened.shape[2]
    kpt_count, pw_count, band_count = lax.axis_size("kpt"), lax.axis_size("pw"), lax.axis_size("band")
    kpt, pw, band = lax.axis_index("kpt"), lax.axis_index("pw"), lax.axis_index("band")
    per_index = points // pw_count
    rows = per_index * half
    blocks_here = columns // block
    deep = round_up(block + HEAD_PARTS, 128)
    width = round_up(-(-(columns + 1) // band_count), 128)
    last = band_count - 1
    head_at = columns - last * width

    selector = (pair_select[:, None] == jnp.arange(pairs)[None, :]).astype(bf16)
    own_valence = valence_columns(valence, valence_head, selector, band, width, last)
    step_one = [
        lax.ppermute(own_valence, "kpt", [(s, s + 1) for s in range(kpt_count - 1)]),
        lax.ppermute(own_valence, "kpt", [(s, s - 1) for s in range(1, kpt_count)]),
    ]

    halves = jnp.moveaxis(conduction.reshape(2, pw_count, per_index, half, columns), 1, 0)
    dealt = deal(halves, "pw")

    plane = jnp.arange(deep)
    is_head = (plane >= block) & (plane < block + HEAD_PARTS)
    heads = lax.dynamic_slice_in_dim(conduction_head, pw * per_index, per_index, 1)
    by_block = []
    for owner in range(pw_count):
        whole = dealt[0]
        for shift in range(1, pw_count):
            whole = jnp.where((pw - owner) % pw_count == shift, dealt[shift], whole)
        for index in range(blocks_here):
            cut = jnp.pad(
                whole[..., index * block : (index + 1) * block], ((0, 0), (0, 0), (0, 0), (0, deep - block))
            )
            by_block.append(jnp.where(is_head, heads[..., None], cut).reshape(2, rows, deep))
    by_block = jnp.stack(by_block)
    arrived = deal(by_block, "kpt")
    own_block = arrived[0]
    middle = kpt_count // 2 + 1

    screen = jnp.pad(screened, ((0, 0), (0, deep - block), (0, band_count * width - columns)))
    screen = lax.dynamic_slice_in_dim(screen, band * width, width, 2)
    row_part = jnp.pad(wing_row, ((0, 0), (0, band_count * width - columns)))
    row_part = lax.dynamic_slice_in_dim(row_part, band * width, width, 1)
    first_kpt = kpt == 0
    row_part = jnp.where(first_kpt, row_part, 0)
    corner = []
    rest = head_value
    for _ in range(HEAD_PARTS):
        part = lax.reduce_precision(rest, 8, 7)
        corner.append(jnp.where(first_kpt, part, 0.0))
        rest = rest - part
    corner = jnp.stack(corner, axis=1).astype(bf16)
    column_part = jnp.concatenate(
        [lax.dynamic_slice_in_dim(wing_column, kpt * block, block, 1), corner], axis=1
    )
    column_part = jnp.pad(column_part, ((0, 0), (0, deep - block - HEAD_PARTS)))
    has_column = (pw == 0) & (band == last)
    screen = jnp.where(plane[None, :, None] == block, row_part[:, None, :], screen)
    screen = jnp.where(
        (jnp.arange(width)[None, None, :] == head_at) & has_column, column_part[:, :, None], screen
    )
    right = jnp.stack(
        [
            jnp.concatenate([screen[0], screen[1]], axis=0),
            jnp.concatenate([screen[1], -screen[0]], axis=0),
        ]
    )

    places = jnp.stack(
        [
            ((pw - pw_shift) % pw_count) * band_count + (band - band_shift) % band_count
            for pw_shift in range(pw_count)
            for band_shift in range(band_count)
        ]
    ).astype(jnp.int32)

    live = jnp.where(jnp.arange(neighbors.shape[1])[None, :] < counts[:, None], weights, 0.0)
    all_points = kpt_count * points
    point_of_row = jnp.sum(
        jnp.where(partner[None, :] == jnp.arange(all_points)[:, None], jnp.arange(all_points)[None, :], 0), axis=1
    ).astype(jnp.int32)

    def spread(group):
        return [own for across in share(group, "pw") for own in share(across, "band")]

    def product(shifts, pieces, right, store):
        sources = jnp.stack([((kpt - shift) % kpt_count).astype(jnp.int32) for shift in shifts])
        where = jnp.append(places, sources)
        return screen_product(where, pieces, right, per_index, half, store, kpt_count)

    near, far = list(range(1, middle)), list(range(middle, kpt_count))
    distant = [arrived[shift] for shift in far]
    store = product([0], spread(own_block[None]), right, None)
    near_group = jnp.stack(after([arrived[shift] for shift in near], [store, step_one, distant]))
    near_pieces = spread(near_group)
    far_across = share(jnp.stack(distant), "pw")
    to_ends, to_others = line_pairs(kpt_count, 2)
    early_rows = max(points // 4, 1)
    first_part = one_way(*[value[:, :early_rows] for value in step_one], *to_ends, "kpt")
    gates = [near_group, distant, first_part]
    ends = {2: [first_part, one_way(*[value[:, early_rows:] for value in step_one], *to_ends, "kpt", gates)]}
    others = {}
    if kpt_count > 3:
        others[2] = [one_way(*step_one, *to_others, "kpt", gates)]
    store = product(near, near_pieces, right, store)
    for step in range(3, kpt_count):
        below, above = others[step - 1][0]
        gates = [store, ends[2]]
        to_ends, to_others = line_pairs(kpt_count, step)
        ends[step] = [one_way(below, above, *to_ends, "kpt", gates)]
        if step < kpt_count - 1:
            others[step] = [one_way(below, above, *to_others, "kpt", gates)]
    far_pieces = [own for across in after(far_across, store) for own in share(across, "band")]
    store = product(far, far_pieces, after(right, others.get(2, ends[2])), store)

    lanes = 2 * pairs
    kept = half // pw_count

    def add_blocks(body, sides, owners, valences, targets, blocks):
        sides, owners = jnp.stack(sides).astype(jnp.int32), jnp.stack(owners)
        targets = jnp.stack(targets).astype(jnp.int32)
        row_ids = (owners[:, None] * points + jnp.arange(points)[None, :]).reshape(-1)
        row_ids = jnp.take(point_of_row, row_ids, mode="clip")
        return contract(row_ids, sides, targets, store, valences, body, blocks)

    def summed(body):
        body = body.reshape(-1, band_count, half, lanes)
        body = sum(deal(jnp.moveaxis(body, 1, 0), "band"))
        body = body.reshape(-1, pw_count, kept, lanes)
        return sum(deal(jnp.moveaxis(body, 1, 0), "pw")).reshape(-1, kept * lanes)

    has_below = [kpt >= step for step in range(kpt_count)]
    has_above = [kpt + step < kpt_count for step in range(kpt_count)]

    def blocks_of(step):
        if step == 1:
            return [[value] for value in step_one] + [[own_valence]], 0, 1
        places, index = [], {}
        for name, moved in (("ends", ends), ("others", others)):
            if step not in moved:
                continue
            parts = moved[step]
            for side in range(2):
                if side and parts[0][1] is parts[0][0]:
                    index[name, side] = index[name, 0]
                    continue
                index[name, side] = len(places)
                places.append([part[side] for part in parts])
        from_below = jnp.where(kpt == kpt_count - 1, index["ends", 0], index.get(("others", 0), 0))
        from_above = jnp.where(kpt == 0, index["ends", 1], index.get(("others", 1), 0))
        return places + [[own_valence]], from_below, from_above

    def slots_of(step):
        places, from_below, from_above = blocks_of(step)
        none = len(places) - 1
        below = jnp.where(has_below[step], from_below, none), jnp.where(has_below[step], kpt - step, kpt)
        above = jnp.where(has_above[step], from_above, none), jnp.where(has_above[step], kpt + step, kpt)
        if 2 * step < kpt_count:
            return places, [below[0], above[0]], [below[1], above[1]]
        return places, [jnp.where(has_below[step], below[0], above[0])], [jnp.where(has_below[step], below[1], above[1])]

    body = add_blocks(None, [jnp.zeros((), jnp.int32)], [kpt], [[own_valence]], [kpt], kpt_count)
    for step in range(1, kpt_count - 1):
        places_here, sides, owners = slots_of(step)
        body = add_blocks(body, sides, owners, places_here, owners, kpt_count)
    early = summed(body)
    places_here, sides, owners = slots_of(kpt_count - 1)
    last_owner = owners[0]
    late = summed(add_blocks(None, sides, owners, places_here, [jnp.zeros((), jnp.int32)], 1))

    match = neighbors[:, :, None] == point_of_row[None, None, :]
    stencil = jnp.sum(jnp.where(match, live[:, :, None], 0.0), axis=1)
    is_late = jnp.arange(all_points) // points == last_owner
    fine = jnp.dot(stencil, jnp.where(is_late[:, None], 0.0, early), precision=highest)
    late_stencil = lax.dynamic_slice_in_dim(stencil, last_owner * points, points, 1)
    fine = fine + jnp.dot(late_stencil, late, precision=highest)
    fine_here = neighbors.shape[0] // kpt_count
    fine = fine.reshape(kpt_count, fine_here, kept, lanes)
    own_fine = lax.dynamic_index_in_dim(fine, kpt, 0, keepdims=False)
    fine = own_fine + sum(piece.astype(f32) for piece in deal(fine.astype(bf16), "kpt")[1:])
    gathered = share(fine, "pw")
    whole = []
    for owner in range(pw_count):
        part = gathered[0]
        for shift in range(1, pw_count):
            part = jnp.where((pw - owner) % pw_count == shift, gathered[shift], part)
        whole.append(part)
    fine = jnp.concatenate(whole, axis=1).reshape(fine_here, half, 2, pairs)
    return jnp.transpose(fine, (2, 0, 1, 3)).reshape(2, fine_here, half * pairs)


def solution(mesh):
    return jax.shard_map(
        on_device,
        mesh=mesh,
        in_specs=(
            P("grp", "kpt", "band", "pw"),
            P("grp", "kpt", "band"),
            P("grp", "kpt", None, "pw"),
            P("grp", "kpt", None),
            P("grp", "kpt", "pw"),
            P("grp", None),
            P("grp", "pw"),
            P("grp"),
            P("grp"),
            P(),
            P(),
            P(),
            P(),
        ),
        out_specs=P("grp", "kpt", "band"),
        check_vma=False,
    )
```

```python
import jax
import jax.numpy as jnp
from jax import lax
from jax.experimental import pallas as pl
from jax.experimental.pallas import tpu as pltpu
from jax.sharding import PartitionSpec as P

highest = lax.Precision.HIGHEST
f32 = jnp.float32
bf16 = jnp.bfloat16
HEAD_PARTS = 3
VMEM_BYTES = 48 * 1024 * 1024


def round_up(value, step):
    return -(-value // step) * step


def shifted(x, name, shift):
    count = lax.axis_size(name)
    pairs = [(source, (source + shift) % count) for source in range(count)]
    return lax.ppermute(x, name, pairs)


def after(x, others):
    return lax.optimization_barrier((x, others))[0]


def share(x, name):
    return [x] + [shifted(x, name, shift) for shift in range(1, lax.axis_size(name))]


def deal(x, name):
    count = lax.axis_size(name)
    me = lax.axis_index(name)
    pieces = []
    for shift in range(count):
        piece = lax.dynamic_index_in_dim(x, (me + shift) % count, 0, keepdims=False)
        pieces.append(shifted(piece, name, shift) if shift else piece)
    return pieces


def valence_columns(valence, valence_head, selector, core, width, last):
    parts, points, pairs, columns = valence.shape
    head_at = columns - last * width

    def kernel(core_ref, valence_ref, head_ref, selector_ref, out_ref):
        column = lax.broadcasted_iota(jnp.int32, (pairs, width), 1)
        at_last = core_ref[0] == last
        limit = jnp.where(at_last, head_at, width)
        head_column = jnp.where(at_last, head_at, width)
        for point in range(points):
            rows = valence_ref[0, point].astype(f32)
            head = jnp.broadcast_to(head_ref[0, point].astype(f32), (pairs, width))
            rows = jnp.where(column < limit, rows, 0.0)
            rows = jnp.where(column == head_column, head, rows)
            moved = jnp.dot(selector_ref[...], rows.astype(bf16), preferred_element_type=f32)
            out_ref[0, point] = moved.astype(bf16)

    return pl.pallas_call(
        kernel,
        out_shape=jax.ShapeDtypeStruct((parts, points, pairs, width), bf16),
        grid_spec=pltpu.PrefetchScalarGridSpec(
            num_scalar_prefetch=1,
            grid=(parts,),
            in_specs=[
                pl.BlockSpec((1, points, pairs, width), lambda x, core: (x, 0, 0, core[0])),
                pl.BlockSpec((1, points, pairs, 1), lambda x, core: (x, 0, 0, 0)),
                pl.BlockSpec((pairs, pairs), lambda x, core: (0, 0)),
            ],
            out_specs=pl.BlockSpec((1, points, pairs, width), lambda x, core: (x, 0, 0, 0)),
        ),
        compiler_params=pltpu.CompilerParams(vmem_limit_bytes=VMEM_BYTES),
        name="valence_columns",
    )(core.reshape(1), valence, valence_head[..., None], selector)


def one_way(below, above, pairs_below, pairs_above, name, gates=()):
    senders = [pair[0] for pair in pairs_below + pairs_above]
    takers = [pair[1] for pair in pairs_below + pairs_above]
    if len(set(senders)) < len(senders) or len(set(takers)) < len(takers):
        below, above = after((below, above), gates)
        return lax.ppermute(below, name, pairs_below), lax.ppermute(above, name, pairs_above)
    sent = below
    if above is not below:
        sends_below = jnp.isin(lax.axis_index(name), jnp.array([pair[0] for pair in pairs_below]))
        sent = jnp.where(sends_below, below, above)
    moved = lax.ppermute(after(sent, gates), name, pairs_below + pairs_above)
    return moved, moved


def line_pairs(count, step):
    below = [(s, s + 1) for s in range(step - 1, count - 1)]
    above = [(s, s - 1) for s in range(1, count - step + 1)]
    to_ends = [[pair for pair in below if pair[1] == count - 1], [pair for pair in above if pair[1] == 0]]
    to_others = [[pair for pair in below if pair[1] < count - 1], [pair for pair in above if pair[1] > 0]]
    return to_ends, to_others


def screen_product(places, pieces, right, per_index, half, store, blocks):
    _, deep, width = right.shape
    planes = deep // 2
    rows = per_index * half
    count = len(pieces)
    sources = pieces[0].shape[0]
    bands = 2
    pw_count = count // bands
    points = pw_count * per_index
    tile = 512 if width % 512 == 0 else min(256, width)

    def kernel(place_ref, *refs):
        piece_refs, right_ref, out_ref, left_ref = refs[:count], refs[count], refs[-2], refs[-1]

        @pl.when((pl.program_id(1) == 0) & (pl.program_id(2) == 0))
        def _():
            for index in range(count):
                start = pl.multiple_of(place_ref[index] * rows, rows)
                left_ref[pl.ds(start, rows), 0:planes] = piece_refs[index][0, 0]
                left_ref[pl.ds(start, rows), planes:deep] = piece_refs[index][0, 1]

        total = jnp.dot(left_ref[...], right_ref[0], preferred_element_type=f32).astype(bf16)
        for pw in range(pw_count):
            for band in range(bands):
                for point in range(per_index):
                    start = (pw * bands + band) * rows + point * half
                    out_ref[pw * per_index + point, band, 0] = total[start : start + half]

    whole = pl.BlockSpec((1, 2, rows, planes), lambda s, x, n, place: (s, 0, 0, 0))
    kept = [] if store is None else [store]
    return pl.pallas_call(
        kernel,
        out_shape=jax.ShapeDtypeStruct((blocks * points, bands, 2, half, width), bf16),
        grid_spec=pltpu.PrefetchScalarGridSpec(
            num_scalar_prefetch=1,
            grid=(sources, 2, width // tile),
            in_specs=[whole] * count
            + [pl.BlockSpec((1, deep, tile), lambda s, x, n, place: (x, 0, n))]
            + [pl.BlockSpec(memory_space=pl.ANY)] * len(kept),
            out_specs=pl.BlockSpec(
                (points, bands, 1, half, tile), lambda s, x, n, place: (place[count + s], 0, x, 0, n)
            ),
            scratch_shapes=[pltpu.VMEM((count * rows, deep), bf16)],
        ),
        input_output_aliases={count + 2: 0} if kept else {},
        compiler_params=pltpu.CompilerParams(vmem_limit_bytes=VMEM_BYTES),
        cost_estimate=pl.CostEstimate(flops=1, bytes_accessed=1, transcendentals=0),
        name="screen_product",
    )(places, *pieces, right, *kept)


def contract(row_ids, sides, owners, store, valences, body, blocks):
    _, bands, _, half, width = store.shape
    _, _, pairs, _ = valences[0][0].shape
    points = sum(part.shape[1] for part in valences[0])
    slots = sides.shape[0]
    group = 2 if points % 2 == 0 else 1
    steps = points // group
    given, places = [], []
    for side, parts in enumerate(valences):
        first = 0
        for part in parts:
            given.append(part)
            places.append((side, first, first + part.shape[1] // group))
            first = places[-1][2]

    def kernel(row_ref, side_ref, owner_ref, *refs):
        store_refs, valence_refs, out_ref = refs[:group], refs[group : group + len(given)], refs[-1]
        lane = lax.broadcasted_iota(jnp.int32, (half, 2 * pairs), 1)
        side = side_ref[pl.program_id(0)]
        step = pl.program_id(1)

        def rows_of(valence_ref):
            for index in range(group):
                left = store_refs[index][0].reshape(bands * 2 * half, width)
                right = valence_ref[:, index].reshape(2 * pairs, width)
                square = lax.dot_general(left, right, (((1,), (1,)), ((), ())), preferred_element_type=f32)
                for band in range(bands):
                    first = square[2 * band * half : (2 * band + 1) * half]
                    second = square[(2 * band + 1) * half : (2 * band + 2) * half]
                    turned = pltpu.roll(second, pairs, 1)
                    total = first + jnp.where(lane < pairs, -turned, turned)
                    out_ref[index, band * half : (band + 1) * half, :] = total

        for valence_ref, (place, first, end) in zip(valence_refs, places):

            @pl.when((side == place) & (step >= first) & (step < end))
            def _(valence_ref=valence_ref):
                rows_of(valence_ref)

    def store_spec(index):
        return pl.BlockSpec(
            (1, bands, 2, half, width),
            lambda slot, step, row, side, owner: (row[slot * points + step * group + index], 0, 0, 0, 0),
        )

    def valence_spec(place, first, end):
        return pl.BlockSpec(
            (2, group, pairs, width),
            lambda slot, step, row, side, owner: (
                0,
                jnp.where((side[slot] == place) & (step >= first) & (step < end), step - first, 0),
                0,
                0,
            ),
        )

    kept = [] if body is None else [body]
    return pl.pallas_call(
        kernel,
        out_shape=jax.ShapeDtypeStruct((blocks * points, bands * half, 2 * pairs), f32),
        grid_spec=pltpu.PrefetchScalarGridSpec(
            num_scalar_prefetch=3,
            grid=(slots, steps),
            in_specs=[store_spec(index) for index in range(group)]
            + [valence_spec(*place) for place in places]
            + [pl.BlockSpec(memory_space=pl.ANY)] * len(kept),
            out_specs=pl.BlockSpec(
                (group, bands * half, 2 * pairs),
                lambda slot, step, row, side, owner: (owner[slot] * steps + step, 0, 0),
            ),
        ),
        input_output_aliases={3 + group + len(given): 0} if kept else {},
        compiler_params=pltpu.CompilerParams(vmem_limit_bytes=VMEM_BYTES),
        cost_estimate=pl.CostEstimate(flops=1, bytes_accessed=1, transcendentals=0),
        name="contract",
    )(row_ids, sides, owners, *([store] * group), *given, *kept)


def on_device(
    conduction,
    conduction_head,
    valence,
    valence_head,
    screened,
    wing_column,
    wing_row,
    head_value,
    partner,
    pair_select,
    neighbors,
    weights,
    counts,
):
    points = conduction.shape[1]
    half = conduction.shape[2]
    pairs = valence.shape[2]
    block, columns = screened.shape[1], screened.shape[2]
    kpt_count, pw_count, band_count = lax.axis_size("kpt"), lax.axis_size("pw"), lax.axis_size("band")
    kpt, pw, band = lax.axis_index("kpt"), lax.axis_index("pw"), lax.axis_index("band")
    per_index = points // pw_count
    rows = per_index * half
    blocks_here = columns // block
    deep = round_up(block + HEAD_PARTS, 128)
    width = round_up(-(-(columns + 1) // band_count), 128)
    last = band_count - 1
    head_at = columns - last * width

    selector = (pair_select[:, None] == jnp.arange(pairs)[None, :]).astype(bf16)
    own_valence = valence_columns(valence, valence_head, selector, band, width, last)
    step_one = [
        lax.ppermute(own_valence, "kpt", [(s, s + 1) for s in range(kpt_count - 1)]),
        lax.ppermute(own_valence, "kpt", [(s, s - 1) for s in range(1, kpt_count)]),
    ]

    halves = jnp.moveaxis(conduction.reshape(2, pw_count, per_index, half, columns), 1, 0)
    dealt = deal(halves, "pw")

    plane = jnp.arange(deep)
    is_head = (plane >= block) & (plane < block + HEAD_PARTS)
    heads = lax.dynamic_slice_in_dim(conduction_head, pw * per_index, per_index, 1)
    by_block = []
    for owner in range(pw_count):
        whole = dealt[0]
        for shift in range(1, pw_count):
            whole = jnp.where((pw - owner) % pw_count == shift, dealt[shift], whole)
        for index in range(blocks_here):
            cut = jnp.pad(
                whole[..., index * block : (index + 1) * block], ((0, 0), (0, 0), (0, 0), (0, deep - block))
            )
            by_block.append(jnp.where(is_head, heads[..., None], cut).reshape(2, rows, deep))
    by_block = jnp.stack(by_block)
    middle = kpt_count // 2 + 1
    own_block = lax.dynamic_index_in_dim(by_block, kpt, 0, keepdims=False)
    own_across = share(own_block[None], "pw")
    arrived = [own_block]
    for shift in range(1, kpt_count):
        piece = lax.dynamic_index_in_dim(by_block, (kpt + shift) % kpt_count, 0, keepdims=False)
        arrived.append(shifted(piece if shift < middle else after(piece, own_across), "kpt", shift))

    screen = jnp.pad(screened, ((0, 0), (0, deep - block), (0, band_count * width - columns)))
    screen = lax.dynamic_slice_in_dim(screen, band * width, width, 2)
    row_part = jnp.pad(wing_row, ((0, 0), (0, band_count * width - columns)))
    row_part = lax.dynamic_slice_in_dim(row_part, band * width, width, 1)
    first_kpt = kpt == 0
    row_part = jnp.where(first_kpt, row_part, 0)
    corner = []
    rest = head_value
    for _ in range(HEAD_PARTS):
        part = lax.reduce_precision(rest, 8, 7)
        corner.append(jnp.where(first_kpt, part, 0.0))
        rest = rest - part
    corner = jnp.stack(corner, axis=1).astype(bf16)
    column_part = jnp.concatenate(
        [lax.dynamic_slice_in_dim(wing_column, kpt * block, block, 1), corner], axis=1
    )
    column_part = jnp.pad(column_part, ((0, 0), (0, deep - block - HEAD_PARTS)))
    has_column = (pw == 0) & (band == last)
    screen = jnp.where(plane[None, :, None] == block, row_part[:, None, :], screen)
    screen = jnp.where(
        (jnp.arange(width)[None, None, :] == head_at) & has_column, column_part[:, :, None], screen
    )
    right = jnp.stack(
        [
            jnp.concatenate([screen[0], screen[1]], axis=0),
            jnp.concatenate([screen[1], -screen[0]], axis=0),
        ]
    )

    places = jnp.stack(
        [
            ((pw - pw_shift) % pw_count) * band_count + (band - band_shift) % band_count
            for pw_shift in range(pw_count)
            for band_shift in range(band_count)
        ]
    ).astype(jnp.int32)

    live = jnp.where(jnp.arange(neighbors.shape[1])[None, :] < counts[:, None], weights, 0.0)
    all_points = kpt_count * points
    point_of_row = jnp.sum(
        jnp.where(partner[None, :] == jnp.arange(all_points)[:, None], jnp.arange(all_points)[None, :], 0), axis=1
    ).astype(jnp.int32)

    def spread(across):
        return [own for value in across for own in share(value, "band")]

    def product(shifts, pieces, right, store):
        sources = jnp.stack([((kpt - shift) % kpt_count).astype(jnp.int32) for shift in shifts])
        where = jnp.append(places, sources)
        return screen_product(where, pieces, right, per_index, half, store, kpt_count)

    near, far = list(range(1, middle)), list(range(middle, kpt_count))
    distant = [arrived[shift] for shift in far]
    store = product([0], spread(own_across), right, None)
    near_group = jnp.stack(after([arrived[shift] for shift in near], [store, step_one, distant]))
    near_pieces = spread(share(near_group, "pw"))
    far_across = share(jnp.stack(distant), "pw")
    to_ends, to_others = line_pairs(kpt_count, 2)
    few, more = max(points // 4, 1), max(points // 2, 1)

    def rows_of(first, end):
        return [value[:, first:end] for value in step_one]

    ends, others = {2: [one_way(*rows_of(0, more), *to_ends, "kpt")]}, {}
    if kpt_count > 3:
        others[2] = [one_way(*rows_of(0, few), *to_others, "kpt")]
    gates = [near_group, distant, ends[2][0], others.get(2, [])[:1]]
    if kpt_count > 3:
        others[2].append(one_way(*rows_of(few, points), *to_others, "kpt", gates))
    ends[2].append(one_way(*rows_of(more, points), *to_ends, "kpt", gates))
    if kpt_count > 3:
        ends[3] = [one_way(*others[2][0], *line_pairs(kpt_count, 3)[0], "kpt", [ends[2], near_pieces[0]])]
    store = product(near, near_pieces, right, store)
    for step in range(3, kpt_count):
        gates = [store, ends[2], ends[3][:1]]
        to_ends, to_others = line_pairs(kpt_count, step)
        sent = others[step - 1]
        skip = 1 if step == 3 else 0
        ends.setdefault(step, []).extend(one_way(*part, *to_ends, "kpt", gates) for part in sent[skip:])
        if step < kpt_count - 1:
            others[step] = [one_way(*part, *to_others, "kpt", gates) for part in sent]
    far_pieces = spread(after(far_across, store))
    store = product(far, far_pieces, after(right, others.get(2, ends[2])), store)

    lanes = 2 * pairs
    kept = half // pw_count

    def add_blocks(body, sides, owners, valences, targets, blocks):
        sides, owners = jnp.stack(sides).astype(jnp.int32), jnp.stack(owners)
        targets = jnp.stack(targets).astype(jnp.int32)
        row_ids = (owners[:, None] * points + jnp.arange(points)[None, :]).reshape(-1)
        row_ids = jnp.take(point_of_row, row_ids, mode="clip")
        return contract(row_ids, sides, targets, store, valences, body, blocks)

    def summed(body):
        body = body.reshape(-1, band_count, half, lanes)
        body = sum(deal(jnp.moveaxis(body, 1, 0), "band"))
        body = body.reshape(-1, pw_count, kept, lanes)
        return sum(deal(jnp.moveaxis(body, 1, 0), "pw")).reshape(-1, kept * lanes)

    has_below = [kpt >= step for step in range(kpt_count)]
    has_above = [kpt + step < kpt_count for step in range(kpt_count)]

    def blocks_of(step):
        if step == 1:
            return [[value] for value in step_one] + [[own_valence]], 0, 1
        places, index = [], {}
        for name, moved in (("ends", ends), ("others", others)):
            if step not in moved:
                continue
            parts = moved[step]
            for side in range(2):
                if side and parts[0][1] is parts[0][0]:
                    index[name, side] = index[name, 0]
                    continue
                index[name, side] = len(places)
                places.append([part[side] for part in parts])
        from_below = jnp.where(kpt == kpt_count - 1, index["ends", 0], index.get(("others", 0), 0))
        from_above = jnp.where(kpt == 0, index["ends", 1], index.get(("others", 1), 0))
        return places + [[own_valence]], from_below, from_above

    def slots_of(step):
        places, from_below, from_above = blocks_of(step)
        none = len(places) - 1
        below = jnp.where(has_below[step], from_below, none), jnp.where(has_below[step], kpt - step, kpt)
        above = jnp.where(has_above[step], from_above, none), jnp.where(has_above[step], kpt + step, kpt)
        if 2 * step < kpt_count:
            return places, [below[0], above[0]], [below[1], above[1]]
        return places, [jnp.where(has_below[step], below[0], above[0])], [jnp.where(has_below[step], below[1], above[1])]

    body = add_blocks(None, [jnp.zeros((), jnp.int32)], [kpt], [[own_valence]], [kpt], kpt_count)
    for step in range(1, kpt_count - 1):
        places_here, sides, owners = slots_of(step)
        body = add_blocks(body, sides, owners, places_here, owners, kpt_count)
    early = summed(body)
    places_here, sides, owners = slots_of(kpt_count - 1)
    last_owner = owners[0]
    late = summed(add_blocks(None, sides, owners, places_here, [jnp.zeros((), jnp.int32)], 1))

    match = neighbors[:, :, None] == point_of_row[None, None, :]
    stencil = jnp.sum(jnp.where(match, live[:, :, None], 0.0), axis=1)
    is_late = jnp.arange(all_points) // points == last_owner
    fine = jnp.dot(stencil, jnp.where(is_late[:, None], 0.0, early), precision=highest)
    late_stencil = lax.dynamic_slice_in_dim(stencil, last_owner * points, points, 1)
    fine = fine + jnp.dot(late_stencil, late, precision=highest)
    fine_here = neighbors.shape[0] // kpt_count
    fine = fine.reshape(kpt_count, fine_here, kept, lanes)
    own_fine = lax.dynamic_index_in_dim(fine, kpt, 0, keepdims=False)
    fine = own_fine + sum(piece.astype(f32) for piece in deal(fine.astype(bf16), "kpt")[1:])
    gathered = share(fine, "pw")
    whole = []
    for owner in range(pw_count):
        part = gathered[0]
        for shift in range(1, pw_count):
            part = jnp.where((pw - owner) % pw_count == shift, gathered[shift], part)
        whole.append(part)
    fine = jnp.concatenate(whole, axis=1).reshape(fine_here, half, 2, pairs)
    return jnp.transpose(fine, (2, 0, 1, 3)).reshape(2, fine_here, half * pairs)


def solution(mesh):
    return jax.shard_map(
        on_device,
        mesh=mesh,
        in_specs=(
            P("grp", "kpt", "band", "pw"),
            P("grp", "kpt", "band"),
            P("grp", "kpt", None, "pw"),
            P("grp", "kpt", None),
            P("grp", "kpt", "pw"),
            P("grp", None),
            P("grp", "pw"),
            P("grp"),
            P("grp"),
            P(),
            P(),
            P(),
            P(),
        ),
        out_specs=P("grp", "kpt", "band"),
        check_vma=False,
    )
```

```python
import jax
import jax.numpy as jnp
from jax import lax
from jax.experimental import pallas as pl
from jax.experimental.pallas import tpu as pltpu
from jax.sharding import PartitionSpec as P

highest = lax.Precision.HIGHEST
f32 = jnp.float32
bf16 = jnp.bfloat16
HEAD_PARTS = 3
VMEM_BYTES = 48 * 1024 * 1024


def round_up(value, step):
    return -(-value // step) * step


def shifted(x, name, shift):
    count = lax.axis_size(name)
    pairs = [(source, (source + shift) % count) for source in range(count)]
    return lax.ppermute(x, name, pairs)


def after(x, others):
    return lax.optimization_barrier((x, others))[0]


def share(x, name):
    return [x] + [shifted(x, name, shift) for shift in range(1, lax.axis_size(name))]


def deal(x, name):
    count = lax.axis_size(name)
    me = lax.axis_index(name)
    pieces = []
    for shift in range(count):
        piece = lax.dynamic_index_in_dim(x, (me + shift) % count, 0, keepdims=False)
        pieces.append(shifted(piece, name, shift) if shift else piece)
    return pieces


def valence_columns(valence, valence_head, selector, core, width, last):
    parts, points, pairs, columns = valence.shape
    head_at = columns - last * width

    def kernel(core_ref, valence_ref, head_ref, selector_ref, out_ref):
        column = lax.broadcasted_iota(jnp.int32, (pairs, width), 1)
        at_last = core_ref[0] == last
        limit = jnp.where(at_last, head_at, width)
        head_column = jnp.where(at_last, head_at, width)
        for point in range(points):
            rows = valence_ref[0, point].astype(f32)
            head = jnp.broadcast_to(head_ref[0, point].astype(f32), (pairs, width))
            rows = jnp.where(column < limit, rows, 0.0)
            rows = jnp.where(column == head_column, head, rows)
            moved = jnp.dot(selector_ref[...], rows.astype(bf16), preferred_element_type=f32)
            out_ref[0, point] = moved.astype(bf16)

    return pl.pallas_call(
        kernel,
        out_shape=jax.ShapeDtypeStruct((parts, points, pairs, width), bf16),
        grid_spec=pltpu.PrefetchScalarGridSpec(
            num_scalar_prefetch=1,
            grid=(parts,),
            in_specs=[
                pl.BlockSpec((1, points, pairs, width), lambda x, core: (x, 0, 0, core[0])),
                pl.BlockSpec((1, points, pairs, 1), lambda x, core: (x, 0, 0, 0)),
                pl.BlockSpec((pairs, pairs), lambda x, core: (0, 0)),
            ],
            out_specs=pl.BlockSpec((1, points, pairs, width), lambda x, core: (x, 0, 0, 0)),
        ),
        compiler_params=pltpu.CompilerParams(vmem_limit_bytes=VMEM_BYTES),
        name="valence_columns",
    )(core.reshape(1), valence, valence_head[..., None], selector)


def single(pairs_below, pairs_above):
    pairs = pairs_below + pairs_above
    return len({pair[0] for pair in pairs}) == len(pairs) and len({pair[1] for pair in pairs}) == len(pairs)


def chosen(below, above, pairs_below, pairs_above, name):
    if above is below or not single(pairs_below, pairs_above):
        return below, above
    sends_below = jnp.isin(lax.axis_index(name), jnp.array([pair[0] for pair in pairs_below]))
    sent = jnp.where(sends_below, below, above)
    return sent, sent


def one_way(below, above, pairs_below, pairs_above, name, gates=()):
    below, above = chosen(below, above, pairs_below, pairs_above, name)
    if above is below and single(pairs_below, pairs_above):
        moved = lax.ppermute(after(below, gates), name, pairs_below + pairs_above)
        return moved, moved
    below, above = after((below, above), gates)
    return lax.ppermute(below, name, pairs_below), lax.ppermute(above, name, pairs_above)


def line_pairs(count, step):
    below = [(s, s + 1) for s in range(step - 1, count - 1)]
    above = [(s, s - 1) for s in range(1, count - step + 1)]
    to_ends = [[pair for pair in below if pair[1] == count - 1], [pair for pair in above if pair[1] == 0]]
    to_others = [[pair for pair in below if pair[1] < count - 1], [pair for pair in above if pair[1] > 0]]
    return to_ends, to_others


def screen_product(places, pieces, right, per_index, half, store, blocks):
    _, deep, width = right.shape
    planes = deep // 2
    rows = per_index * half
    count = len(pieces)
    sources = pieces[0].shape[0]
    bands = 2
    pw_count = count // bands
    points = pw_count * per_index
    tile = 512 if width % 512 == 0 else min(256, width)

    def kernel(place_ref, *refs):
        piece_refs, right_ref, out_ref, left_ref = refs[:count], refs[count], refs[-2], refs[-1]

        @pl.when((pl.program_id(1) == 0) & (pl.program_id(2) == 0))
        def _():
            for index in range(count):
                start = pl.multiple_of(place_ref[index] * rows, rows)
                left_ref[pl.ds(start, rows), 0:planes] = piece_refs[index][0, 0]
                left_ref[pl.ds(start, rows), planes:deep] = piece_refs[index][0, 1]

        total = jnp.dot(left_ref[...], right_ref[0], preferred_element_type=f32).astype(bf16)
        for pw in range(pw_count):
            for band in range(bands):
                for point in range(per_index):
                    start = (pw * bands + band) * rows + point * half
                    out_ref[pw * per_index + point, band, 0] = total[start : start + half]

    whole = pl.BlockSpec((1, 2, rows, planes), lambda s, x, n, place: (s, 0, 0, 0))
    kept = [] if store is None else [store]
    return pl.pallas_call(
        kernel,
        out_shape=jax.ShapeDtypeStruct((blocks * points, bands, 2, half, width), bf16),
        grid_spec=pltpu.PrefetchScalarGridSpec(
            num_scalar_prefetch=1,
            grid=(sources, 2, width // tile),
            in_specs=[whole] * count
            + [pl.BlockSpec((1, deep, tile), lambda s, x, n, place: (x, 0, n))]
            + [pl.BlockSpec(memory_space=pl.ANY)] * len(kept),
            out_specs=pl.BlockSpec(
                (points, bands, 1, half, tile), lambda s, x, n, place: (place[count + s], 0, x, 0, n)
            ),
            scratch_shapes=[pltpu.VMEM((count * rows, deep), bf16)],
        ),
        input_output_aliases={count + 2: 0} if kept else {},
        compiler_params=pltpu.CompilerParams(vmem_limit_bytes=VMEM_BYTES),
        cost_estimate=pl.CostEstimate(flops=1, bytes_accessed=1, transcendentals=0),
        name="screen_product",
    )(places, *pieces, right, *kept)


def contract(row_ids, sides, owners, store, valences, body, blocks):
    _, bands, _, half, width = store.shape
    _, _, pairs, _ = valences[0][0].shape
    points = sum(part.shape[1] for part in valences[0])
    slots = sides.shape[0]
    group = 2 if points % 2 == 0 else 1
    steps = points // group
    given, places = [], []
    for side, parts in enumerate(valences):
        first = 0
        for part in parts:
            given.append(part)
            places.append((side, first, first + part.shape[1] // group))
            first = places[-1][2]

    def kernel(row_ref, side_ref, owner_ref, *refs):
        store_refs, valence_refs, out_ref = refs[:group], refs[group : group + len(given)], refs[-1]
        lane = lax.broadcasted_iota(jnp.int32, (half, 2 * pairs), 1)
        side = side_ref[pl.program_id(0)]
        step = pl.program_id(1)

        def rows_of(valence_ref):
            for index in range(group):
                left = store_refs[index][0].reshape(bands * 2 * half, width)
                right = valence_ref[:, index].reshape(2 * pairs, width)
                square = lax.dot_general(left, right, (((1,), (1,)), ((), ())), preferred_element_type=f32)
                for band in range(bands):
                    first = square[2 * band * half : (2 * band + 1) * half]
                    second = square[(2 * band + 1) * half : (2 * band + 2) * half]
                    turned = pltpu.roll(second, pairs, 1)
                    total = first + jnp.where(lane < pairs, -turned, turned)
                    out_ref[index, band * half : (band + 1) * half, :] = total

        for valence_ref, (place, first, end) in zip(valence_refs, places):

            @pl.when((side == place) & (step >= first) & (step < end))
            def _(valence_ref=valence_ref):
                rows_of(valence_ref)

    def store_spec(index):
        return pl.BlockSpec(
            (1, bands, 2, half, width),
            lambda slot, step, row, side, owner: (row[slot * points + step * group + index], 0, 0, 0, 0),
        )

    def valence_spec(place, first, end):
        return pl.BlockSpec(
            (2, group, pairs, width),
            lambda slot, step, row, side, owner: (
                0,
                jnp.where((side[slot] == place) & (step >= first) & (step < end), step - first, 0),
                0,
                0,
            ),
        )

    kept = [] if body is None else [body]
    return pl.pallas_call(
        kernel,
        out_shape=jax.ShapeDtypeStruct((blocks * points, bands * half, 2 * pairs), f32),
        grid_spec=pltpu.PrefetchScalarGridSpec(
            num_scalar_prefetch=3,
            grid=(slots, steps),
            in_specs=[store_spec(index) for index in range(group)]
            + [valence_spec(*place) for place in places]
            + [pl.BlockSpec(memory_space=pl.ANY)] * len(kept),
            out_specs=pl.BlockSpec(
                (group, bands * half, 2 * pairs),
                lambda slot, step, row, side, owner: (owner[slot] * steps + step, 0, 0),
            ),
        ),
        input_output_aliases={3 + group + len(given): 0} if kept else {},
        compiler_params=pltpu.CompilerParams(vmem_limit_bytes=VMEM_BYTES),
        cost_estimate=pl.CostEstimate(flops=1, bytes_accessed=1, transcendentals=0),
        name="contract",
    )(row_ids, sides, owners, *([store] * group), *given, *kept)


def on_device(
    conduction,
    conduction_head,
    valence,
    valence_head,
    screened,
    wing_column,
    wing_row,
    head_value,
    partner,
    pair_select,
    neighbors,
    weights,
    counts,
):
    points = conduction.shape[1]
    half = conduction.shape[2]
    pairs = valence.shape[2]
    block, columns = screened.shape[1], screened.shape[2]
    kpt_count, pw_count, band_count = lax.axis_size("kpt"), lax.axis_size("pw"), lax.axis_size("band")
    kpt, pw, band = lax.axis_index("kpt"), lax.axis_index("pw"), lax.axis_index("band")
    per_index = points // pw_count
    rows = per_index * half
    blocks_here = columns // block
    deep = round_up(block + HEAD_PARTS, 128)
    width = round_up(-(-(columns + 1) // band_count), 128)
    last = band_count - 1
    head_at = columns - last * width

    selector = (pair_select[:, None] == jnp.arange(pairs)[None, :]).astype(bf16)
    own_valence = valence_columns(valence, valence_head, selector, band, width, last)
    step_one = [
        lax.ppermute(own_valence, "kpt", [(s, s + 1) for s in range(kpt_count - 1)]),
        lax.ppermute(own_valence, "kpt", [(s, s - 1) for s in range(1, kpt_count)]),
    ]

    halves = jnp.moveaxis(conduction.reshape(2, pw_count, per_index, half, columns), 1, 0)
    dealt = deal(after(halves, own_valence), "pw")

    plane = jnp.arange(deep)
    is_head = (plane >= block) & (plane < block + HEAD_PARTS)
    heads = lax.dynamic_slice_in_dim(conduction_head, pw * per_index, per_index, 1)
    by_block = []
    for owner in range(pw_count):
        whole = dealt[0]
        for shift in range(1, pw_count):
            whole = jnp.where((pw - owner) % pw_count == shift, dealt[shift], whole)
        for index in range(blocks_here):
            cut = jnp.pad(
                whole[..., index * block : (index + 1) * block], ((0, 0), (0, 0), (0, 0), (0, deep - block))
            )
            by_block.append(jnp.where(is_head, heads[..., None], cut).reshape(2, rows, deep))
    by_block = jnp.stack(by_block)
    middle = kpt_count // 2 + 1
    own_block = lax.dynamic_index_in_dim(by_block, kpt, 0, keepdims=False)
    own_across = share(own_block[None], "pw")
    arrived = [own_block]
    for shift in range(1, kpt_count):
        piece = lax.dynamic_index_in_dim(by_block, (kpt + shift) % kpt_count, 0, keepdims=False)
        arrived.append(shifted(piece if shift < middle else after(piece, own_across), "kpt", shift))

    screen = jnp.pad(screened, ((0, 0), (0, deep - block), (0, band_count * width - columns)))
    screen = lax.dynamic_slice_in_dim(screen, band * width, width, 2)
    row_part = jnp.pad(wing_row, ((0, 0), (0, band_count * width - columns)))
    row_part = lax.dynamic_slice_in_dim(row_part, band * width, width, 1)
    first_kpt = kpt == 0
    row_part = jnp.where(first_kpt, row_part, 0)
    corner = []
    rest = head_value
    for _ in range(HEAD_PARTS):
        part = lax.reduce_precision(rest, 8, 7)
        corner.append(jnp.where(first_kpt, part, 0.0))
        rest = rest - part
    corner = jnp.stack(corner, axis=1).astype(bf16)
    column_part = jnp.concatenate(
        [lax.dynamic_slice_in_dim(wing_column, kpt * block, block, 1), corner], axis=1
    )
    column_part = jnp.pad(column_part, ((0, 0), (0, deep - block - HEAD_PARTS)))
    has_column = (pw == 0) & (band == last)
    screen = jnp.where(plane[None, :, None] == block, row_part[:, None, :], screen)
    screen = jnp.where(
        (jnp.arange(width)[None, None, :] == head_at) & has_column, column_part[:, :, None], screen
    )
    screen = after(screen, step_one)
    right = jnp.stack(
        [
            jnp.concatenate([screen[0], screen[1]], axis=0),
            jnp.concatenate([screen[1], -screen[0]], axis=0),
        ]
    )

    places = jnp.stack(
        [
            ((pw - pw_shift) % pw_count) * band_count + (band - band_shift) % band_count
            for pw_shift in range(pw_count)
            for band_shift in range(band_count)
        ]
    ).astype(jnp.int32)

    live = jnp.where(jnp.arange(neighbors.shape[1])[None, :] < counts[:, None], weights, 0.0)
    all_points = kpt_count * points
    point_of_row = jnp.sum(
        jnp.where(partner[None, :] == jnp.arange(all_points)[:, None], jnp.arange(all_points)[None, :], 0), axis=1
    ).astype(jnp.int32)

    def spread(across):
        return [own for value in across for own in share(value, "band")]

    def product(shifts, pieces, right, store):
        sources = jnp.stack([((kpt - shift) % kpt_count).astype(jnp.int32) for shift in shifts])
        where = jnp.append(places, sources)
        return screen_product(where, pieces, right, per_index, half, store, kpt_count)

    near, far = list(range(1, middle)), list(range(middle, kpt_count))
    distant = [arrived[shift] for shift in far]
    store = product([0], spread(own_across), right, None)
    to_ends, to_others = line_pairs(kpt_count, 2)
    onward = chosen(*step_one, *to_others, "kpt") if kpt_count > 3 else ()
    near_group = jnp.stack(after([arrived[shift] for shift in near], [store, step_one, distant, onward]))
    near_pieces = spread(share(near_group, "pw"))
    far_across = share(jnp.stack(distant), "pw")
    early_rows = max(points // 4, 1)
    first_part = one_way(*[value[:, :early_rows] for value in step_one], *to_ends, "kpt")
    gates = [near_group, distant, first_part]
    ends = {2: [first_part, one_way(*[value[:, early_rows:] for value in step_one], *to_ends, "kpt", gates)]}
    others = {}
    if kpt_count > 3:
        others[2] = [one_way(*onward, *to_others, "kpt", gates)]
    store = product(near, near_pieces, right, store)
    for step in range(3, kpt_count):
        below, above = others[step - 1][0]
        gates = [store, ends[2]]
        to_ends, to_others = line_pairs(kpt_count, step)
        ends[step] = [one_way(below, above, *to_ends, "kpt", gates)]
        if step < kpt_count - 1:
            others[step] = [one_way(below, above, *to_others, "kpt", gates)]
    far_pieces = [own for across in after(far_across, store) for own in share(across, "band")]
    store = product(far, far_pieces, after(right, others.get(2, ends[2])), store)

    lanes = 2 * pairs
    kept = half // pw_count

    def add_blocks(body, sides, owners, valences, targets, blocks):
        sides, owners = jnp.stack(sides).astype(jnp.int32), jnp.stack(owners)
        targets = jnp.stack(targets).astype(jnp.int32)
        row_ids = (owners[:, None] * points + jnp.arange(points)[None, :]).reshape(-1)
        row_ids = jnp.take(point_of_row, row_ids, mode="clip")
        return contract(row_ids, sides, targets, store, valences, body, blocks)

    def summed(body):
        body = body.reshape(-1, band_count, half, lanes)
        body = sum(deal(jnp.moveaxis(body, 1, 0), "band"))
        body = body.reshape(-1, pw_count, kept, lanes)
        return sum(deal(jnp.moveaxis(body, 1, 0), "pw")).reshape(-1, kept * lanes)

    has_below = [kpt >= step for step in range(kpt_count)]
    has_above = [kpt + step < kpt_count for step in range(kpt_count)]

    def blocks_of(step):
        if step == 1:
            return [[value] for value in step_one] + [[own_valence]], 0, 1
        places, index = [], {}
        for name, moved in (("ends", ends), ("others", others)):
            if step not in moved:
                continue
            parts = moved[step]
            for side in range(2):
                if side and parts[0][1] is parts[0][0]:
                    index[name, side] = index[name, 0]
                    continue
                index[name, side] = len(places)
                places.append([part[side] for part in parts])
        from_below = jnp.where(kpt == kpt_count - 1, index["ends", 0], index.get(("others", 0), 0))
        from_above = jnp.where(kpt == 0, index["ends", 1], index.get(("others", 1), 0))
        return places + [[own_valence]], from_below, from_above

    def slots_of(step):
        places, from_below, from_above = blocks_of(step)
        none = len(places) - 1
        below = jnp.where(has_below[step], from_below, none), jnp.where(has_below[step], kpt - step, kpt)
        above = jnp.where(has_above[step], from_above, none), jnp.where(has_above[step], kpt + step, kpt)
        if 2 * step < kpt_count:
            return places, [below[0], above[0]], [below[1], above[1]]
        return places, [jnp.where(has_below[step], below[0], above[0])], [jnp.where(has_below[step], below[1], above[1])]

    body = add_blocks(None, [jnp.zeros((), jnp.int32)], [kpt], [[own_valence]], [kpt], kpt_count)
    for step in range(1, kpt_count - 1):
        places_here, sides, owners = slots_of(step)
        body = add_blocks(body, sides, owners, places_here, owners, kpt_count)
    early = summed(body)
    places_here, sides, owners = slots_of(kpt_count - 1)
    last_owner = owners[0]
    late = summed(add_blocks(None, sides, owners, places_here, [jnp.zeros((), jnp.int32)], 1))

    match = neighbors[:, :, None] == point_of_row[None, None, :]
    stencil = jnp.sum(jnp.where(match, live[:, :, None], 0.0), axis=1)
    is_late = jnp.arange(all_points) // points == last_owner
    fine = jnp.dot(stencil, jnp.where(is_late[:, None], 0.0, early), precision=highest)
    late_stencil = lax.dynamic_slice_in_dim(stencil, last_owner * points, points, 1)
    fine = fine + jnp.dot(late_stencil, late, precision=highest)
    fine_here = neighbors.shape[0] // kpt_count
    fine = fine.reshape(kpt_count, fine_here, kept, lanes)
    own_fine = lax.dynamic_index_in_dim(fine, kpt, 0, keepdims=False)
    fine = own_fine + sum(piece.astype(f32) for piece in deal(fine.astype(bf16), "kpt")[1:])
    gathered = share(fine, "pw")
    whole = []
    for owner in range(pw_count):
        part = gathered[0]
        for shift in range(1, pw_count):
            part = jnp.where((pw - owner) % pw_count == shift, gathered[shift], part)
        whole.append(part)
    fine = jnp.concatenate(whole, axis=1).reshape(fine_here, half, 2, pairs)
    return jnp.transpose(fine, (2, 0, 1, 3)).reshape(2, fine_here, half * pairs)


def solution(mesh):
    return jax.shard_map(
        on_device,
        mesh=mesh,
        in_specs=(
            P("grp", "kpt", "band", "pw"),
            P("grp", "kpt", "band"),
            P("grp", "kpt", None, "pw"),
            P("grp", "kpt", None),
            P("grp", "kpt", "pw"),
            P("grp", None),
            P("grp", "pw"),
            P("grp"),
            P("grp"),
            P(),
            P(),
            P(),
            P(),
        ),
        out_specs=P("grp", "kpt", "band"),
        check_vma=False,
    )
```

```python
import jax
import jax.numpy as jnp
from jax import lax
from jax.experimental import pallas as pl
from jax.experimental.pallas import tpu as pltpu
from jax.sharding import PartitionSpec as P

highest = lax.Precision.HIGHEST
f32 = jnp.float32
bf16 = jnp.bfloat16
HEAD_PARTS = 3
VMEM_BYTES = 48 * 1024 * 1024


def round_up(value, step):
    return -(-value // step) * step


def shifted(x, name, shift):
    count = lax.axis_size(name)
    pairs = [(source, (source + shift) % count) for source in range(count)]
    return lax.ppermute(x, name, pairs)


def after(x, others):
    return lax.optimization_barrier((x, others))[0]


def share(x, name):
    return [x] + [shifted(x, name, shift) for shift in range(1, lax.axis_size(name))]


def deal(x, name):
    count = lax.axis_size(name)
    me = lax.axis_index(name)
    pieces = []
    for shift in range(count):
        piece = lax.dynamic_index_in_dim(x, (me + shift) % count, 0, keepdims=False)
        pieces.append(shifted(piece, name, shift) if shift else piece)
    return pieces


def valence_columns(valence, valence_head, selector, core, width, last):
    parts, points, pairs, columns = valence.shape
    head_at = columns - last * width

    def kernel(core_ref, valence_ref, head_ref, selector_ref, out_ref):
        column = lax.broadcasted_iota(jnp.int32, (pairs, width), 1)
        at_last = core_ref[0] == last
        limit = jnp.where(at_last, head_at, width)
        head_column = jnp.where(at_last, head_at, width)
        for point in range(points):
            rows = valence_ref[0, point].astype(f32)
            head = jnp.broadcast_to(head_ref[0, point].astype(f32), (pairs, width))
            rows = jnp.where(column < limit, rows, 0.0)
            rows = jnp.where(column == head_column, head, rows)
            moved = jnp.dot(selector_ref[...], rows.astype(bf16), preferred_element_type=f32)
            out_ref[0, point] = moved.astype(bf16)

    return pl.pallas_call(
        kernel,
        out_shape=jax.ShapeDtypeStruct((parts, points, pairs, width), bf16),
        grid_spec=pltpu.PrefetchScalarGridSpec(
            num_scalar_prefetch=1,
            grid=(parts,),
            in_specs=[
                pl.BlockSpec((1, points, pairs, width), lambda x, core: (x, 0, 0, core[0])),
                pl.BlockSpec((1, points, pairs, 1), lambda x, core: (x, 0, 0, 0)),
                pl.BlockSpec((pairs, pairs), lambda x, core: (0, 0)),
            ],
            out_specs=pl.BlockSpec((1, points, pairs, width), lambda x, core: (x, 0, 0, 0)),
        ),
        compiler_params=pltpu.CompilerParams(vmem_limit_bytes=VMEM_BYTES),
        name="valence_columns",
    )(core.reshape(1), valence, valence_head[..., None], selector)


def single(pairs_below, pairs_above):
    pairs = pairs_below + pairs_above
    return len({pair[0] for pair in pairs}) == len(pairs) and len({pair[1] for pair in pairs}) == len(pairs)


def chosen(below, above, pairs_below, pairs_above, name):
    if above is below or not single(pairs_below, pairs_above):
        return below, above
    sends_below = jnp.isin(lax.axis_index(name), jnp.array([pair[0] for pair in pairs_below]))
    sent = jnp.where(sends_below, below, above)
    return sent, sent


def one_way(below, above, pairs_below, pairs_above, name, gates=()):
    below, above = chosen(below, above, pairs_below, pairs_above, name)
    if above is below and single(pairs_below, pairs_above):
        moved = lax.ppermute(after(below, gates), name, pairs_below + pairs_above)
        return moved, moved
    below, above = after((below, above), gates)
    return lax.ppermute(below, name, pairs_below), lax.ppermute(above, name, pairs_above)


def line_pairs(count, step):
    below = [(s, s + 1) for s in range(step - 1, count - 1)]
    above = [(s, s - 1) for s in range(1, count - step + 1)]
    to_ends = [[pair for pair in below if pair[1] == count - 1], [pair for pair in above if pair[1] == 0]]
    to_others = [[pair for pair in below if pair[1] < count - 1], [pair for pair in above if pair[1] > 0]]
    return to_ends, to_others


def screen_product(places, pieces, right, per_index, half, store, blocks):
    _, deep, width = right.shape
    planes = deep // 2
    rows = per_index * half
    count = len(pieces)
    sources = pieces[0].shape[0]
    bands = 2
    pw_count = count // bands
    points = pw_count * per_index
    tile = 512 if width % 512 == 0 else min(256, width)

    def kernel(place_ref, *refs):
        piece_refs, right_ref, out_ref, left_ref = refs[:count], refs[count], refs[-2], refs[-1]

        @pl.when((pl.program_id(1) == 0) & (pl.program_id(2) == 0))
        def _():
            for index in range(count):
                start = pl.multiple_of(place_ref[index] * rows, rows)
                left_ref[pl.ds(start, rows), 0:planes] = piece_refs[index][0, 0]
                left_ref[pl.ds(start, rows), planes:deep] = piece_refs[index][0, 1]

        total = jnp.dot(left_ref[...], right_ref[0], preferred_element_type=f32).astype(bf16)
        for pw in range(pw_count):
            for band in range(bands):
                for point in range(per_index):
                    start = (pw * bands + band) * rows + point * half
                    out_ref[pw * per_index + point, band, 0] = total[start : start + half]

    whole = pl.BlockSpec((1, 2, rows, planes), lambda s, x, n, place: (s, 0, 0, 0))
    kept = [] if store is None else [store]
    return pl.pallas_call(
        kernel,
        out_shape=jax.ShapeDtypeStruct((blocks * points, bands, 2, half, width), bf16),
        grid_spec=pltpu.PrefetchScalarGridSpec(
            num_scalar_prefetch=1,
            grid=(sources, 2, width // tile),
            in_specs=[whole] * count
            + [pl.BlockSpec((1, deep, tile), lambda s, x, n, place: (x, 0, n))]
            + [pl.BlockSpec(memory_space=pl.ANY)] * len(kept),
            out_specs=pl.BlockSpec(
                (points, bands, 1, half, tile), lambda s, x, n, place: (place[count + s], 0, x, 0, n)
            ),
            scratch_shapes=[pltpu.VMEM((count * rows, deep), bf16)],
        ),
        input_output_aliases={count + 2: 0} if kept else {},
        compiler_params=pltpu.CompilerParams(vmem_limit_bytes=VMEM_BYTES),
        cost_estimate=pl.CostEstimate(flops=1, bytes_accessed=1, transcendentals=0),
        name="screen_product",
    )(places, *pieces, right, *kept)


def contract(row_ids, sides, owners, store, valences, body, blocks):
    _, bands, _, half, width = store.shape
    _, _, pairs, _ = valences[0][0].shape
    points = sum(part.shape[1] for part in valences[0])
    slots = sides.shape[0]
    group = 2 if points % 2 == 0 else 1
    steps = points // group
    given, places = [], []
    for side, parts in enumerate(valences):
        first = 0
        for part in parts:
            given.append(part)
            places.append((side, first, first + part.shape[1] // group))
            first = places[-1][2]

    def kernel(row_ref, side_ref, owner_ref, *refs):
        store_refs, valence_refs, out_ref = refs[:group], refs[group : group + len(given)], refs[-1]
        lane = lax.broadcasted_iota(jnp.int32, (half, 2 * pairs), 1)
        side = side_ref[pl.program_id(0)]
        step = pl.program_id(1)

        def rows_of(valence_ref):
            for index in range(group):
                left = store_refs[index][0].reshape(bands * 2 * half, width)
                right = valence_ref[:, index].reshape(2 * pairs, width)
                square = lax.dot_general(left, right, (((1,), (1,)), ((), ())), preferred_element_type=f32)
                for band in range(bands):
                    first = square[2 * band * half : (2 * band + 1) * half]
                    second = square[(2 * band + 1) * half : (2 * band + 2) * half]
                    turned = pltpu.roll(second, pairs, 1)
                    total = first + jnp.where(lane < pairs, -turned, turned)
                    out_ref[index, band * half : (band + 1) * half, :] = total

        for valence_ref, (place, first, end) in zip(valence_refs, places):

            @pl.when((side == place) & (step >= first) & (step < end))
            def _(valence_ref=valence_ref):
                rows_of(valence_ref)

    def store_spec(index):
        return pl.BlockSpec(
            (1, bands, 2, half, width),
            lambda slot, step, row, side, owner: (row[slot * points + step * group + index], 0, 0, 0, 0),
        )

    def valence_spec(place, first, end):
        return pl.BlockSpec(
            (2, group, pairs, width),
            lambda slot, step, row, side, owner: (
                0,
                jnp.where((side[slot] == place) & (step >= first) & (step < end), step - first, 0),
                0,
                0,
            ),
        )

    kept = [] if body is None else [body]
    return pl.pallas_call(
        kernel,
        out_shape=jax.ShapeDtypeStruct((blocks * points, bands * half, 2 * pairs), f32),
        grid_spec=pltpu.PrefetchScalarGridSpec(
            num_scalar_prefetch=3,
            grid=(slots, steps),
            in_specs=[store_spec(index) for index in range(group)]
            + [valence_spec(*place) for place in places]
            + [pl.BlockSpec(memory_space=pl.ANY)] * len(kept),
            out_specs=pl.BlockSpec(
                (group, bands * half, 2 * pairs),
                lambda slot, step, row, side, owner: (owner[slot] * steps + step, 0, 0),
            ),
        ),
        input_output_aliases={3 + group + len(given): 0} if kept else {},
        compiler_params=pltpu.CompilerParams(vmem_limit_bytes=VMEM_BYTES),
        cost_estimate=pl.CostEstimate(flops=1, bytes_accessed=1, transcendentals=0),
        name="contract",
    )(row_ids, sides, owners, *([store] * group), *given, *kept)


def on_device(
    conduction,
    conduction_head,
    valence,
    valence_head,
    screened,
    wing_column,
    wing_row,
    head_value,
    partner,
    pair_select,
    neighbors,
    weights,
    counts,
):
    points = conduction.shape[1]
    half = conduction.shape[2]
    pairs = valence.shape[2]
    block, columns = screened.shape[1], screened.shape[2]
    kpt_count, pw_count, band_count = lax.axis_size("kpt"), lax.axis_size("pw"), lax.axis_size("band")
    kpt, pw, band = lax.axis_index("kpt"), lax.axis_index("pw"), lax.axis_index("band")
    per_index = points // pw_count
    rows = per_index * half
    blocks_here = columns // block
    deep = round_up(block + HEAD_PARTS, 128)
    width = round_up(-(-(columns + 1) // band_count), 128)
    last = band_count - 1
    head_at = columns - last * width

    selector = (pair_select[:, None] == jnp.arange(pairs)[None, :]).astype(bf16)
    own_valence = valence_columns(valence, valence_head, selector, band, width, last)
    step_one = [
        lax.ppermute(own_valence, "kpt", [(s, s + 1) for s in range(kpt_count - 1)]),
        lax.ppermute(own_valence, "kpt", [(s, s - 1) for s in range(1, kpt_count)]),
    ]

    halves = jnp.moveaxis(conduction.reshape(2, pw_count, per_index, half, columns), 1, 0)
    dealt = deal(halves, "pw")

    plane = jnp.arange(deep)
    is_head = (plane >= block) & (plane < block + HEAD_PARTS)
    heads = lax.dynamic_slice_in_dim(conduction_head, pw * per_index, per_index, 1)
    by_block = []
    for owner in range(pw_count):
        whole = dealt[0]
        for shift in range(1, pw_count):
            whole = jnp.where((pw - owner) % pw_count == shift, dealt[shift], whole)
        for index in range(blocks_here):
            cut = jnp.pad(
                whole[..., index * block : (index + 1) * block], ((0, 0), (0, 0), (0, 0), (0, deep - block))
            )
            by_block.append(jnp.where(is_head, heads[..., None], cut).reshape(2, rows, deep))
    by_block = jnp.stack(by_block)
    arrived = deal(by_block, "kpt")
    own_block = arrived[0]
    middle = kpt_count // 2 + 1

    screen = jnp.pad(screened, ((0, 0), (0, deep - block), (0, band_count * width - columns)))
    screen = lax.dynamic_slice_in_dim(screen, band * width, width, 2)
    row_part = jnp.pad(wing_row, ((0, 0), (0, band_count * width - columns)))
    row_part = lax.dynamic_slice_in_dim(row_part, band * width, width, 1)
    first_kpt = kpt == 0
    row_part = jnp.where(first_kpt, row_part, 0)
    corner = []
    rest = head_value
    for _ in range(HEAD_PARTS):
        part = lax.reduce_precision(rest, 8, 7)
        corner.append(jnp.where(first_kpt, part, 0.0))
        rest = rest - part
    corner = jnp.stack(corner, axis=1).astype(bf16)
    column_part = jnp.concatenate(
        [lax.dynamic_slice_in_dim(wing_column, kpt * block, block, 1), corner], axis=1
    )
    column_part = jnp.pad(column_part, ((0, 0), (0, deep - block - HEAD_PARTS)))
    has_column = (pw == 0) & (band == last)
    screen = jnp.where(plane[None, :, None] == block, row_part[:, None, :], screen)
    screen = jnp.where(
        (jnp.arange(width)[None, None, :] == head_at) & has_column, column_part[:, :, None], screen
    )
    right = jnp.stack(
        [
            jnp.concatenate([screen[0], screen[1]], axis=0),
            jnp.concatenate([screen[1], -screen[0]], axis=0),
        ]
    )

    places = jnp.stack(
        [
            ((pw - pw_shift) % pw_count) * band_count + (band - band_shift) % band_count
            for pw_shift in range(pw_count)
            for band_shift in range(band_count)
        ]
    ).astype(jnp.int32)

    live = jnp.where(jnp.arange(neighbors.shape[1])[None, :] < counts[:, None], weights, 0.0)
    all_points = kpt_count * points
    point_of_row = jnp.sum(
        jnp.where(partner[None, :] == jnp.arange(all_points)[:, None], jnp.arange(all_points)[None, :], 0), axis=1
    ).astype(jnp.int32)

    def spread(group):
        return [own for across in share(group, "pw") for own in share(across, "band")]

    def product(shifts, pieces, right, store):
        sources = jnp.stack([((kpt - shift) % kpt_count).astype(jnp.int32) for shift in shifts])
        where = jnp.append(places, sources)
        return screen_product(where, pieces, right, per_index, half, store, kpt_count)

    near, far = list(range(1, middle)), list(range(middle, kpt_count))
    distant = [arrived[shift] for shift in far]
    store = product([0], spread(own_block[None]), right, None)
    to_ends, to_others = line_pairs(kpt_count, 2)
    onward = chosen(*step_one, *to_others, "kpt") if kpt_count > 3 else ()
    near_group = jnp.stack(after([arrived[shift] for shift in near], [store, step_one, distant, onward]))
    near_pieces = spread(near_group)
    far_across = share(jnp.stack(distant), "pw")
    early_rows = max(points // 4, 1)
    first_part = one_way(*[value[:, :early_rows] for value in step_one], *to_ends, "kpt")
    gates = [near_group, distant, first_part]
    ends = {2: [first_part, one_way(*[value[:, early_rows:] for value in step_one], *to_ends, "kpt", gates)]}
    others = {}
    if kpt_count > 3:
        others[2] = [one_way(*onward, *to_others, "kpt", gates)]
    store = product(near, near_pieces, right, store)
    for step in range(3, kpt_count):
        below, above = others[step - 1][0]
        gates = [store, ends[2]]
        to_ends, to_others = line_pairs(kpt_count, step)
        ends[step] = [one_way(below, above, *to_ends, "kpt", gates)]
        if step < kpt_count - 1:
            others[step] = [one_way(below, above, *to_others, "kpt", gates)]
    far_pieces = [own for across in after(far_across, store) for own in share(across, "band")]
    store = product(far, far_pieces, after(right, others.get(2, ends[2])), store)

    lanes = 2 * pairs
    kept = half // pw_count

    def add_blocks(body, sides, owners, valences, targets, blocks):
        sides, owners = jnp.stack(sides).astype(jnp.int32), jnp.stack(owners)
        targets = jnp.stack(targets).astype(jnp.int32)
        row_ids = (owners[:, None] * points + jnp.arange(points)[None, :]).reshape(-1)
        row_ids = jnp.take(point_of_row, row_ids, mode="clip")
        return contract(row_ids, sides, targets, store, valences, body, blocks)

    def summed(body):
        body = body.reshape(-1, band_count, half, lanes)
        body = sum(deal(jnp.moveaxis(body, 1, 0), "band"))
        body = body.reshape(-1, pw_count, kept, lanes)
        return sum(deal(jnp.moveaxis(body, 1, 0), "pw")).reshape(-1, kept * lanes)

    has_below = [kpt >= step for step in range(kpt_count)]
    has_above = [kpt + step < kpt_count for step in range(kpt_count)]

    def blocks_of(step):
        if step == 1:
            return [[value] for value in step_one] + [[own_valence]], 0, 1
        places, index = [], {}
        for name, moved in (("ends", ends), ("others", others)):
            if step not in moved:
                continue
            parts = moved[step]
            for side in range(2):
                if side and parts[0][1] is parts[0][0]:
                    index[name, side] = index[name, 0]
                    continue
                index[name, side] = len(places)
                places.append([part[side] for part in parts])
        from_below = jnp.where(kpt == kpt_count - 1, index["ends", 0], index.get(("others", 0), 0))
        from_above = jnp.where(kpt == 0, index["ends", 1], index.get(("others", 1), 0))
        return places + [[own_valence]], from_below, from_above

    def slots_of(step):
        places, from_below, from_above = blocks_of(step)
        none = len(places) - 1
        below = jnp.where(has_below[step], from_below, none), jnp.where(has_below[step], kpt - step, kpt)
        above = jnp.where(has_above[step], from_above, none), jnp.where(has_above[step], kpt + step, kpt)
        if 2 * step < kpt_count:
            return places, [below[0], above[0]], [below[1], above[1]]
        return places, [jnp.where(has_below[step], below[0], above[0])], [jnp.where(has_below[step], below[1], above[1])]

    body = add_blocks(None, [jnp.zeros((), jnp.int32)], [kpt], [[own_valence]], [kpt], kpt_count)
    for step in range(1, kpt_count - 1):
        places_here, sides, owners = slots_of(step)
        body = add_blocks(body, sides, owners, places_here, owners, kpt_count)
    early = summed(body)
    places_here, sides, owners = slots_of(kpt_count - 1)
    last_owner = owners[0]
    late = summed(add_blocks(None, sides, owners, places_here, [jnp.zeros((), jnp.int32)], 1))

    match = neighbors[:, :, None] == point_of_row[None, None, :]
    stencil = jnp.sum(jnp.where(match, live[:, :, None], 0.0), axis=1)
    is_late = jnp.arange(all_points) // points == last_owner
    fine = jnp.dot(stencil, jnp.where(is_late[:, None], 0.0, early), precision=highest)
    late_stencil = lax.dynamic_slice_in_dim(stencil, last_owner * points, points, 1)
    fine = fine + jnp.dot(late_stencil, late, precision=highest)
    fine_here = neighbors.shape[0] // kpt_count
    fine = fine.reshape(kpt_count, fine_here, kept, lanes)
    own_fine = lax.dynamic_index_in_dim(fine, kpt, 0, keepdims=False)
    fine = own_fine + sum(piece.astype(f32) for piece in deal(fine.astype(bf16), "kpt")[1:])
    gathered = share(fine, "pw")
    whole = []
    for owner in range(pw_count):
        part = gathered[0]
        for shift in range(1, pw_count):
            part = jnp.where((pw - owner) % pw_count == shift, gathered[shift], part)
        whole.append(part)
    fine = jnp.concatenate(whole, axis=1).reshape(fine_here, half, 2, pairs)
    return jnp.transpose(fine, (2, 0, 1, 3)).reshape(2, fine_here, half * pairs)


def solution(mesh):
    return jax.shard_map(
        on_device,
        mesh=mesh,
        in_specs=(
            P("grp", "kpt", "band", "pw"),
            P("grp", "kpt", "band"),
            P("grp", "kpt", None, "pw"),
            P("grp", "kpt", None),
            P("grp", "kpt", "pw"),
            P("grp", None),
            P("grp", "pw"),
            P("grp"),
            P("grp"),
            P(),
            P(),
            P(),
            P(),
        ),
        out_specs=P("grp", "kpt", "band"),
        check_vma=False,
    )
```

```python
import jax
import jax.numpy as jnp
from jax import lax
from jax.experimental import pallas as pl
from jax.experimental.pallas import tpu as pltpu
from jax.sharding import PartitionSpec as P

highest = lax.Precision.HIGHEST
f32 = jnp.float32
bf16 = jnp.bfloat16
HEAD_PARTS = 3
VMEM_BYTES = 48 * 1024 * 1024


def round_up(value, step):
    return -(-value // step) * step


def shifted(x, name, shift):
    count = lax.axis_size(name)
    pairs = [(source, (source + shift) % count) for source in range(count)]
    return lax.ppermute(x, name, pairs)


def after(x, others):
    return lax.optimization_barrier((x, others))[0]


def share(x, name):
    return [x] + [shifted(x, name, shift) for shift in range(1, lax.axis_size(name))]


def deal(x, name):
    count = lax.axis_size(name)
    me = lax.axis_index(name)
    pieces = []
    for shift in range(count):
        piece = lax.dynamic_index_in_dim(x, (me + shift) % count, 0, keepdims=False)
        pieces.append(shifted(piece, name, shift) if shift else piece)
    return pieces


def valence_columns(valence, valence_head, selector, core, width, last):
    parts, points, pairs, columns = valence.shape
    head_at = columns - last * width

    def kernel(core_ref, valence_ref, head_ref, selector_ref, out_ref):
        column = lax.broadcasted_iota(jnp.int32, (pairs, width), 1)
        at_last = core_ref[0] == last
        limit = jnp.where(at_last, head_at, width)
        head_column = jnp.where(at_last, head_at, width)
        for point in range(points):
            rows = valence_ref[0, point].astype(f32)
            head = jnp.broadcast_to(head_ref[0, point].astype(f32), (pairs, width))
            rows = jnp.where(column < limit, rows, 0.0)
            rows = jnp.where(column == head_column, head, rows)
            moved = jnp.dot(selector_ref[...], rows.astype(bf16), preferred_element_type=f32)
            out_ref[0, point] = moved.astype(bf16)

    return pl.pallas_call(
        kernel,
        out_shape=jax.ShapeDtypeStruct((parts, points, pairs, width), bf16),
        grid_spec=pltpu.PrefetchScalarGridSpec(
            num_scalar_prefetch=1,
            grid=(parts,),
            in_specs=[
                pl.BlockSpec((1, points, pairs, width), lambda x, core: (x, 0, 0, core[0])),
                pl.BlockSpec((1, points, pairs, 1), lambda x, core: (x, 0, 0, 0)),
                pl.BlockSpec((pairs, pairs), lambda x, core: (0, 0)),
            ],
            out_specs=pl.BlockSpec((1, points, pairs, width), lambda x, core: (x, 0, 0, 0)),
        ),
        compiler_params=pltpu.CompilerParams(vmem_limit_bytes=VMEM_BYTES),
        name="valence_columns",
    )(core.reshape(1), valence, valence_head[..., None], selector)


def one_way(below, above, pairs_below, pairs_above, name, gates=()):
    senders = [pair[0] for pair in pairs_below + pairs_above]
    takers = [pair[1] for pair in pairs_below + pairs_above]
    if len(set(senders)) < len(senders) or len(set(takers)) < len(takers):
        below, above = after((below, above), gates)
        return lax.ppermute(below, name, pairs_below), lax.ppermute(above, name, pairs_above)
    sent = below
    if above is not below:
        sends_below = jnp.isin(lax.axis_index(name), jnp.array([pair[0] for pair in pairs_below]))
        sent = jnp.where(sends_below, below, above)
    moved = lax.ppermute(after(sent, gates), name, pairs_below + pairs_above)
    return moved, moved


def line_pairs(count, step):
    below = [(s, s + 1) for s in range(step - 1, count - 1)]
    above = [(s, s - 1) for s in range(1, count - step + 1)]
    to_ends = [[pair for pair in below if pair[1] == count - 1], [pair for pair in above if pair[1] == 0]]
    to_others = [[pair for pair in below if pair[1] < count - 1], [pair for pair in above if pair[1] > 0]]
    return to_ends, to_others


def screen_product(places, pieces, right, per_index, half, store, blocks):
    _, deep, width = right.shape
    planes = deep // 2
    rows = per_index * half
    count = len(pieces)
    sources = pieces[0].shape[0]
    bands = 2
    pw_count = count // bands
    points = pw_count * per_index
    tile = 512 if width % 512 == 0 else min(256, width)

    def kernel(place_ref, *refs):
        piece_refs, right_ref, out_ref, left_ref = refs[:count], refs[count], refs[-2], refs[-1]

        @pl.when((pl.program_id(1) == 0) & (pl.program_id(2) == 0))
        def _():
            for index in range(count):
                start = pl.multiple_of(place_ref[index] * rows, rows)
                left_ref[pl.ds(start, rows), 0:planes] = piece_refs[index][0, 0]
                left_ref[pl.ds(start, rows), planes:deep] = piece_refs[index][0, 1]

        total = jnp.dot(left_ref[...], right_ref[0], preferred_element_type=f32).astype(bf16)
        for pw in range(pw_count):
            for band in range(bands):
                for point in range(per_index):
                    start = (pw * bands + band) * rows + point * half
                    out_ref[pw * per_index + point, band, 0] = total[start : start + half]

    whole = pl.BlockSpec((1, 2, rows, planes), lambda s, x, n, place: (s, 0, 0, 0))
    kept = [] if store is None else [store]
    return pl.pallas_call(
        kernel,
        out_shape=jax.ShapeDtypeStruct((blocks * points, bands, 2, half, width), bf16),
        grid_spec=pltpu.PrefetchScalarGridSpec(
            num_scalar_prefetch=1,
            grid=(sources, 2, width // tile),
            in_specs=[whole] * count
            + [pl.BlockSpec((1, deep, tile), lambda s, x, n, place: (x, 0, n))]
            + [pl.BlockSpec(memory_space=pl.ANY)] * len(kept),
            out_specs=pl.BlockSpec(
                (points, bands, 1, half, tile), lambda s, x, n, place: (place[count + s], 0, x, 0, n)
            ),
            scratch_shapes=[pltpu.VMEM((count * rows, deep), bf16)],
        ),
        input_output_aliases={count + 2: 0} if kept else {},
        compiler_params=pltpu.CompilerParams(vmem_limit_bytes=VMEM_BYTES),
        cost_estimate=pl.CostEstimate(flops=1, bytes_accessed=1, transcendentals=0),
        name="screen_product",
    )(places, *pieces, right, *kept)


def contract(row_ids, sides, owners, store, valences, body, blocks):
    _, bands, _, half, width = store.shape
    _, _, pairs, _ = valences[0][0].shape
    points = sum(part.shape[1] for part in valences[0])
    slots = sides.shape[0]
    group = max(size for size in (1, 2, 4) if all(part.shape[1] % size == 0 for parts in valences for part in parts))
    steps = points // group
    given, places = [], []
    for side, parts in enumerate(valences):
        first = 0
        for part in parts:
            given.append(part)
            places.append((side, first, first + part.shape[1] // group))
            first = places[-1][2]

    def kernel(row_ref, side_ref, owner_ref, *refs):
        store_refs, valence_refs, out_ref = refs[:group], refs[group : group + len(given)], refs[-1]
        lane = lax.broadcasted_iota(jnp.int32, (half, 2 * pairs), 1)
        side = side_ref[pl.program_id(0)]
        step = pl.program_id(1)

        def rows_of(valence_ref):
            for index in range(group):
                left = store_refs[index][0].reshape(bands * 2 * half, width)
                right = valence_ref[:, index].reshape(2 * pairs, width)
                square = lax.dot_general(left, right, (((1,), (1,)), ((), ())), preferred_element_type=f32)
                for band in range(bands):
                    first = square[2 * band * half : (2 * band + 1) * half]
                    second = square[(2 * band + 1) * half : (2 * band + 2) * half]
                    turned = pltpu.roll(second, pairs, 1)
                    total = first + jnp.where(lane < pairs, -turned, turned)
                    out_ref[index, band * half : (band + 1) * half, :] = total

        for valence_ref, (place, first, end) in zip(valence_refs, places):

            @pl.when((side == place) & (step >= first) & (step < end))
            def _(valence_ref=valence_ref):
                rows_of(valence_ref)

    def store_spec(index):
        return pl.BlockSpec(
            (1, bands, 2, half, width),
            lambda slot, step, row, side, owner: (row[slot * points + step * group + index], 0, 0, 0, 0),
        )

    def valence_spec(place, first, end):
        return pl.BlockSpec(
            (2, group, pairs, width),
            lambda slot, step, row, side, owner: (
                0,
                jnp.where((side[slot] == place) & (step >= first) & (step < end), step - first, 0),
                0,
                0,
            ),
        )

    kept = [] if body is None else [body]
    return pl.pallas_call(
        kernel,
        out_shape=jax.ShapeDtypeStruct((blocks * points, bands * half, 2 * pairs), f32),
        grid_spec=pltpu.PrefetchScalarGridSpec(
            num_scalar_prefetch=3,
            grid=(slots, steps),
            in_specs=[store_spec(index) for index in range(group)]
            + [valence_spec(*place) for place in places]
            + [pl.BlockSpec(memory_space=pl.ANY)] * len(kept),
            out_specs=pl.BlockSpec(
                (group, bands * half, 2 * pairs),
                lambda slot, step, row, side, owner: (owner[slot] * steps + step, 0, 0),
            ),
        ),
        input_output_aliases={3 + group + len(given): 0} if kept else {},
        compiler_params=pltpu.CompilerParams(vmem_limit_bytes=VMEM_BYTES),
        cost_estimate=pl.CostEstimate(flops=1, bytes_accessed=1, transcendentals=0),
        name="contract",
    )(row_ids, sides, owners, *([store] * group), *given, *kept)


def on_device(
    conduction,
    conduction_head,
    valence,
    valence_head,
    screened,
    wing_column,
    wing_row,
    head_value,
    partner,
    pair_select,
    neighbors,
    weights,
    counts,
):
    points = conduction.shape[1]
    half = conduction.shape[2]
    pairs = valence.shape[2]
    block, columns = screened.shape[1], screened.shape[2]
    kpt_count, pw_count, band_count = lax.axis_size("kpt"), lax.axis_size("pw"), lax.axis_size("band")
    kpt, pw, band = lax.axis_index("kpt"), lax.axis_index("pw"), lax.axis_index("band")
    per_index = points // pw_count
    rows = per_index * half
    blocks_here = columns // block
    deep = round_up(block + HEAD_PARTS, 128)
    width = round_up(-(-(columns + 1) // band_count), 128)
    last = band_count - 1
    head_at = columns - last * width

    selector = (pair_select[:, None] == jnp.arange(pairs)[None, :]).astype(bf16)
    own_valence = valence_columns(valence, valence_head, selector, band, width, last)
    step_one = [
        lax.ppermute(own_valence, "kpt", [(s, s + 1) for s in range(kpt_count - 1)]),
        lax.ppermute(own_valence, "kpt", [(s, s - 1) for s in range(1, kpt_count)]),
    ]

    halves = jnp.moveaxis(conduction.reshape(2, pw_count, per_index, half, columns), 1, 0)
    dealt = deal(halves, "pw")

    plane = jnp.arange(deep)
    is_head = (plane >= block) & (plane < block + HEAD_PARTS)
    heads = lax.dynamic_slice_in_dim(conduction_head, pw * per_index, per_index, 1)
    by_block = []
    for owner in range(pw_count):
        whole = dealt[0]
        for shift in range(1, pw_count):
            whole = jnp.where((pw - owner) % pw_count == shift, dealt[shift], whole)
        for index in range(blocks_here):
            cut = jnp.pad(
                whole[..., index * block : (index + 1) * block], ((0, 0), (0, 0), (0, 0), (0, deep - block))
            )
            by_block.append(jnp.where(is_head, heads[..., None], cut).reshape(2, rows, deep))
    by_block = jnp.stack(by_block)
    arrived = deal(by_block, "kpt")
    own_block = arrived[0]
    middle = kpt_count // 2 + 1

    screen = jnp.pad(screened, ((0, 0), (0, deep - block), (0, band_count * width - columns)))
    screen = lax.dynamic_slice_in_dim(screen, band * width, width, 2)
    row_part = jnp.pad(wing_row, ((0, 0), (0, band_count * width - columns)))
    row_part = lax.dynamic_slice_in_dim(row_part, band * width, width, 1)
    first_kpt = kpt == 0
    row_part = jnp.where(first_kpt, row_part, 0)
    corner = []
    rest = head_value
    for _ in range(HEAD_PARTS):
        part = lax.reduce_precision(rest, 8, 7)
        corner.append(jnp.where(first_kpt, part, 0.0))
        rest = rest - part
    corner = jnp.stack(corner, axis=1).astype(bf16)
    column_part = jnp.concatenate(
        [lax.dynamic_slice_in_dim(wing_column, kpt * block, block, 1), corner], axis=1
    )
    column_part = jnp.pad(column_part, ((0, 0), (0, deep - block - HEAD_PARTS)))
    has_column = (pw == 0) & (band == last)
    screen = jnp.where(plane[None, :, None] == block, row_part[:, None, :], screen)
    screen = jnp.where(
        (jnp.arange(width)[None, None, :] == head_at) & has_column, column_part[:, :, None], screen
    )
    right = jnp.stack(
        [
            jnp.concatenate([screen[0], screen[1]], axis=0),
            jnp.concatenate([screen[1], -screen[0]], axis=0),
        ]
    )

    places = jnp.stack(
        [
            ((pw - pw_shift) % pw_count) * band_count + (band - band_shift) % band_count
            for pw_shift in range(pw_count)
            for band_shift in range(band_count)
        ]
    ).astype(jnp.int32)

    live = jnp.where(jnp.arange(neighbors.shape[1])[None, :] < counts[:, None], weights, 0.0)
    all_points = kpt_count * points
    point_of_row = jnp.sum(
        jnp.where(partner[None, :] == jnp.arange(all_points)[:, None], jnp.arange(all_points)[None, :], 0), axis=1
    ).astype(jnp.int32)

    def spread(group):
        return [own for across in share(group, "pw") for own in share(across, "band")]

    def product(shifts, pieces, right, store):
        sources = jnp.stack([((kpt - shift) % kpt_count).astype(jnp.int32) for shift in shifts])
        where = jnp.append(places, sources)
        return screen_product(where, pieces, right, per_index, half, store, kpt_count)

    near, far = list(range(1, middle)), list(range(middle, kpt_count))
    distant = [arrived[shift] for shift in far]
    store = product([0], spread(own_block[None]), right, None)
    near_group = jnp.stack(after([arrived[shift] for shift in near], [store, step_one, distant]))
    near_pieces = spread(near_group)
    far_across = share(jnp.stack(distant), "pw")
    to_ends, to_others = line_pairs(kpt_count, 2)
    early_rows = max(points // 4, 1)
    first_part = one_way(*[value[:, :early_rows] for value in step_one], *to_ends, "kpt")
    gates = [near_group, distant, first_part]
    ends = {2: [first_part, one_way(*[value[:, early_rows:] for value in step_one], *to_ends, "kpt", gates)]}
    others = {}
    if kpt_count > 3:
        others[2] = [one_way(*step_one, *to_others, "kpt", gates)]
    store = product(near, near_pieces, right, store)
    for step in range(3, kpt_count):
        below, above = others[step - 1][0]
        gates = [store, ends[2]]
        to_ends, to_others = line_pairs(kpt_count, step)
        ends[step] = [one_way(below, above, *to_ends, "kpt", gates)]
        if step < kpt_count - 1:
            others[step] = [one_way(below, above, *to_others, "kpt", gates)]
    far_pieces = [own for across in after(far_across, store) for own in share(across, "band")]
    store = product(far, far_pieces, after(right, others.get(2, ends[2])), store)

    lanes = 2 * pairs
    kept = half // pw_count

    def add_blocks(body, sides, owners, valences, targets, blocks):
        sides, owners = jnp.stack(sides).astype(jnp.int32), jnp.stack(owners)
        targets = jnp.stack(targets).astype(jnp.int32)
        row_ids = (owners[:, None] * points + jnp.arange(points)[None, :]).reshape(-1)
        row_ids = jnp.take(point_of_row, row_ids, mode="clip")
        return contract(row_ids, sides, targets, store, valences, body, blocks)

    def summed(body):
        body = body.reshape(-1, band_count, half, lanes)
        body = sum(deal(jnp.moveaxis(body, 1, 0), "band"))
        body = body.reshape(-1, pw_count, kept, lanes)
        return sum(deal(jnp.moveaxis(body, 1, 0), "pw")).reshape(-1, kept * lanes)

    has_below = [kpt >= step for step in range(kpt_count)]
    has_above = [kpt + step < kpt_count for step in range(kpt_count)]

    def blocks_of(step):
        if step == 1:
            return [[value] for value in step_one] + [[own_valence]], 0, 1
        places, index = [], {}
        for name, moved in (("ends", ends), ("others", others)):
            if step not in moved:
                continue
            parts = moved[step]
            for side in range(2):
                if side and parts[0][1] is parts[0][0]:
                    index[name, side] = index[name, 0]
                    continue
                index[name, side] = len(places)
                places.append([part[side] for part in parts])
        from_below = jnp.where(kpt == kpt_count - 1, index["ends", 0], index.get(("others", 0), 0))
        from_above = jnp.where(kpt == 0, index["ends", 1], index.get(("others", 1), 0))
        return places + [[own_valence]], from_below, from_above

    def slots_of(step):
        places, from_below, from_above = blocks_of(step)
        none = len(places) - 1
        below = jnp.where(has_below[step], from_below, none), jnp.where(has_below[step], kpt - step, kpt)
        above = jnp.where(has_above[step], from_above, none), jnp.where(has_above[step], kpt + step, kpt)
        if 2 * step < kpt_count:
            return places, [below[0], above[0]], [below[1], above[1]]
        return places, [jnp.where(has_below[step], below[0], above[0])], [jnp.where(has_below[step], below[1], above[1])]

    body = add_blocks(None, [jnp.zeros((), jnp.int32)], [kpt], [[own_valence]], [kpt], kpt_count)
    for step in range(1, kpt_count - 1):
        places_here, sides, owners = slots_of(step)
        body = add_blocks(body, sides, owners, places_here, owners, kpt_count)
    early = summed(body)
    places_here, sides, owners = slots_of(kpt_count - 1)
    last_owner = owners[0]
    late = summed(add_blocks(None, sides, owners, places_here, [jnp.zeros((), jnp.int32)], 1))

    match = neighbors[:, :, None] == point_of_row[None, None, :]
    stencil = jnp.sum(jnp.where(match, live[:, :, None], 0.0), axis=1)
    is_late = jnp.arange(all_points) // points == last_owner
    fine = jnp.dot(stencil, jnp.where(is_late[:, None], 0.0, early), precision=highest)
    late_stencil = lax.dynamic_slice_in_dim(stencil, last_owner * points, points, 1)
    fine = fine + jnp.dot(late_stencil, late, precision=highest)
    fine_here = neighbors.shape[0] // kpt_count
    fine = fine.reshape(kpt_count, fine_here, kept, lanes)
    own_fine = lax.dynamic_index_in_dim(fine, kpt, 0, keepdims=False)
    fine = own_fine + sum(piece.astype(f32) for piece in deal(fine.astype(bf16), "kpt")[1:])
    gathered = share(fine, "pw")
    whole = []
    for owner in range(pw_count):
        part = gathered[0]
        for shift in range(1, pw_count):
            part = jnp.where((pw - owner) % pw_count == shift, gathered[shift], part)
        whole.append(part)
    fine = jnp.concatenate(whole, axis=1).reshape(fine_here, half, 2, pairs)
    return jnp.transpose(fine, (2, 0, 1, 3)).reshape(2, fine_here, half * pairs)


def solution(mesh):
    return jax.shard_map(
        on_device,
        mesh=mesh,
        in_specs=(
            P("grp", "kpt", "band", "pw"),
            P("grp", "kpt", "band"),
            P("grp", "kpt", None, "pw"),
            P("grp", "kpt", None),
            P("grp", "kpt", "pw"),
            P("grp", None),
            P("grp", "pw"),
            P("grp"),
            P("grp"),
            P(),
            P(),
            P(),
            P(),
        ),
        out_specs=P("grp", "kpt", "band"),
        check_vma=False,
    )
```
